32 devices in a mesh: sec: 2 (over x), gy: 4 (over z), gz: 4 (over y, core).
Axes of the slice: x: 2, y: 2, z: 4, core: 2. Of those that a mesh axis runs over, the one named last changes fastest.
Arguments:
- inflow: float32 [5, 128, 1024], P(None, 'gy', 'gz'), may hold values from -6 to 6
- initial: float32 [2, 5, 128, 1024], P('sec', None, 'gy', 'gz'), may hold values from -6 to 6
- solid: int32 [2, 128, 1024], P('sec', 'gy', 'gz'), may hold values 0 or 1
- speed_y: float32 [5], replicated, may hold values from -1 to 1
- speed_z: float32 [5], replicated, may hold values from -1 to 1
- vigneron: float32 [5], replicated, may hold values from 0.2 to 0.9
- coupling: float32 [5, 5], replicated, may hold values from -2.5 to 2.5
Outputs:
- marched: float32 [2, 5, 128, 1024], P('sec', None, 'gy', 'gz')
The draws below stay inside these ranges and needn't reach their ends.
Inputs may be any that keep to these rules, and one draw needn't show every extreme that they name: `solid`: 1 marks a cell inside the body, 0 a fluid cell.
All inputs are finite; a program needn't handle non-finite values. No bound on the sum of `solid` on one device may be relied on, other than what follows from the above.
Results may differ from the reference program's by a relative error of at most 0.00025.
Values sent between devices are 32-bit elements; how exact they have to be, the bound alone decides.
No kernel may reach another device: no remote copies, remote signals or barrier semaphores. Data moves between devices by JAX's collectives and lax.ppermute only.
A program may use at most 64 MiB of HBM per device.

```python
import jax
import jax.numpy as jnp
from jax import lax

NVAR = 5
ITERS = 4
CORRECTORS = 3
NEWTON = 2
NSEC = 2
NY = 128
NZ = 1024


def place_ends(values, key, low, top_value):
    longest = values.shape.index(max(values.shape))
    spots = []
    for shift in (0, 1):
        where = [jax.random.randint(jax.random.fold_in(key, axis), (), 0, length) for axis, length in enumerate(values.shape)]
        where[longest] = (where[longest] + shift) % values.shape[longest]
        spots.append(tuple(where))
    return values.at[spots[0]].set(low).at[spots[1]].set(top_value)


def steps_of(key, shape, pieces, least, largest):
    loudness, own = 1.0, jax.random.fold_in(key, 6)
    for position, shards_of in pieces:
        draws = jnp.exp(jax.random.uniform(jax.random.fold_in(own, position), (shards_of,), jnp.float32, least / len(pieces), largest / len(pieces)))
        loudness = loudness * jnp.repeat(draws, shape[position] // shards_of).reshape([-1 if axis == position else 1 for axis in range(len(shape))])
    return loudness


def gaussian(rng, dims, scale, reach, cuts=(), held_as=jnp.bfloat16):
    entries = jax.random.normal(rng, dims, jnp.float32) * scale
    if len(cuts) > 0:
        entries = steps_of(rng, dims, cuts, -0.22, 0.18) * entries
    return jnp.clip(entries, min=-reach, max=reach).astype(held_as)


def setup_inputs(seed: int = 0) -> dict:
    streams_of = jax.random.split(jax.random.key(seed), 8)
    return {
        "inflow": gaussian(streams_of[0], (NVAR, NY, NZ), 1.0, 6.0, ((1, 4), (2, 4)), jnp.float32),
        "initial": gaussian(streams_of[1], (NSEC, NVAR, NY, NZ), 1.0, 6.0, ((0, 2), (2, 4), (3, 4)), jnp.float32),
        "solid": place_ends((jax.random.randint(streams_of[2], (NSEC, NY, NZ), 0, 8) < 1).astype(jnp.int32), jax.random.fold_in(streams_of[2], 1), 0, 1),
        "speed_y": jnp.clip(jax.random.uniform(streams_of[3], (NVAR,), jnp.float32, -1.0, 1.0), -1.0, 1.0),
        "speed_z": jnp.clip(jax.random.uniform(streams_of[4], (NVAR,), jnp.float32, -1.0, 1.0), -1.0, 1.0),
        "vigneron": jnp.clip(jax.random.uniform(streams_of[5], (NVAR,), jnp.float32, 0.2, 0.9), 0.2, 0.9),
        "coupling": gaussian(streams_of[6], (NVAR, NVAR), NVAR ** -0.5, 2.5, (), jnp.float32),
    }


STEP_RATIO = 0.25
WENO_EPS = 1e-6


def weno_face(left_far, left_near, center, right_near, right_far):
    smooth_left = (13.0 / 12.0) * (left_far - 2.0 * left_near + center) ** 2 + 0.25 * (left_far - 4.0 * left_near + 3.0 * center) ** 2
    smooth_middle = (13.0 / 12.0) * (left_near - 2.0 * center + right_near) ** 2 + 0.25 * (left_near - right_near) ** 2
    smooth_right = (13.0 / 12.0) * (center - 2.0 * right_near + right_far) ** 2 + 0.25 * (3.0 * center - 4.0 * right_near + right_far) ** 2
    weight_left = 0.1 / (WENO_EPS + smooth_left) ** 2
    weight_middle = 0.6 / (WENO_EPS + smooth_middle) ** 2
    weight_right = 0.3 / (WENO_EPS + smooth_right) ** 2
    guess_left = (2.0 * left_far - 7.0 * left_near + 11.0 * center) / 6.0
    guess_middle = (-left_near + 5.0 * center + 2.0 * right_near) / 6.0
    guess_right = (2.0 * center + 5.0 * right_near - right_far) / 6.0
    total = weight_left * guess_left + weight_middle * guess_middle + weight_right * guess_right
    return total / (weight_left + weight_middle + weight_right)


def sweep(padded, speeds, axis):
    count = padded.shape[axis] - 6
    plus_flux = jnp.maximum(speeds, 0.0)[:, None, None] * padded
    minus_flux = jnp.minimum(speeds, 0.0)[:, None, None] * padded

    def window(source, offset):
        return lax.slice_in_dim(source, offset, offset + count + 1, axis=axis)

    faces = weno_face(window(plus_flux, 0), window(plus_flux, 1), window(plus_flux, 2), window(plus_flux, 3), window(plus_flux, 4))
    faces = faces + weno_face(window(minus_flux, 5), window(minus_flux, 4), window(minus_flux, 3), window(minus_flux, 2), window(minus_flux, 1))
    return lax.slice_in_dim(faces, 1, count + 1, axis=axis) - lax.slice_in_dim(faces, 0, count, axis=axis)


def crossflow(padded, speed_y, speed_z):
    rows_part = sweep(padded[:, :, 3:-3], speed_y, 1)
    cols_part = sweep(padded[:, 3:-3, :], speed_z, 2)
    return rows_part + cols_part


def streamwise(field, factor):
    return field + factor * field ** 3 / (1.0 + field ** 2)


def slope(field, factor):
    return 1.0 + factor * field ** 2 * (3.0 + field ** 2) / (1.0 + field ** 2) ** 2


def correct(padded, current, upstream, diff, blocked, params):
    speed_y, speed_z, vigneron, coupling = params
    factor = vigneron[:, None, None]
    mixed = jnp.einsum("vw,wyz->vyz", coupling, current, precision=lax.Precision.HIGHEST)
    target = streamwise(upstream, factor) - STEP_RATIO * crossflow(padded, speed_y, speed_z) + STEP_RATIO * mixed - (1.0 - factor) * diff
    guess = current
    for newton_index in range(NEWTON):
        guess = guess - (streamwise(guess, factor) - target) / slope(guess, factor)
    return jnp.where(blocked[None], 0.0, guess)


def station(upstream, diff, blocked, params):
    current = upstream
    for corrector_index in range(CORRECTORS):
        padded = jnp.pad(current, ((0, 0), (3, 3), (3, 3)))
        current = correct(padded, current, upstream, diff, blocked, params)
    return current


def reference(inflow, initial, solid, speed_y, speed_z, vigneron, coupling):
    params = (speed_y, speed_z, vigneron, coupling)
    solid_cells = solid != 0
    planes = initial
    for iterate in range(ITERS):
        prior_upstream = jnp.concatenate([inflow[None], planes[:-1]], axis=0)

        def march(upstream, inputs):
            prior_here, prior_above, solid_here = inputs
            updated = station(upstream, prior_here - prior_above, solid_here, params)
            return updated, updated

        final_plane, planes = lax.scan(march, inflow, (planes, prior_upstream, solid_cells))
    return planes
```

```python
import functools

import jax
import jax.numpy as jnp
from jax import lax
from jax.experimental import pallas as pl
from jax.experimental.pallas import tpu as pltpu
from jax.sharding import PartitionSpec as P

NVAR = 5
ITERS = 4
CORRECTORS = 3
NEWTON = 2

STEP_RATIO = 0.25
WENO_EPS = 1e-06


def passed_along(value, axis, steps):
    count = lax.axis_size(axis)
    initial, last = (max(0, -steps), min(count, count - steps))
    return lax.ppermute(value, axis, [(source, source + steps) for source in range(initial, last)])


def extended(block, sides, width):
    for axis, dim in sides:
        count = lax.axis_size(axis)
        forward = [(i, i + 1) for i in range(count - 1)]
        backward = [(target, source) for source, target in forward]
        low = lax.ppermute(
            lax.slice_in_dim(block, block.shape[dim] - width, None, axis=dim), axis, forward
        )
        high = lax.ppermute(lax.slice_in_dim(block, 0, width, axis=dim), axis, backward)
        block = jnp.concatenate([low, block, high], axis=dim)
    return block


def weno_face(left_far, left_near, center, right_near, right_far):
    smooth_left = (
        13.0 / 12.0 * (left_far - 2.0 * left_near + center) ** 2
        + 0.25 * (left_far - 4.0 * left_near + 3.0 * center) ** 2
    )
    smooth_middle = (
        13.0 / 12.0 * (left_near - 2.0 * center + right_near) ** 2
        + 0.25 * (left_near - right_near) ** 2
    )
    smooth_right = (
        13.0 / 12.0 * (center - 2.0 * right_near + right_far) ** 2
        + 0.25 * (3.0 * center - 4.0 * right_near + right_far) ** 2
    )
    weight_left = 0.1 / (WENO_EPS + smooth_left) ** 2
    weight_middle = 0.6 / (WENO_EPS + smooth_middle) ** 2
    weight_right = 0.3 / (WENO_EPS + smooth_right) ** 2
    guess_left = (2.0 * left_far - 7.0 * left_near + 11.0 * center) / 6.0
    guess_middle = (-left_near + 5.0 * center + 2.0 * right_near) / 6.0
    guess_right = (2.0 * center + 5.0 * right_near - right_far) / 6.0
    total = weight_left * guess_left + weight_middle * guess_middle + weight_right * guess_right
    return total / (weight_left + weight_middle + weight_right)


def sweep(padded, speeds, axis):
    count = padded.shape[axis] - 6
    plus_flux = jnp.maximum(speeds, 0.0)[:, None, None] * padded
    minus_flux = jnp.minimum(speeds, 0.0)[:, None, None] * padded

    def window(source, offset):
        return lax.slice_in_dim(source, offset, offset + count + 1, axis=axis)

    faces = weno_face(*(window(plus_flux, i) for i in (0, 1, 2, 3, 4)))
    faces = faces + weno_face(*(window(minus_flux, i) for i in (5, 4, 3, 2, 1)))
    return lax.slice_in_dim(faces, 1, count + 1, axis=axis) - lax.slice_in_dim(
        faces, 0, count, axis=axis
    )


def crossflow(padded, speed_y, speed_z):
    rows_part = sweep(padded[:, :, 3:-3], speed_y, 1)
    cols_part = sweep(padded[:, 3:-3, :], speed_z, 2)
    return rows_part + cols_part


def streamwise(field, factor):
    return field + factor * field**3 / (1.0 + field**2)


def slope(field, factor):
    return 1.0 + factor * field**2 * (3.0 + field**2) / (1.0 + field**2) ** 2


def correct(padded, current, upstream, diff, blocked, params):
    speed_y, speed_z, vigneron, coupling = params
    factor = vigneron[:, None, None]
    mixed = jnp.einsum("vw,wyz->vyz", coupling, current, precision=lax.Precision.HIGHEST)
    target = (
        streamwise(upstream, factor)
        - STEP_RATIO * crossflow(padded, speed_y, speed_z)
        + STEP_RATIO * mixed
        - (1.0 - factor) * diff
    )
    guess = current
    for newton_index in range(NEWTON):
        guess = guess - (streamwise(guess, factor) - target) / slope(guess, factor)
    return jnp.where(blocked[None], 0.0, guess)


def per_device(inflow, initial, solid, speed_y, speed_z, vigneron, coupling):
    params = (speed_y, speed_z, vigneron, coupling)
    sections = lax.axis_size("sec")
    position = lax.axis_index("sec")
    is_first = position == 0
    start_plane = initial[0]
    guess_above = passed_along(start_plane, "sec", 1)
    guess_above = jnp.where(is_first, inflow, guess_above)
    solid_tile = solid[0] != 0

    def station(upstream, diff):
        current = upstream
        for corrector_index in range(CORRECTORS):
            padded = extended(current, (("gy", 1), ("gz", 2)), 3)
            current = correct(padded, current, upstream, diff, solid_tile, params)
        return current

    def advance(step_index, carry):
        sent, own_prior, upstream_prior = carry
        received = passed_along(sent, "sec", 1)
        received = jnp.where(is_first, inflow, received)
        iterate = step_index - position + 1
        active = (iterate >= 1) & (iterate <= ITERS)
        updated = station(received, own_prior - upstream_prior)
        own_next = jnp.where(active, updated, own_prior)
        upstream_next = jnp.where(active, received, upstream_prior)
        return (own_next, own_next, upstream_next)

    result = lax.fori_loop(
        0, ITERS + sections - 1, advance, (start_plane, start_plane, guess_above)
    )
    return result[1][None]


LANES = 128
SLAB = 32
TILE = 256
MEMBERS = 8
PIECE = 32
GUARD = 16
LEFT = 40
ROWS = GUARD + LEFT + SLAB + LEFT + GUARD
CHUNK_IN = 72
CHUNK_OUT = 40
NEAR = 24
EDGE_ONE = 11 * SLAB + 6 * NEAR
EDGE_TWO = 11 * 8
CHANNELS = 17


def lane_iota():
    return lax.broadcasted_iota(jnp.int32, (8, LANES), 1)


def turned(value, shift):
    shift = shift % LANES
    return value if shift == 0 else pltpu.roll(value, shift, 1)


def slab_of(member, odd):
    sec, gy = member // 4, member % 4
    j = 2 * gy + (sec ^ (gy & 1))
    return jnp.where(odd, MEMBERS - 1 - j, j)


def pack_kernel(place, inflow, initial, solid, out, stacked, turned_ref, solids):
    sec, odd = place[0], place[1] == 1
    for group in range(2):
        for p in range(4):
            rows = pl.ds(p * PIECE, PIECE)
            if group == 0:
                stacked[rows, :] = initial[0, p]
            elif p == 0:
                stacked[rows, :] = initial[0, 4]
            else:
                stacked[rows, :] = inflow[jnp.minimum(3 * sec + p - 1, NVAR - 1)]
        for half in range(2):
            turned_ref[pl.ds(half * LANES, LANES), :] = stacked[:, half * LANES:(half + 1) * LANES].T
        for member in range(MEMBERS):
            j = slab_of(member, odd)
            out[member, pl.ds(group * SLAB, SLAB), :] = turned_ref[
                pl.ds(pl.multiple_of(j * SLAB, SLAB), SLAB), :
            ]
    solids[...] = jnp.zeros_like(solids)
    for half in range(2):
        solids[pl.ds(half * PIECE, PIECE), :] = solid[
            0, :, half * LANES:(half + 1) * LANES
        ].astype(jnp.float32)
    turned_ref[pl.ds(0, LANES), :] = solids[...].T
    quarter = lane_iota() // PIECE
    for member in range(MEMBERS):
        j = slab_of(member, odd)
        half, within = j // 4, j % 4
        packed = jnp.zeros((8, LANES), jnp.float32)
        for octet in range(4):
            piece = turned_ref[pl.ds(pl.multiple_of(within * SLAB + octet * 8, 8), 8), :]
            piece = pltpu.roll(piece, (PIECE * (octet - half)) % LANES, 1)
            packed = jnp.where(quarter == octet, piece, packed)
        out[member, pl.ds(2 * SLAB, 8), :] = packed


def assemble_kernel(got, own, right_one, left_one, right_two, left_two):
    quarter = lane_iota() // PIECE

    def gathered(sec, row, shift):
        value = None
        for gy in range(4):
            piece = turned(got[sec * 4 + gy, pl.ds(row, 8), :], PIECE * gy - shift)
            value = piece if value is None else jnp.where(quarter == gy, piece, value)
        return value

    def source(channel, octet):
        if channel < 3:
            return gathered(0, SLAB + 8 * octet, PIECE * (channel + 1))
        if channel < 5:
            return gathered(1, SLAB + 8 * octet, PIECE * (channel - 2))
        sec, v = (channel - 5) // 6, (channel - 5) % 6
        if v < 4:
            return gathered(sec, 8 * octet, PIECE * v)
        if v == 4:
            return gathered(sec, SLAB + 8 * octet, 0)
        return gathered(sec, 2 * SLAB, PIECE * octet)

    for channel in range(CHANNELS):
        for octet in range(4):
            value = source(channel, octet)
            own[channel, pl.ds(8 * octet, 8), :] = value
            if channel < 11:
                rows = pl.ds(channel * SLAB + 8 * octet, 8)
                right_one[rows, :] = value
                left_one[rows, :] = value
                if octet == 3:
                    right_two[pl.ds(8 * channel, 8), :] = value
                if octet == 0:
                    left_two[pl.ds(8 * channel, 8), :] = value
            else:
                at = 11 * SLAB + (channel - 11) * NEAR
                if octet > 0:
                    right_one[pl.ds(at + 8 * (octet - 1), 8), :] = value
                if octet < 3:
                    left_one[pl.ds(at + 8 * octet, 8), :] = value


def unpack_kernel(place, got, out, stacked, packed):
    odd = place[1] == 1
    quarter = lane_iota() // PIECE

    def member_of(j):
        j = jnp.where(odd, MEMBERS - 1 - j, j)
        gy = j // 2
        sec = (j % 2 + gy % 2) % 2
        return sec * 4 + gy

    for half in range(2):
        for within in range(4):
            member = member_of(4 * half + within)
            stacked[pl.ds(within * SLAB, SLAB), :] = got[member, pl.ds(0, SLAB), :]
        block = stacked[...].T
        for v in range(4):
            out[0, v, :, half * LANES:(half + 1) * LANES] = block[v * PIECE:(v + 1) * PIECE]
    for within in range(4):
        low = got[member_of(within), pl.ds(SLAB, 8), :]
        high = got[member_of(4 + within), pl.ds(SLAB, 8), :]
        for octet in range(4):
            packed[pl.ds(within * SLAB + 8 * octet, 8), :] = jnp.where(
                quarter == 0, turned(low, -PIECE * octet), turned(high, PIECE - PIECE * octet)
            )
    block = packed[...].T
    for half in range(2):
        out[0, 4, :, half * LANES:(half + 1) * LANES] = block[half * PIECE:(half + 1) * PIECE]


def weighted(d1, d2, d3, d4, t1, t2, t3):
    a = 3.0 * d2 - d1
    b = d2 + d3
    c = 3.0 * d3 - d4
    y1 = pltpu.reciprocal(t1 + a * a, approx=True)
    y2 = pltpu.reciprocal(t2 + b * b, approx=True)
    y3 = pltpu.reciprocal(t3 + c * c, approx=True)
    g1, g2, g3 = y1 * y1, y2 * y2, y3 * y3
    p1 = (a + a - d2) * (1.0 / 6.0)
    p2 = b + d3
    p3 = (c + d3) * 0.5
    over = g1 * p1 + g2 * p2 + g3 * p3
    under = g1 + 6.0 * g2 + 3.0 * g3
    return over * pltpu.reciprocal(under, approx=True)


def main_kernel(
    place, speed_y, speed_z, vigneron, coupling,
    own, from_left, from_right, from_left_two, from_right_two,
    out,
    inf, still, base, first, second, s0, s1, work_inf, delta, curve, face, blocked, start1,
):
    lane = lane_iota()
    center = GUARD + LEFT

    def fill(ref, index, channel, wide):
        ref = ref.at[index] if index is not None else ref
        ref[pl.ds(0, GUARD), :] = jnp.zeros((GUARD, LANES), jnp.float32)
        ref[pl.ds(ROWS - GUARD, GUARD), :] = jnp.zeros((GUARD, LANES), jnp.float32)
        ref[pl.ds(center, SLAB), :] = own[channel]
        if wide:
            ref[pl.ds(GUARD, 8), :] = from_left_two[pl.ds(8 * channel, 8), :]
            ref[pl.ds(GUARD + 8, SLAB), :] = from_left[pl.ds(SLAB * channel, SLAB), :]
            ref[pl.ds(center + SLAB, SLAB), :] = from_right[pl.ds(SLAB * channel, SLAB), :]
            ref[pl.ds(center + 2 * SLAB, 8), :] = from_right_two[pl.ds(8 * channel, 8), :]
        else:
            at = 11 * SLAB + (channel - 11) * NEAR
            zeros = jnp.zeros((16, LANES), jnp.float32)
            ref[pl.ds(GUARD, 16), :] = zeros
            ref[pl.ds(center - NEAR, NEAR), :] = from_left[pl.ds(at, NEAR), :]
            ref[pl.ds(center + SLAB, NEAR), :] = from_right[pl.ds(at, NEAR), :]
            ref[pl.ds(center + SLAB + NEAR, 16), :] = zeros

    for v in range(NVAR):
        fill(inf, v, v, True)
        fill(s0.at[0], v, 5 + v, True)
        fill(s1, v, 11 + v, False)
    fill(blocked, 0, 10, True)
    fill(blocked, 1, 16, False)
    slab, last = place[2], place[3]
    for octet in range(ROWS // 8):
        rows = pl.ds(8 * octet, 8)
        column = slab * SLAB + 8 * octet - center + lax.broadcasted_iota(jnp.int32, (8, LANES), 0)
        outside = (column < 0) | (column >= last)
        for station in range(2):
            blocked[station, rows, :] = jnp.where(
                outside | (blocked[station, rows, :] != 0.0), 0.0, 1.0
            )
    for ref in (first, second, s0.at[1]):
        for v in range(NVAR):
            ref[v] = jnp.zeros((ROWS, LANES), jnp.float32)

    sy = [speed_y[v] for v in range(NVAR)]
    sz = [speed_z[v] for v in range(NVAR)]
    half_y = [0.5 * jnp.maximum(s, -s) for s in sy]
    half_z = [0.5 * jnp.maximum(s, -s) for s in sz]
    step_z = [jnp.where(s >= 0.0, 1, -1) for s in sz]
    turn_y = [jnp.where(s >= 0.0, 1, LANES - 1) for s in sy]
    back_y = [jnp.where(s >= 0.0, LANES - 1, 1) for s in sy]
    wind_y = [jnp.where(s >= 0.0, 0, LANES - 1) for s in sy]
    minus_y = [jnp.where(s >= 0.0, 0, 1) for s in sy]
    vig = [vigneron[v] for v in range(NVAR)]

    def newton(v, guess, target):
        for _ in range(NEWTON):
            r = pltpu.reciprocal(1.0 + guess * guess, approx=True)
            z = (2.0 * vig[v]) * r
            over = (z * (1.0 - r)) * guess + target
            under = z * (0.5 - r) + (1.0 + vig[v])
            guess = over * pltpu.reciprocal(under, approx=True)
        return guess

    def energy(v, field):
        r = pltpu.reciprocal(1.0 + field * field, approx=True)
        return field * ((1.0 + vig[v]) - vig[v] * r)

    def octet_rows(g):
        return pl.multiple_of(GUARD + 8 * g, 8)

    def pairs(g0, extra, body, carry):
        def two(i, c):
            for k in range(2):
                c = body(g0 - extra + 2 * i + k, c)
            return c
        return lax.fori_loop(0, 7 - g0 + extra, two, carry)

    def fluxes(src, g0):
        def differ(g, carry):
            at = octet_rows(g)
            packed = []
            for v in range(NVAR):
                here = src[v, pl.ds(at, 8), :]
                down = src[v, pl.ds(at + step_z[v], 8), :]
                up = src[v, pl.ds(at - step_z[v], 8), :]
                d = (down - here) * half_z[v]
                t = d - (here - up) * half_z[v]
                delta[v, pl.ds(at, 8), :] = d
                curve[v, pl.ds(at, 8), :] = (13.0 / 3.0) * (t * t) + WENO_EPS
                edge = pltpu.roll(here, (2 * g + 2 * minus_y[v]) & (LANES - 1), 1)
                packed.append(jnp.where(lane // 2 == g, edge, carry[v]))
            return tuple(packed)

        zero = jnp.zeros((8, LANES), jnp.float32)
        edges = pairs(g0, 1, differ, (zero,) * NVAR)

        entry = []
        for v in range(NVAR):
            u = edges[v] * half_y[v]
            d4 = pltpu.roll(u, back_y[v], 1) - u
            t3 = d4 - u
            flat = jnp.full((8, LANES), WENO_EPS, jnp.float32)
            entry.append(weighted(
                zero, zero, u, d4, flat,
                (13.0 / 3.0) * (u * u) + WENO_EPS, (13.0 / 3.0) * (t3 * t3) + WENO_EPS,
            ))

        def across(g, carry):
            at = octet_rows(g)
            for v in range(NVAR):
                s = step_z[v]
                d3 = delta[v, pl.ds(at, 8), :]
                d2 = delta[v, pl.ds(at - s, 8), :]
                d1 = delta[v, pl.ds(at - 2 * s, 8), :]
                d4 = delta[v, pl.ds(at + s, 8), :]
                t1 = curve[v, pl.ds(at - s, 8), :]
                t2 = curve[v, pl.ds(at, 8), :]
                t3 = curve[v, pl.ds(at + s, 8), :]
                face[v, pl.ds(at, 8), :] = half_z[v] * src[v, pl.ds(at, 8), :] + weighted(
                    d1, d2, d3, d4, t1, t2, t3
                )
            return carry

        pairs(g0, 0, across, 0)
        return entry

    def sources(src, g, entry):
        at = octet_rows(g)
        field = [src[v, pl.ds(at, 8), :] for v in range(NVAR)]
        result = []
        for v in range(NVAR):
            upwind = lane == wind_y[v]
            downwind = lane == (LANES - 1) - wind_y[v]
            u = half_y[v] * field[v]
            d3 = jnp.where(downwind, 0.0, pltpu.roll(u, back_y[v], 1)) - u
            d2 = jnp.where(upwind, u, pltpu.roll(d3, turn_y[v], 1))
            d1 = jnp.where(upwind, 0.0, pltpu.roll(d2, turn_y[v], 1))
            d4 = jnp.where(downwind, 0.0, pltpu.roll(d3, back_y[v], 1))
            t = d3 - d2
            t2 = (13.0 / 3.0) * (t * t) + WENO_EPS
            end = (13.0 / 3.0) * (u * u) + WENO_EPS
            t1 = jnp.where(upwind, end, pltpu.roll(t2, turn_y[v], 1))
            t3 = jnp.where(downwind, end, pltpu.roll(t2, back_y[v], 1))
            ahead = u + weighted(d1, d2, d3, d4, t1, t2, t3)
            first_face = pltpu.roll(
                entry[v], (wind_y[v] - 2 * g - minus_y[v]) & (LANES - 1), 1
            )
            behind = jnp.where(upwind, first_face, pltpu.roll(ahead, turn_y[v], 1))
            columns = face[v, pl.ds(at, 8), :] - face[v, pl.ds(at - step_z[v], 8), :]
            mixed = coupling[v, 0] * field[0]
            for w in range(1, NVAR):
                mixed = mixed + coupling[v, w] * field[w]
            result.append(STEP_RATIO * mixed - (2.0 * STEP_RATIO) * ((ahead - behind) + columns))
        return field, result

    def corrector(src, dst, station, g0):
        entry = fluxes(src, g0)

        def step(g, carry):
            at = octet_rows(g)
            field, terms = sources(src, g, entry)
            fluid = blocked[station, pl.ds(at, 8), :]
            for v in range(NVAR):
                value = newton(v, field[v], still[v, pl.ds(at, 8), :] + terms[v])
                dst[v, pl.ds(at, 8), :] = jnp.where(fluid != 0.0, value, 0.0)
            return carry

        pairs(g0, 0, step, 0)

    def reach(e):
        return (LEFT - 1 - e) // 8

    g0 = reach(33)
    entry = fluxes(inf, g0)

    def prepare(g, carry):
        at = octet_rows(g)
        field, terms = sources(inf, g, entry)
        for v in range(NVAR):
            base[v, pl.ds(at, 8), :] = energy(v, field[v])
            work_inf[v, pl.ds(at, 8), :] = terms[v]
        return carry

    pairs(g0, 0, prepare, 0)

    def iterate(k, carry):
        old, new = s0.at[k % 2], s0.at[1 - k % 2]

        def first_of_0(g, c):
            at = octet_rows(g)
            fluid = blocked[0, pl.ds(at, 8), :]
            for v in range(NVAR):
                here = inf[v, pl.ds(at, 8), :]
                prior = old[v, pl.ds(at, 8), :]
                fixed = base[v, pl.ds(at, 8), :] - (1.0 - vig[v]) * (prior - here)
                still[v, pl.ds(at, 8), :] = fixed
                value = newton(v, here, fixed + work_inf[v, pl.ds(at, 8), :])
                first[v, pl.ds(at, 8), :] = jnp.where(fluid != 0.0, value, 0.0)
            return c

        pairs((6 + 6 * k) // 8, 0, first_of_0, 0)
        corrector(first, second, 0, (9 + 6 * k) // 8)
        corrector(second, new, 0, (12 + 6 * k) // 8)

        def start_of_1(g, c):
            at = octet_rows(g)
            for v in range(NVAR):
                above = new[v, pl.ds(at, 8), :]
                prior = s1[v, pl.ds(at, 8), :] - old[v, pl.ds(at, 8), :]
                still[v, pl.ds(at, 8), :] = energy(v, above) - (1.0 - vig[v]) * prior
            return c

        pairs((15 + 6 * k) // 8, 0, start_of_1, 0)
        corrector(new, first, 1, (15 + 6 * k) // 8)
        corrector(first, second, 1, (18 + 6 * k) // 8)
        corrector(second, s1, 1, (21 + 6 * k) // 8)
        return carry

    lax.fori_loop(0, ITERS, iterate, 0)

    quarter = lane // PIECE
    for station, result in enumerate((s0.at[ITERS % 2], s1)):
        for octet in range(4):
            field = [result[v, pl.ds(center + 8 * octet, 8), :] for v in range(NVAR)]
            for gy in range(4):
                member = station * 4 + gy
                value = None
                for p in range(4):
                    piece = turned(field[p], PIECE * (p - gy))
                    value = piece if value is None else jnp.where(quarter == p, piece, value)
                out[member, pl.ds(8 * octet, 8), :] = value
                piece = turned(field[4], PIECE * (octet - gy))
                if octet > 0:
                    piece = jnp.where(quarter == octet, piece, out[member, pl.ds(SLAB, 8), :])
                out[member, pl.ds(SLAB, 8), :] = piece


def slabs_per_device(inflow, initial, solid, speed_y, speed_z, vigneron, coupling):
    mesh_axes = ("sec", "gy", "gz")
    nz_parts = lax.axis_size("gz")
    sec, gy, gz = (lax.axis_index(a) for a in mesh_axes)
    path = []
    for z in range(nz_parts):
        members = [(s, y) for y in range(4) for s in ((0, 1) if y % 2 == 0 else (1, 0))]
        path += [(s * 4 + y) * nz_parts + z for s, y in (members if z % 2 == 0 else members[::-1])]

    def along(value, steps):
        count = len(path)
        low, high = max(0, -steps), min(count, count - steps)
        return lax.ppermute(value, mesh_axes, [(path[i], path[i + steps]) for i in range(low, high)])

    odd = gz % 2
    j = 2 * gy + (sec + gy) % 2
    slab = gz * MEMBERS + jnp.where(odd == 1, MEMBERS - 1 - j, j)
    place = jnp.stack(
        [sec, odd, slab, jnp.asarray(len(path) * SLAB, jnp.int32)]
    ).astype(jnp.int32)

    smem = pl.BlockSpec(memory_space=pltpu.SMEM)
    vmem = pl.BlockSpec(memory_space=pltpu.VMEM)
    f32 = functools.partial(jax.ShapeDtypeStruct, dtype=jnp.float32)

    packed = pl.pallas_call(
        pack_kernel,
        out_shape=f32((MEMBERS, CHUNK_IN, LANES)),
        in_specs=[smem, vmem, vmem, vmem],
        out_specs=vmem,
        scratch_shapes=[
            pltpu.VMEM((LANES, TILE), jnp.float32),
            pltpu.VMEM((TILE, LANES), jnp.float32),
            pltpu.VMEM((LANES, LANES), jnp.float32),
        ],
        name="pack",
    )(place, inflow, initial, solid)
    got = lax.all_to_all(packed, ("sec", "gy"), 0, 0)
    own, right_one, left_one, right_two, left_two = pl.pallas_call(
        assemble_kernel,
        out_shape=[
            f32((CHANNELS, SLAB, LANES)),
            f32((EDGE_ONE, LANES)),
            f32((EDGE_ONE, LANES)),
            f32((EDGE_TWO, LANES)),
            f32((EDGE_TWO, LANES)),
        ],
        in_specs=[vmem],
        out_specs=[vmem] * 5,
        name="assemble",
    )(got)
    window = pltpu.VMEM((NVAR, ROWS, LANES), jnp.float32)
    sent = pl.pallas_call(
        main_kernel,
        out_shape=f32((MEMBERS, CHUNK_OUT, LANES)),
        in_specs=[smem] * 5 + [vmem] * 5,
        out_specs=vmem,
        scratch_shapes=[
            window, window, window, window, window,
            pltpu.VMEM((2, NVAR, ROWS, LANES), jnp.float32),
            window, window, window, window, window,
            pltpu.VMEM((2, ROWS, LANES), jnp.float32),
            window,
        ],
        compiler_params=pltpu.CompilerParams(vmem_limit_bytes=32 * 1024 * 1024),
        name="march",
    )(
        place, speed_y, speed_z, vigneron, coupling,
        own, along(right_one, 1), along(left_one, -1), along(right_two, 2), along(left_two, -2),
    )
    returned = lax.all_to_all(sent, ("sec", "gy"), 0, 0)
    return pl.pallas_call(
        unpack_kernel,
        out_shape=f32((1, NVAR, PIECE, TILE)),
        in_specs=[smem, vmem],
        out_specs=vmem,
        scratch_shapes=[
            pltpu.VMEM((LANES, LANES), jnp.float32),
            pltpu.VMEM((LANES, LANES), jnp.float32),
        ],
        name="unpack",
    )(place, returned)


def chosen(*args):
    inflow, initial = args[0], args[1]
    fits = (
        lax.axis_size("sec") == 2
        and lax.axis_size("gy") == 4
        and inflow.shape == (NVAR, PIECE, TILE)
        and initial.shape == (1, NVAR, PIECE, TILE)
    )
    return slabs_per_device(*args) if fits else per_device(*args)


def solution(mesh):
    return jax.shard_map(
        chosen,
        mesh=mesh,
        in_specs=(
            P(None, "gy", "gz"),
            P("sec", None, "gy", "gz"),
            P("sec", "gy", "gz"),
            P(),
            P(),
            P(),
            P(),
        ),
        out_specs=P("sec", None, "gy", "gz"),
        check_vma=False,
    )
```

```python
import functools

import jax
import jax.numpy as jnp
from jax import lax
from jax.experimental import pallas as pl
from jax.experimental.pallas import tpu as pltpu
from jax.sharding import PartitionSpec as P

NVAR = 5
ITERS = 4
CORRECTORS = 3
NEWTON = 2

STEP_RATIO = 0.25
WENO_EPS = 1e-06


def passed_along(value, axis, steps):
    count = lax.axis_size(axis)
    initial, last = (max(0, -steps), min(count, count - steps))
    return lax.ppermute(value, axis, [(source, source + steps) for source in range(initial, last)])


def extended(block, sides, width):
    for axis, dim in sides:
        count = lax.axis_size(axis)
        forward = [(i, i + 1) for i in range(count - 1)]
        backward = [(target, source) for source, target in forward]
        low = lax.ppermute(
            lax.slice_in_dim(block, block.shape[dim] - width, None, axis=dim), axis, forward
        )
        high = lax.ppermute(lax.slice_in_dim(block, 0, width, axis=dim), axis, backward)
        block = jnp.concatenate([low, block, high], axis=dim)
    return block


def weno_face(left_far, left_near, center, right_near, right_far):
    smooth_left = (
        13.0 / 12.0 * (left_far - 2.0 * left_near + center) ** 2
        + 0.25 * (left_far - 4.0 * left_near + 3.0 * center) ** 2
    )
    smooth_middle = (
        13.0 / 12.0 * (left_near - 2.0 * center + right_near) ** 2
        + 0.25 * (left_near - right_near) ** 2
    )
    smooth_right = (
        13.0 / 12.0 * (center - 2.0 * right_near + right_far) ** 2
        + 0.25 * (3.0 * center - 4.0 * right_near + right_far) ** 2
    )
    weight_left = 0.1 / (WENO_EPS + smooth_left) ** 2
    weight_middle = 0.6 / (WENO_EPS + smooth_middle) ** 2
    weight_right = 0.3 / (WENO_EPS + smooth_right) ** 2
    guess_left = (2.0 * left_far - 7.0 * left_near + 11.0 * center) / 6.0
    guess_middle = (-left_near + 5.0 * center + 2.0 * right_near) / 6.0
    guess_right = (2.0 * center + 5.0 * right_near - right_far) / 6.0
    total = weight_left * guess_left + weight_middle * guess_middle + weight_right * guess_right
    return total / (weight_left + weight_middle + weight_right)


def sweep(padded, speeds, axis):
    count = padded.shape[axis] - 6
    plus_flux = jnp.maximum(speeds, 0.0)[:, None, None] * padded
    minus_flux = jnp.minimum(speeds, 0.0)[:, None, None] * padded

    def window(source, offset):
        return lax.slice_in_dim(source, offset, offset + count + 1, axis=axis)

    faces = weno_face(*(window(plus_flux, i) for i in (0, 1, 2, 3, 4)))
    faces = faces + weno_face(*(window(minus_flux, i) for i in (5, 4, 3, 2, 1)))
    return lax.slice_in_dim(faces, 1, count + 1, axis=axis) - lax.slice_in_dim(
        faces, 0, count, axis=axis
    )


def crossflow(padded, speed_y, speed_z):
    rows_part = sweep(padded[:, :, 3:-3], speed_y, 1)
    cols_part = sweep(padded[:, 3:-3, :], speed_z, 2)
    return rows_part + cols_part


def streamwise(field, factor):
    return field + factor * field**3 / (1.0 + field**2)


def slope(field, factor):
    return 1.0 + factor * field**2 * (3.0 + field**2) / (1.0 + field**2) ** 2


def correct(padded, current, upstream, diff, blocked, params):
    speed_y, speed_z, vigneron, coupling = params
    factor = vigneron[:, None, None]
    mixed = jnp.einsum("vw,wyz->vyz", coupling, current, precision=lax.Precision.HIGHEST)
    target = (
        streamwise(upstream, factor)
        - STEP_RATIO * crossflow(padded, speed_y, speed_z)
        + STEP_RATIO * mixed
        - (1.0 - factor) * diff
    )
    guess = current
    for newton_index in range(NEWTON):
        guess = guess - (streamwise(guess, factor) - target) / slope(guess, factor)
    return jnp.where(blocked[None], 0.0, guess)


def per_device(inflow, initial, solid, speed_y, speed_z, vigneron, coupling):
    params = (speed_y, speed_z, vigneron, coupling)
    sections = lax.axis_size("sec")
    position = lax.axis_index("sec")
    is_first = position == 0
    start_plane = initial[0]
    guess_above = passed_along(start_plane, "sec", 1)
    guess_above = jnp.where(is_first, inflow, guess_above)
    solid_tile = solid[0] != 0

    def station(upstream, diff):
        current = upstream
        for corrector_index in range(CORRECTORS):
            padded = extended(current, (("gy", 1), ("gz", 2)), 3)
            current = correct(padded, current, upstream, diff, solid_tile, params)
        return current

    def advance(step_index, carry):
        sent, own_prior, upstream_prior = carry
        received = passed_along(sent, "sec", 1)
        received = jnp.where(is_first, inflow, received)
        iterate = step_index - position + 1
        active = (iterate >= 1) & (iterate <= ITERS)
        updated = station(received, own_prior - upstream_prior)
        own_next = jnp.where(active, updated, own_prior)
        upstream_next = jnp.where(active, received, upstream_prior)
        return (own_next, own_next, upstream_next)

    result = lax.fori_loop(
        0, ITERS + sections - 1, advance, (start_plane, start_plane, guess_above)
    )
    return result[1][None]


LANES = 128
SLAB = 32
TILE = 256
MEMBERS = 8
PIECE = 32
GUARD = 16
LEFT = 40
ROWS = GUARD + LEFT + SLAB + LEFT + GUARD
CHUNK_IN = 72
CHUNK_OUT = 40
NEAR = 24
EDGE_ONE = 11 * SLAB + 6 * NEAR
EDGE_TWO = 11 * 8
CHANNELS = 17


def lane_iota():
    return lax.broadcasted_iota(jnp.int32, (8, LANES), 1)


def turned(value, shift):
    shift = shift % LANES
    return value if shift == 0 else pltpu.roll(value, shift, 1)


def slab_of(member, odd):
    sec, gy = member // 4, member % 4
    j = 2 * gy + (sec ^ (gy & 1))
    return jnp.where(odd, MEMBERS - 1 - j, j)


def pack_kernel(place, inflow, initial, solid, out, stacked, turned_ref, solids):
    sec, odd = place[0], place[1] == 1
    for group in range(2):
        for p in range(4):
            rows = pl.ds(p * PIECE, PIECE)
            if group == 0:
                stacked[rows, :] = initial[0, p]
            elif p == 0:
                stacked[rows, :] = initial[0, 4]
            else:
                stacked[rows, :] = inflow[jnp.minimum(3 * sec + p - 1, NVAR - 1)]
        for half in range(2):
            turned_ref[pl.ds(half * LANES, LANES), :] = stacked[:, half * LANES:(half + 1) * LANES].T
        for member in range(MEMBERS):
            j = slab_of(member, odd)
            out[member, pl.ds(group * SLAB, SLAB), :] = turned_ref[
                pl.ds(pl.multiple_of(j * SLAB, SLAB), SLAB), :
            ]
    solids[...] = jnp.zeros_like(solids)
    for half in range(2):
        solids[pl.ds(half * PIECE, PIECE), :] = solid[
            0, :, half * LANES:(half + 1) * LANES
        ].astype(jnp.float32)
    turned_ref[pl.ds(0, LANES), :] = solids[...].T
    quarter = lane_iota() // PIECE
    for member in range(MEMBERS):
        j = slab_of(member, odd)
        half, within = j // 4, j % 4
        packed = jnp.zeros((8, LANES), jnp.float32)
        for octet in range(4):
            piece = turned_ref[pl.ds(pl.multiple_of(within * SLAB + octet * 8, 8), 8), :]
            piece = pltpu.roll(piece, (PIECE * (octet - half)) % LANES, 1)
            packed = jnp.where(quarter == octet, piece, packed)
        out[member, pl.ds(2 * SLAB, 8), :] = packed


def assemble_kernel(got, own, right_one, left_one, right_two, left_two):
    quarter = lane_iota() // PIECE

    def gathered(sec, row, shift):
        value = None
        for gy in range(4):
            piece = turned(got[sec * 4 + gy, pl.ds(row, 8), :], PIECE * gy - shift)
            value = piece if value is None else jnp.where(quarter == gy, piece, value)
        return value

    def source(channel, octet):
        if channel < 3:
            return gathered(0, SLAB + 8 * octet, PIECE * (channel + 1))
        if channel < 5:
            return gathered(1, SLAB + 8 * octet, PIECE * (channel - 2))
        sec, v = (channel - 5) // 6, (channel - 5) % 6
        if v < 4:
            return gathered(sec, 8 * octet, PIECE * v)
        if v == 4:
            return gathered(sec, SLAB + 8 * octet, 0)
        return gathered(sec, 2 * SLAB, PIECE * octet)

    for channel in range(CHANNELS):
        for octet in range(4):
            value = source(channel, octet)
            own[channel, pl.ds(8 * octet, 8), :] = value
            if channel < 11:
                rows = pl.ds(channel * SLAB + 8 * octet, 8)
                right_one[rows, :] = value
                left_one[rows, :] = value
                if octet == 3:
                    right_two[pl.ds(8 * channel, 8), :] = value
                if octet == 0:
                    left_two[pl.ds(8 * channel, 8), :] = value
            else:
                at = 11 * SLAB + (channel - 11) * NEAR
                if octet > 0:
                    right_one[pl.ds(at + 8 * (octet - 1), 8), :] = value
                if octet < 3:
                    left_one[pl.ds(at + 8 * octet, 8), :] = value


def unpack_kernel(place, got, out, stacked, packed):
    odd = place[1] == 1
    quarter = lane_iota() // PIECE

    def member_of(j):
        j = jnp.where(odd, MEMBERS - 1 - j, j)
        gy = j // 2
        sec = (j % 2 + gy % 2) % 2
        return sec * 4 + gy

    for half in range(2):
        for within in range(4):
            member = member_of(4 * half + within)
            stacked[pl.ds(within * SLAB, SLAB), :] = got[member, pl.ds(0, SLAB), :]
        block = stacked[...].T
        for v in range(4):
            out[0, v, :, half * LANES:(half + 1) * LANES] = block[v * PIECE:(v + 1) * PIECE]
    for within in range(4):
        low = got[member_of(within), pl.ds(SLAB, 8), :]
        high = got[member_of(4 + within), pl.ds(SLAB, 8), :]
        for octet in range(4):
            packed[pl.ds(within * SLAB + 8 * octet, 8), :] = jnp.where(
                quarter == 0, turned(low, -PIECE * octet), turned(high, PIECE - PIECE * octet)
            )
    block = packed[...].T
    for half in range(2):
        out[0, 4, :, half * LANES:(half + 1) * LANES] = block[half * PIECE:(half + 1) * PIECE]


def weighted(d1, d2, d3, d4, t1, t2, t3):
    a = 3.0 * d2 - d1
    b = d2 + d3
    c = 3.0 * d3 - d4
    y1 = pltpu.reciprocal(t1 + a * a, approx=True)
    y2 = pltpu.reciprocal(t2 + b * b, approx=True)
    y3 = pltpu.reciprocal(t3 + c * c, approx=True)
    g1, g2, g3 = y1 * y1, y2 * y2, y3 * y3
    p1 = (a + a - d2) * (1.0 / 6.0)
    p2 = b + d3
    p3 = (c + d3) * 0.5
    over = g1 * p1 + g2 * p2 + g3 * p3
    under = g1 + 6.0 * g2 + 3.0 * g3
    return over * pltpu.reciprocal(under, approx=True)


def main_kernel(
    place, speed_y, speed_z, vigneron, coupling,
    own, from_left, from_right, from_left_two, from_right_two,
    out,
    inf, still, base, first, second, s0, s1, work_inf, delta, curve, face, blocked,
    across, delta_y, curve_y, face_y, rows_part,
):
    lane = lane_iota()
    center = GUARD + LEFT

    def fill(ref, channel, wide):
        ref[pl.ds(0, GUARD), :] = jnp.zeros((GUARD, LANES), jnp.float32)
        ref[pl.ds(ROWS - GUARD, GUARD), :] = jnp.zeros((GUARD, LANES), jnp.float32)
        ref[pl.ds(center, SLAB), :] = own[channel]
        if wide:
            ref[pl.ds(GUARD, 8), :] = from_left_two[pl.ds(8 * channel, 8), :]
            ref[pl.ds(GUARD + 8, SLAB), :] = from_left[pl.ds(SLAB * channel, SLAB), :]
            ref[pl.ds(center + SLAB, SLAB), :] = from_right[pl.ds(SLAB * channel, SLAB), :]
            ref[pl.ds(center + 2 * SLAB, 8), :] = from_right_two[pl.ds(8 * channel, 8), :]
        else:
            at = 11 * SLAB + (channel - 11) * NEAR
            zeros = jnp.zeros((16, LANES), jnp.float32)
            ref[pl.ds(GUARD, 16), :] = zeros
            ref[pl.ds(center - NEAR, NEAR), :] = from_left[pl.ds(at, NEAR), :]
            ref[pl.ds(center + SLAB, NEAR), :] = from_right[pl.ds(at, NEAR), :]
            ref[pl.ds(center + SLAB + NEAR, 16), :] = zeros

    for v in range(NVAR):
        fill(inf.at[v], v, True)
        fill(s0.at[0, v], 5 + v, True)
        fill(s1.at[v], 11 + v, False)
    fill(blocked.at[0], 10, True)
    fill(blocked.at[1], 16, False)
    slab, last = place[2], place[3]
    for octet in range(ROWS // 8):
        rows = pl.ds(8 * octet, 8)
        column = slab * SLAB + 8 * octet - center + lax.broadcasted_iota(jnp.int32, (8, LANES), 0)
        outside = (column < 0) | (column >= last)
        for station in range(2):
            blocked[station, rows, :] = jnp.where(
                outside | (blocked[station, rows, :] != 0.0), 0.0, 1.0
            )
    for ref in (first, second, s0.at[1]):
        for v in range(NVAR):
            ref[v] = jnp.zeros((ROWS, LANES), jnp.float32)
    for v in range(NVAR):
        across[v, pl.ds(0, GUARD), :] = jnp.zeros((GUARD, LANES), jnp.float32)
        across[v, pl.ds(GUARD + LANES, GUARD), :] = jnp.zeros((GUARD, LANES), jnp.float32)

    sy = [speed_y[v] for v in range(NVAR)]
    sz = [speed_z[v] for v in range(NVAR)]
    half_y = [0.5 * jnp.maximum(s, -s) for s in sy]
    half_z = [0.5 * jnp.maximum(s, -s) for s in sz]
    step_y = [jnp.where(s >= 0.0, 1, -1) for s in sy]
    step_z = [jnp.where(s >= 0.0, 1, -1) for s in sz]
    vig = [vigneron[v] for v in range(NVAR)]

    def newton(v, guess, target):
        for _ in range(NEWTON):
            r = pltpu.reciprocal(1.0 + guess * guess, approx=True)
            z = (2.0 * vig[v]) * r
            over = (z * (1.0 - r)) * guess + target
            under = z * (0.5 - r) + (1.0 + vig[v])
            guess = over * pltpu.reciprocal(under, approx=True)
        return guess

    def energy(v, field):
        r = pltpu.reciprocal(1.0 + field * field, approx=True)
        return field * ((1.0 + vig[v]) - vig[v] * r)

    def octet_rows(g):
        return pl.multiple_of(GUARD + 8 * g, 8)

    def pairs(low, high, body):
        def two(i, c):
            for k in range(2):
                body(octet_rows(low + 2 * i + k))
            return c
        lax.fori_loop(0, (high - low) // 2, two, 0)

    def differences(src, half, step, d_ref, t_ref):
        def body(at):
            for v in range(NVAR):
                here = src[v, pl.ds(at, 8), :]
                down = src[v, pl.ds(at + step[v], 8), :]
                up = src[v, pl.ds(at - step[v], 8), :]
                d = (down - here) * half[v]
                t = d - (here - up) * half[v]
                d_ref[v, pl.ds(at, 8), :] = d
                t_ref[v, pl.ds(at, 8), :] = (13.0 / 3.0) * (t * t) + WENO_EPS
        return body

    def faces(src, half, step, d_ref, t_ref, f_ref, shift=None):
        def body(at):
            for v in range(NVAR):
                s = step[v]
                rows = at if shift is None else at + shift[v]
                d3 = d_ref[v, pl.ds(rows, 8), :]
                d2 = d_ref[v, pl.ds(rows - s, 8), :]
                d1 = d_ref[v, pl.ds(rows - 2 * s, 8), :]
                d4 = d_ref[v, pl.ds(rows + s, 8), :]
                t1 = t_ref[v, pl.ds(rows - s, 8), :]
                t2 = t_ref[v, pl.ds(rows, 8), :]
                t3 = t_ref[v, pl.ds(rows + s, 8), :]
                f_ref[v, pl.ds(rows, 8), :] = half[v] * src[v, pl.ds(rows, 8), :] + weighted(
                    d1, d2, d3, d4, t1, t2, t3
                )
        return body

    def fluxes(src, g0):
        for v in range(NVAR):
            across[v, pl.ds(GUARD, LANES), :] = src[v, pl.ds(GUARD - 8, LANES), :].T
        pairs(-1, 17, differences(across, half_y, step_y, delta_y, curve_y))
        row_faces = faces(across, half_y, step_y, delta_y, curve_y, face_y)
        pairs(0, 16, row_faces)
        faces(across, half_y, step_y, delta_y, curve_y, face_y,
              [jnp.where(s >= 0.0, -8, LANES) for s in sy])(GUARD)
        for v in range(NVAR):
            rows_part[v] = (
                face_y[v, pl.ds(GUARD, LANES), :] - face_y[v, pl.ds(GUARD - step_y[v], LANES), :]
            ).T
        pairs(g0 - 1, 15 - g0, differences(src, half_z, step_z, delta, curve))
        pairs(g0, 14 - g0, faces(src, half_z, step_z, delta, curve, face))

    def sources(src, at):
        field = [src[v, pl.ds(at, 8), :] for v in range(NVAR)]
        result = []
        for v in range(NVAR):
            columns = face[v, pl.ds(at, 8), :] - face[v, pl.ds(at - step_z[v], 8), :]
            rows = rows_part[v, pl.ds(pl.multiple_of(at - (GUARD - 8), 8), 8), :]
            mixed = (STEP_RATIO * coupling[v, 0]) * field[0]
            for w in range(1, NVAR):
                mixed = mixed + (STEP_RATIO * coupling[v, w]) * field[w]
            result.append(mixed - (2.0 * STEP_RATIO) * (rows + columns))
        return field, result

    def corrector(src, dst, station, g0):
        fluxes(src, g0)

        def step(at):
            field, terms = sources(src, at)
            fluid = blocked[station, pl.ds(at, 8), :]
            for v in range(NVAR):
                value = newton(v, field[v], still[v, pl.ds(at, 8), :] + terms[v])
                dst[v, pl.ds(at, 8), :] = jnp.where(fluid != 0.0, value, 0.0)

        pairs(g0, 14 - g0, step)

    fluxes(inf, 0)

    def prepare(at):
        field, terms = sources(inf, at)
        for v in range(NVAR):
            base[v, pl.ds(at, 8), :] = energy(v, field[v])
            work_inf[v, pl.ds(at, 8), :] = terms[v]

    pairs(0, 14, prepare)

    def iterate(k, carry):
        old, new = s0.at[k % 2], s0.at[1 - k % 2]

        def first_of_0(at):
            fluid = blocked[0, pl.ds(at, 8), :]
            for v in range(NVAR):
                here = inf[v, pl.ds(at, 8), :]
                prior = old[v, pl.ds(at, 8), :]
                fixed = base[v, pl.ds(at, 8), :] - (1.0 - vig[v]) * (prior - here)
                still[v, pl.ds(at, 8), :] = fixed
                value = newton(v, here, fixed + work_inf[v, pl.ds(at, 8), :])
                first[v, pl.ds(at, 8), :] = jnp.where(fluid != 0.0, value, 0.0)

        g0 = (6 + 6 * k) // 8
        pairs(g0, 14 - g0, first_of_0)
        corrector(first, second, 0, (9 + 6 * k) // 8)
        corrector(second, new, 0, (12 + 6 * k) // 8)

        def start_of_1(at):
            for v in range(NVAR):
                above = new[v, pl.ds(at, 8), :]
                prior = s1[v, pl.ds(at, 8), :] - old[v, pl.ds(at, 8), :]
                still[v, pl.ds(at, 8), :] = energy(v, above) - (1.0 - vig[v]) * prior

        g0 = (15 + 6 * k) // 8
        pairs(g0, 14 - g0, start_of_1)
        corrector(new, first, 1, g0)
        corrector(first, second, 1, (18 + 6 * k) // 8)
        corrector(second, s1, 1, (21 + 6 * k) // 8)
        return carry

    lax.fori_loop(0, ITERS, iterate, 0)

    quarter = lane // PIECE
    for station, result in enumerate((s0.at[ITERS % 2], s1)):
        for octet in range(4):
            field = [result[v, pl.ds(center + 8 * octet, 8), :] for v in range(NVAR)]
            for gy in range(4):
                member = station * 4 + gy
                value = None
                for p in range(4):
                    piece = turned(field[p], PIECE * (p - gy))
                    value = piece if value is None else jnp.where(quarter == p, piece, value)
                out[member, pl.ds(8 * octet, 8), :] = value
                piece = turned(field[4], PIECE * (octet - gy))
                if octet > 0:
                    piece = jnp.where(quarter == octet, piece, out[member, pl.ds(SLAB, 8), :])
                out[member, pl.ds(SLAB, 8), :] = piece


def slabs_per_device(inflow, initial, solid, speed_y, speed_z, vigneron, coupling):
    mesh_axes = ("sec", "gy", "gz")
    nz_parts = lax.axis_size("gz")
    sec, gy, gz = (lax.axis_index(a) for a in mesh_axes)
    path = []
    for z in range(nz_parts):
        members = [(s, y) for y in range(4) for s in ((0, 1) if y % 2 == 0 else (1, 0))]
        path += [(s * 4 + y) * nz_parts + z for s, y in (members if z % 2 == 0 else members[::-1])]

    def along(value, steps):
        count = len(path)
        low, high = max(0, -steps), min(count, count - steps)
        return lax.ppermute(value, mesh_axes, [(path[i], path[i + steps]) for i in range(low, high)])

    odd = gz % 2
    j = 2 * gy + (sec + gy) % 2
    slab = gz * MEMBERS + jnp.where(odd == 1, MEMBERS - 1 - j, j)
    place = jnp.stack(
        [sec, odd, slab, jnp.asarray(len(path) * SLAB, jnp.int32)]
    ).astype(jnp.int32)

    smem = pl.BlockSpec(memory_space=pltpu.SMEM)
    vmem = pl.BlockSpec(memory_space=pltpu.VMEM)
    f32 = functools.partial(jax.ShapeDtypeStruct, dtype=jnp.float32)

    packed = pl.pallas_call(
        pack_kernel,
        out_shape=f32((MEMBERS, CHUNK_IN, LANES)),
        in_specs=[smem, vmem, vmem, vmem],
        out_specs=vmem,
        scratch_shapes=[
            pltpu.VMEM((LANES, TILE), jnp.float32),
            pltpu.VMEM((TILE, LANES), jnp.float32),
            pltpu.VMEM((LANES, LANES), jnp.float32),
        ],
        name="pack",
    )(place, inflow, initial, solid)
    got = lax.all_to_all(packed, ("sec", "gy"), 0, 0)
    own, right_one, left_one, right_two, left_two = pl.pallas_call(
        assemble_kernel,
        out_shape=[
            f32((CHANNELS, SLAB, LANES)),
            f32((EDGE_ONE, LANES)),
            f32((EDGE_ONE, LANES)),
            f32((EDGE_TWO, LANES)),
            f32((EDGE_TWO, LANES)),
        ],
        in_specs=[vmem],
        out_specs=[vmem] * 5,
        name="assemble",
    )(got)
    window = pltpu.VMEM((NVAR, ROWS, LANES), jnp.float32)
    plane = pltpu.VMEM((NVAR, LANES + 2 * GUARD, LANES), jnp.float32)
    sent = pl.pallas_call(
        main_kernel,
        out_shape=f32((MEMBERS, CHUNK_OUT, LANES)),
        in_specs=[smem] * 5 + [vmem] * 5,
        out_specs=vmem,
        scratch_shapes=[
            window, window, window, window, window,
            pltpu.VMEM((2, NVAR, ROWS, LANES), jnp.float32),
            window, window, window, window, window,
            pltpu.VMEM((2, ROWS, LANES), jnp.float32),
            plane, plane, plane, plane, pltpu.VMEM((NVAR, LANES, LANES), jnp.float32),
        ],
        compiler_params=pltpu.CompilerParams(vmem_limit_bytes=32 * 1024 * 1024),
        name="march",
    )(
        place, speed_y, speed_z, vigneron, coupling,
        own, along(right_one, 1), along(left_one, -1), along(right_two, 2), along(left_two, -2),
    )
    returned = lax.all_to_all(sent, ("sec", "gy"), 0, 0)
    return pl.pallas_call(
        unpack_kernel,
        out_shape=f32((1, NVAR, PIECE, TILE)),
        in_specs=[smem, vmem],
        out_specs=vmem,
        scratch_shapes=[
            pltpu.VMEM((LANES, LANES), jnp.float32),
            pltpu.VMEM((LANES, LANES), jnp.float32),
        ],
        name="unpack",
    )(place, returned)


def chosen(*args):
    inflow, initial = args[0], args[1]
    fits = (
        lax.axis_size("sec") == 2
        and lax.axis_size("gy") == 4
        and inflow.shape == (NVAR, PIECE, TILE)
        and initial.shape == (1, NVAR, PIECE, TILE)
    )
    return slabs_per_device(*args) if fits else per_device(*args)


def solution(mesh):
    return jax.shard_map(
        chosen,
        mesh=mesh,
        in_specs=(
            P(None, "gy", "gz"),
            P("sec", None, "gy", "gz"),
            P("sec", "gy", "gz"),
            P(),
            P(),
            P(),
            P(),
        ),
        out_specs=P("sec", None, "gy", "gz"),
        check_vma=False,
    )
```

```python
import functools

import jax
import jax.numpy as jnp
from jax import lax
from jax.experimental import pallas as pl
from jax.experimental.pallas import tpu as pltpu
from jax.sharding import PartitionSpec as P

NVAR = 5
ITERS = 4
CORRECTORS = 3
NEWTON = 2

STEP_RATIO = 0.25
WENO_EPS = 1e-06


def passed_along(value, axis, steps):
    count = lax.axis_size(axis)
    initial, last = (max(0, -steps), min(count, count - steps))
    return lax.ppermute(value, axis, [(source, source + steps) for source in range(initial, last)])


def extended(block, sides, width):
    for axis, dim in sides:
        count = lax.axis_size(axis)
        forward = [(i, i + 1) for i in range(count - 1)]
        backward = [(target, source) for source, target in forward]
        low = lax.ppermute(
            lax.slice_in_dim(block, block.shape[dim] - width, None, axis=dim), axis, forward
        )
        high = lax.ppermute(lax.slice_in_dim(block, 0, width, axis=dim), axis, backward)
        block = jnp.concatenate([low, block, high], axis=dim)
    return block


def weno_face(left_far, left_near, center, right_near, right_far):
    smooth_left = (
        13.0 / 12.0 * (left_far - 2.0 * left_near + center) ** 2
        + 0.25 * (left_far - 4.0 * left_near + 3.0 * center) ** 2
    )
    smooth_middle = (
        13.0 / 12.0 * (left_near - 2.0 * center + right_near) ** 2
        + 0.25 * (left_near - right_near) ** 2
    )
    smooth_right = (
        13.0 / 12.0 * (center - 2.0 * right_near + right_far) ** 2
        + 0.25 * (3.0 * center - 4.0 * right_near + right_far) ** 2
    )
    weight_left = 0.1 / (WENO_EPS + smooth_left) ** 2
    weight_middle = 0.6 / (WENO_EPS + smooth_middle) ** 2
    weight_right = 0.3 / (WENO_EPS + smooth_right) ** 2
    guess_left = (2.0 * left_far - 7.0 * left_near + 11.0 * center) / 6.0
    guess_middle = (-left_near + 5.0 * center + 2.0 * right_near) / 6.0
    guess_right = (2.0 * center + 5.0 * right_near - right_far) / 6.0
    total = weight_left * guess_left + weight_middle * guess_middle + weight_right * guess_right
    return total / (weight_left + weight_middle + weight_right)


def sweep(padded, speeds, axis):
    count = padded.shape[axis] - 6
    plus_flux = jnp.maximum(speeds, 0.0)[:, None, None] * padded
    minus_flux = jnp.minimum(speeds, 0.0)[:, None, None] * padded

    def window(source, offset):
        return lax.slice_in_dim(source, offset, offset + count + 1, axis=axis)

    faces = weno_face(*(window(plus_flux, i) for i in (0, 1, 2, 3, 4)))
    faces = faces + weno_face(*(window(minus_flux, i) for i in (5, 4, 3, 2, 1)))
    return lax.slice_in_dim(faces, 1, count + 1, axis=axis) - lax.slice_in_dim(
        faces, 0, count, axis=axis
    )


def crossflow(padded, speed_y, speed_z):
    rows_part = sweep(padded[:, :, 3:-3], speed_y, 1)
    cols_part = sweep(padded[:, 3:-3, :], speed_z, 2)
    return rows_part + cols_part


def streamwise(field, factor):
    return field + factor * field**3 / (1.0 + field**2)


def slope(field, factor):
    return 1.0 + factor * field**2 * (3.0 + field**2) / (1.0 + field**2) ** 2


def correct(padded, current, upstream, diff, blocked, params):
    speed_y, speed_z, vigneron, coupling = params
    factor = vigneron[:, None, None]
    mixed = jnp.einsum("vw,wyz->vyz", coupling, current, precision=lax.Precision.HIGHEST)
    target = (
        streamwise(upstream, factor)
        - STEP_RATIO * crossflow(padded, speed_y, speed_z)
        + STEP_RATIO * mixed
        - (1.0 - factor) * diff
    )
    guess = current
    for newton_index in range(NEWTON):
        guess = guess - (streamwise(guess, factor) - target) / slope(guess, factor)
    return jnp.where(blocked[None], 0.0, guess)


def per_device(inflow, initial, solid, speed_y, speed_z, vigneron, coupling):
    params = (speed_y, speed_z, vigneron, coupling)
    sections = lax.axis_size("sec")
    position = lax.axis_index("sec")
    is_first = position == 0
    start_plane = initial[0]
    guess_above = passed_along(start_plane, "sec", 1)
    guess_above = jnp.where(is_first, inflow, guess_above)
    solid_tile = solid[0] != 0

    def station(upstream, diff):
        current = upstream
        for corrector_index in range(CORRECTORS):
            padded = extended(current, (("gy", 1), ("gz", 2)), 3)
            current = correct(padded, current, upstream, diff, solid_tile, params)
        return current

    def advance(step_index, carry):
        sent, own_prior, upstream_prior = carry
        received = passed_along(sent, "sec", 1)
        received = jnp.where(is_first, inflow, received)
        iterate = step_index - position + 1
        active = (iterate >= 1) & (iterate <= ITERS)
        updated = station(received, own_prior - upstream_prior)
        own_next = jnp.where(active, updated, own_prior)
        upstream_next = jnp.where(active, received, upstream_prior)
        return (own_next, own_next, upstream_next)

    result = lax.fori_loop(
        0, ITERS + sections - 1, advance, (start_plane, start_plane, guess_above)
    )
    return result[1][None]


LANES = 128
SLAB = 32
TILE = 256
MEMBERS = 8
PIECE = 32
GUARD = 16
LEFT = 40
ROWS = GUARD + LEFT + SLAB + LEFT + GUARD
CHUNK_IN = 72
CHUNK_OUT = 40
NEAR = 24
EDGE_ONE = 11 * SLAB + 6 * NEAR
EDGE_TWO = 11 * 8
CHANNELS = 17


def lane_iota():
    return lax.broadcasted_iota(jnp.int32, (8, LANES), 1)


def turned(value, shift):
    shift = shift % LANES
    return value if shift == 0 else pltpu.roll(value, shift, 1)


def slab_of(member, odd):
    sec, gy = member // 4, member % 4
    j = 2 * gy + (sec ^ (gy & 1))
    return jnp.where(odd, MEMBERS - 1 - j, j)


def pack_kernel(place, inflow, initial, solid, out, stacked, turned_ref, solids):
    sec, odd = place[0], place[1] == 1
    for group in range(2):
        for p in range(4):
            rows = pl.ds(p * PIECE, PIECE)
            if group == 0:
                stacked[rows, :] = initial[0, p]
            elif p == 0:
                stacked[rows, :] = initial[0, 4]
            else:
                stacked[rows, :] = inflow[jnp.minimum(3 * sec + p - 1, NVAR - 1)]
        for half in range(2):
            turned_ref[pl.ds(half * LANES, LANES), :] = stacked[:, half * LANES:(half + 1) * LANES].T
        for member in range(MEMBERS):
            j = slab_of(member, odd)
            out[member, pl.ds(group * SLAB, SLAB), :] = turned_ref[
                pl.ds(pl.multiple_of(j * SLAB, SLAB), SLAB), :
            ]
    solids[...] = jnp.zeros_like(solids)
    for half in range(2):
        solids[pl.ds(half * PIECE, PIECE), :] = solid[
            0, :, half * LANES:(half + 1) * LANES
        ].astype(jnp.float32)
    turned_ref[pl.ds(0, LANES), :] = solids[...].T
    quarter = lane_iota() // PIECE
    for member in range(MEMBERS):
        j = slab_of(member, odd)
        half, within = j // 4, j % 4
        packed = jnp.zeros((8, LANES), jnp.float32)
        for octet in range(4):
            piece = turned_ref[pl.ds(pl.multiple_of(within * SLAB + octet * 8, 8), 8), :]
            piece = pltpu.roll(piece, (PIECE * (octet - half)) % LANES, 1)
            packed = jnp.where(quarter == octet, piece, packed)
        out[member, pl.ds(2 * SLAB, 8), :] = packed


def assemble_kernel(got, own, right_one, left_one, right_two, left_two):
    quarter = lane_iota() // PIECE

    def gathered(sec, row, shift):
        value = None
        for gy in range(4):
            piece = turned(got[sec * 4 + gy, pl.ds(row, 8), :], PIECE * gy - shift)
            value = piece if value is None else jnp.where(quarter == gy, piece, value)
        return value

    def source(channel, octet):
        if channel < 3:
            return gathered(0, SLAB + 8 * octet, PIECE * (channel + 1))
        if channel < 5:
            return gathered(1, SLAB + 8 * octet, PIECE * (channel - 2))
        sec, v = (channel - 5) // 6, (channel - 5) % 6
        if v < 4:
            return gathered(sec, 8 * octet, PIECE * v)
        if v == 4:
            return gathered(sec, SLAB + 8 * octet, 0)
        return gathered(sec, 2 * SLAB, PIECE * octet)

    for channel in range(CHANNELS):
        for octet in range(4):
            value = source(channel, octet)
            own[channel, pl.ds(8 * octet, 8), :] = value
            if channel < 11:
                rows = pl.ds(channel * SLAB + 8 * octet, 8)
                right_one[rows, :] = value
                left_one[rows, :] = value
                if octet == 3:
                    right_two[pl.ds(8 * channel, 8), :] = value
                if octet == 0:
                    left_two[pl.ds(8 * channel, 8), :] = value
            else:
                at = 11 * SLAB + (channel - 11) * NEAR
                if octet > 0:
                    right_one[pl.ds(at + 8 * (octet - 1), 8), :] = value
                if octet < 3:
                    left_one[pl.ds(at + 8 * octet, 8), :] = value


def unpack_kernel(place, got, out, stacked, packed):
    odd = place[1] == 1
    quarter = lane_iota() // PIECE

    def member_of(j):
        j = jnp.where(odd, MEMBERS - 1 - j, j)
        gy = j // 2
        sec = (j % 2 + gy % 2) % 2
        return sec * 4 + gy

    for half in range(2):
        for within in range(4):
            member = member_of(4 * half + within)
            stacked[pl.ds(within * SLAB, SLAB), :] = got[member, pl.ds(0, SLAB), :]
        block = stacked[...].T
        for v in range(4):
            out[0, v, :, half * LANES:(half + 1) * LANES] = block[v * PIECE:(v + 1) * PIECE]
    for within in range(4):
        low = got[member_of(within), pl.ds(SLAB, 8), :]
        high = got[member_of(4 + within), pl.ds(SLAB, 8), :]
        for octet in range(4):
            packed[pl.ds(within * SLAB + 8 * octet, 8), :] = jnp.where(
                quarter == 0, turned(low, -PIECE * octet), turned(high, PIECE - PIECE * octet)
            )
    block = packed[...].T
    for half in range(2):
        out[0, 4, :, half * LANES:(half + 1) * LANES] = block[half * PIECE:(half + 1) * PIECE]


def weighted(d1, d2, d3, d4, t1, t2, t3):
    a = 3.0 * d2 - d1
    b = d2 + d3
    c = 3.0 * d3 - d4
    y1 = pltpu.reciprocal(t1 + a * a, approx=True)
    y2 = pltpu.reciprocal(t2 + b * b, approx=True)
    y3 = pltpu.reciprocal(t3 + c * c, approx=True)
    g1, g2, g3 = (1.0 / 6.0) * (y1 * y1), y2 * y2, 0.5 * (y3 * y3)
    over = g1 * (a + a - d2) + g2 * (b + d3) + g3 * (c + d3)
    under = g1 + g2 + g3
    return over * pltpu.reciprocal(under, approx=True)


def main_kernel(
    place, speed_y, speed_z, vigneron, coupling,
    own, from_left, from_right, from_left_two, from_right_two,
    out,
    inf, still, base, cur, s0, s1, work_inf, delta, curve, face, rows_part, blocked, half_block, *per_block,
):
    across, delta_y, curve_y, face_y = (per_block[NVAR * i:NVAR * (i + 1)] for i in range(4))
    lane = lane_iota()
    center = GUARD + LEFT

    def fill(ref, channel, wide):
        ref[pl.ds(0, GUARD), :] = jnp.zeros((GUARD, LANES), jnp.float32)
        ref[pl.ds(ROWS - GUARD, GUARD), :] = jnp.zeros((GUARD, LANES), jnp.float32)
        ref[pl.ds(center, SLAB), :] = own[channel]
        if wide:
            ref[pl.ds(GUARD, 8), :] = from_left_two[pl.ds(8 * channel, 8), :]
            ref[pl.ds(GUARD + 8, SLAB), :] = from_left[pl.ds(SLAB * channel, SLAB), :]
            ref[pl.ds(center + SLAB, SLAB), :] = from_right[pl.ds(SLAB * channel, SLAB), :]
            ref[pl.ds(center + 2 * SLAB, 8), :] = from_right_two[pl.ds(8 * channel, 8), :]
        else:
            at = 11 * SLAB + (channel - 11) * NEAR
            zeros = jnp.zeros((16, LANES), jnp.float32)
            ref[pl.ds(GUARD, 16), :] = zeros
            ref[pl.ds(center - NEAR, NEAR), :] = from_left[pl.ds(at, NEAR), :]
            ref[pl.ds(center + SLAB, NEAR), :] = from_right[pl.ds(at, NEAR), :]
            ref[pl.ds(center + SLAB + NEAR, 16), :] = zeros

    for v in range(NVAR):
        fill(inf.at[v], v, True)
        fill(s0.at[v], 5 + v, True)
        fill(cur.at[v], 11 + v, False)
    fill(blocked.at[0], 10, True)
    fill(blocked.at[1], 16, False)
    slab, last = place[2], place[3]
    for octet in range(ROWS // 8):
        rows = pl.ds(8 * octet, 8)
        column = slab * SLAB + 8 * octet - center + lax.broadcasted_iota(jnp.int32, (8, LANES), 0)
        outside = (column < 0) | (column >= last)
        for station in range(2):
            blocked[station, rows, :] = jnp.where(
                outside | (blocked[station, rows, :] != 0.0), 0.0, 1.0
            )
    for v in range(NVAR):
        across[v][pl.ds(0, GUARD), :] = jnp.zeros((GUARD, LANES), jnp.float32)
        across[v][pl.ds(GUARD + LANES, GUARD), :] = jnp.zeros((GUARD, LANES), jnp.float32)

    sy = [speed_y[v] for v in range(NVAR)]
    sz = [speed_z[v] for v in range(NVAR)]
    half_y = [0.5 * jnp.maximum(s, -s) for s in sy]
    half_z = [0.5 * jnp.maximum(s, -s) for s in sz]
    step_y = [jnp.where(s >= 0.0, 1, -1) for s in sy]
    step_z = [jnp.where(s >= 0.0, 1, -1) for s in sz]
    vig = [vigneron[v] for v in range(NVAR)]
    forward = [(s >= 0.0).astype(jnp.int32) for s in sy]
    ahead = sum(forward)
    rank, seen = [], 0
    for v in range(NVAR):
        rank.append(jnp.where(forward[v] == 1, seen, ahead + v - seen))
        seen = seen + forward[v]

    def nth(r):
        return sum(jnp.where(rank[v] == r, v, 0) for v in range(NVAR))

    lone = jnp.where(ahead % 2 == 0, NVAR - 1, 0)
    begin = 1 - jnp.minimum(lone, 1)
    couples = [(nth(begin), nth(begin + 1)), (nth(begin + 2), nth(begin + 3)), (nth(lone), nth(lone))]
    for b, (va, vb) in enumerate(couples):
        both = [speed_y[va], speed_y[vb]]
        both = [0.5 * jnp.maximum(s, -s) for s in both]
        half_block[b] = jnp.where(lane < LANES // 2, both[0], both[1])
    mix = [[STEP_RATIO * coupling[v, w] for w in range(NVAR)] for v in range(NVAR)]

    def newton(v, guess, target):
        for _ in range(NEWTON):
            r = pltpu.reciprocal(1.0 + guess * guess, approx=True)
            z = (2.0 * vig[v]) * r
            over = (z * (1.0 - r)) * guess + target
            under = z * (0.5 - r) + (1.0 + vig[v])
            guess = over * pltpu.reciprocal(under, approx=True)
        return guess

    def energy(v, field):
        r = pltpu.reciprocal(1.0 + field * field, approx=True)
        return field * ((1.0 + vig[v]) - vig[v] * r)

    def octet_rows(g):
        return pl.multiple_of(GUARD + 8 * g, 8)

    def pairs(low, high, body):
        def two(i, c):
            for k in range(2):
                body(octet_rows(low + 2 * i + k))
            return c
        lax.fori_loop(0, (high - low) // 2, two, 0)

    def differences(src, half, step, d_ref, t_ref, at):
        here = src[pl.ds(at, 8), :]
        down = src[pl.ds(at + step, 8), :]
        up = src[pl.ds(at - step, 8), :]
        d = down - here
        t = d - (here - up)
        d_ref[pl.ds(at, 8), :] = d * half
        t_ref[pl.ds(at, 8), :] = ((13.0 / 3.0) * (half * half)) * (t * t) + WENO_EPS

    def faces(src, half, step, d_ref, t_ref, f_ref, at):
        d3 = d_ref[pl.ds(at, 8), :]
        d2 = d_ref[pl.ds(at - step, 8), :]
        d1 = d_ref[pl.ds(at - 2 * step, 8), :]
        d4 = d_ref[pl.ds(at + step, 8), :]
        t1 = t_ref[pl.ds(at - step, 8), :]
        t2 = t_ref[pl.ds(at, 8), :]
        t3 = t_ref[pl.ds(at + step, 8), :]
        f_ref[pl.ds(at, 8), :] = (6.0 * half) * src[pl.ds(at, 8), :] + weighted(
            d1, d2, d3, d4, t1, t2, t3
        )

    def fluxes(src, n):
        g0 = 7 - n // 2
        octets = [GUARD + 8 * g for g in range(g0, g0 + n)]
        if n <= 8:
            middle = LANES // 2
            blocks = []
            for b, (va, vb) in enumerate(couples):
                two = [src[v, pl.ds(octets[0] - 8 * (4 - n // 2), middle), :] for v in (va, vb)]
                across[b][pl.ds(GUARD, LANES), :] = jnp.concatenate(two, axis=0).T
                blocks.append((half_block[b], jnp.where(speed_y[va] >= 0.0, 1, -1)))
        else:
            for v in range(NVAR):
                across[v][pl.ds(GUARD, LANES), :] = src[v, pl.ds(GUARD - 8, LANES), :].T
            blocks = list(zip(half_y, step_y))
        for at in [octets[0] - 8] + octets + [octets[-1] + 8]:
            for v in range(NVAR):
                differences(src.at[v], half_z[v], step_z[v], delta.at[v], curve.at[v], at)
        for b, (half, step) in enumerate(blocks):
            row = (across[b], half, step, delta_y[b], curve_y[b])
            for i in range(-1, 17):
                differences(*row, GUARD + 8 * i)
            for i in range(16):
                faces(*row, face_y[b], GUARD + 8 * i)
            faces(*row, face_y[b], GUARD + jnp.where(step > 0, -8, LANES))
            change = (
                face_y[b][pl.ds(GUARD, LANES), :] - face_y[b][pl.ds(GUARD - step, LANES), :]
            ).T
            if n <= 8:
                rows = pl.ds(octets[0] - 8 * (4 - n // 2) - (GUARD - 8), middle)
                rows_part[couples[b][0], rows, :] = change[:middle]
                rows_part[couples[b][1], rows, :] = change[middle:]
            else:
                rows_part[b] = change
        for at in octets:
            for v in range(NVAR):
                faces(src.at[v], half_z[v], step_z[v], delta.at[v], curve.at[v], face.at[v], at)
        return octets

    def sources(src, at):
        field = [src[v, pl.ds(at, 8), :] for v in range(NVAR)]
        result = []
        for v in range(NVAR):
            columns = face[v, pl.ds(at, 8), :] - face[v, pl.ds(at - step_z[v], 8), :]
            rows = rows_part[v, pl.ds(at - (GUARD - 8), 8), :]
            mixed = mix[v][0] * field[0]
            for w in range(1, NVAR):
                mixed = mixed + mix[v][w] * field[w]
            result.append(mixed - (STEP_RATIO / 3.0) * (rows + columns))
        return field, result

    def corrector(station, n):
        for at in fluxes(cur, n):
            field, terms = sources(cur, at)
            fluid = blocked[station, pl.ds(at, 8), :] != 0.0
            for v in range(NVAR):
                value = newton(v, field[v], still[v, pl.ds(at, 8), :] + terms[v])
                cur[v, pl.ds(at, 8), :] = jnp.where(fluid, value, 0.0)

    for at in fluxes(inf, 14):
        field, terms = sources(inf, at)
        for v in range(NVAR):
            base[v, pl.ds(at, 8), :] = energy(v, field[v])
            work_inf[v, pl.ds(at, 8), :] = terms[v]

    def first_of_0(at):
        fluid = blocked[0, pl.ds(at, 8), :] != 0.0
        for v in range(NVAR):
            s1[v, pl.ds(at, 8), :] = cur[v, pl.ds(at, 8), :]
            here = inf[v, pl.ds(at, 8), :]
            prior = s0[v, pl.ds(at, 8), :]
            fixed = base[v, pl.ds(at, 8), :] - (1.0 - vig[v]) * (prior - here)
            still[v, pl.ds(at, 8), :] = fixed
            value = newton(v, here, fixed + work_inf[v, pl.ds(at, 8), :])
            cur[v, pl.ds(at, 8), :] = jnp.where(fluid, value, 0.0)

    def start_of_1(at):
        for v in range(NVAR):
            above = cur[v, pl.ds(at, 8), :]
            prior = s1[v, pl.ds(at, 8), :] - s0[v, pl.ds(at, 8), :]
            still[v, pl.ds(at, 8), :] = energy(v, above) - (1.0 - vig[v]) * prior
            s0[v, pl.ds(at, 8), :] = above

    def pass_of(t, carry):
        k, c = t // 5, t % 5

        @pl.when(c == 0)
        def _():
            g0 = (6 + 6 * k) // 8
            pairs(g0, 14 - g0, first_of_0)

        @pl.when(c == 2)
        def _():
            g0 = (12 + 6 * k) // 8
            pairs(g0, 14 - g0, start_of_1)

        station = (c >= 2).astype(jnp.int32)
        g0 = (9 + 6 * k + 3 * c) // 8
        for n in (12, 10, 8, 6):
            @pl.when(g0 == 7 - n // 2)
            def _(n=n):
                corrector(station, n)
        return carry

    lax.fori_loop(0, 5 * ITERS, pass_of, 0)

    quarter = lane // PIECE
    for station, result in enumerate((s0, cur)):
        for octet in range(4):
            field = [result[v, pl.ds(center + 8 * octet, 8), :] for v in range(NVAR)]
            for gy in range(4):
                member = station * 4 + gy
                value = None
                for p in range(4):
                    piece = turned(field[p], PIECE * (p - gy))
                    value = piece if value is None else jnp.where(quarter == p, piece, value)
                out[member, pl.ds(8 * octet, 8), :] = value
                piece = turned(field[4], PIECE * (octet - gy))
                if octet > 0:
                    piece = jnp.where(quarter == octet, piece, out[member, pl.ds(SLAB, 8), :])
                out[member, pl.ds(SLAB, 8), :] = piece


def slabs_per_device(inflow, initial, solid, speed_y, speed_z, vigneron, coupling):
    mesh_axes = ("sec", "gy", "gz")
    nz_parts = lax.axis_size("gz")
    sec, gy, gz = (lax.axis_index(a) for a in mesh_axes)
    path = []
    for z in range(nz_parts):
        members = [(s, y) for y in range(4) for s in ((0, 1) if y % 2 == 0 else (1, 0))]
        path += [(s * 4 + y) * nz_parts + z for s, y in (members if z % 2 == 0 else members[::-1])]

    def along(value, steps):
        count = len(path)
        low, high = max(0, -steps), min(count, count - steps)
        return lax.ppermute(value, mesh_axes, [(path[i], path[i + steps]) for i in range(low, high)])

    odd = gz % 2
    j = 2 * gy + (sec + gy) % 2
    slab = gz * MEMBERS + jnp.where(odd == 1, MEMBERS - 1 - j, j)
    place = jnp.stack(
        [sec, odd, slab, jnp.asarray(len(path) * SLAB, jnp.int32)]
    ).astype(jnp.int32)

    smem = pl.BlockSpec(memory_space=pltpu.SMEM)
    vmem = pl.BlockSpec(memory_space=pltpu.VMEM)
    f32 = functools.partial(jax.ShapeDtypeStruct, dtype=jnp.float32)

    packed = pl.pallas_call(
        pack_kernel,
        out_shape=f32((MEMBERS, CHUNK_IN, LANES)),
        in_specs=[smem, vmem, vmem, vmem],
        out_specs=vmem,
        scratch_shapes=[
            pltpu.VMEM((LANES, TILE), jnp.float32),
            pltpu.VMEM((TILE, LANES), jnp.float32),
            pltpu.VMEM((LANES, LANES), jnp.float32),
        ],
        name="pack",
    )(place, inflow, initial, solid)
    got = lax.all_to_all(packed, ("sec", "gy"), 0, 0)
    own, right_one, left_one, right_two, left_two = pl.pallas_call(
        assemble_kernel,
        out_shape=[
            f32((CHANNELS, SLAB, LANES)),
            f32((EDGE_ONE, LANES)),
            f32((EDGE_ONE, LANES)),
            f32((EDGE_TWO, LANES)),
            f32((EDGE_TWO, LANES)),
        ],
        in_specs=[vmem],
        out_specs=[vmem] * 5,
        name="assemble",
    )(got)
    window = pltpu.VMEM((NVAR, ROWS, LANES), jnp.float32)
    sent = pl.pallas_call(
        main_kernel,
        out_shape=f32((MEMBERS, CHUNK_OUT, LANES)),
        in_specs=[smem] * 5 + [vmem] * 5,
        out_specs=vmem,
        scratch_shapes=[
            window, window, window, window, window, window, window, window, window, window,
            pltpu.VMEM((NVAR, LANES, LANES), jnp.float32),
            pltpu.VMEM((2, ROWS, LANES), jnp.float32),
            pltpu.VMEM((3, 8, LANES), jnp.float32),
        ] + [pltpu.VMEM((LANES + 2 * GUARD, LANES), jnp.float32)] * (4 * NVAR),
        compiler_params=pltpu.CompilerParams(vmem_limit_bytes=32 * 1024 * 1024),
        name="march",
    )(
        place, speed_y, speed_z, vigneron, coupling,
        own, along(right_one, 1), along(left_one, -1), along(right_two, 2), along(left_two, -2),
    )
    returned = lax.all_to_all(sent, ("sec", "gy"), 0, 0)
    return pl.pallas_call(
        unpack_kernel,
        out_shape=f32((1, NVAR, PIECE, TILE)),
        in_specs=[smem, vmem],
        out_specs=vmem,
        scratch_shapes=[
            pltpu.VMEM((LANES, LANES), jnp.float32),
            pltpu.VMEM((LANES, LANES), jnp.float32),
        ],
        name="unpack",
    )(place, returned)


def chosen(*args):
    inflow, initial = args[0], args[1]
    fits = (
        lax.axis_size("sec") == 2
        and lax.axis_size("gy") == 4
        and inflow.shape == (NVAR, PIECE, TILE)
        and initial.shape == (1, NVAR, PIECE, TILE)
    )
    return slabs_per_device(*args) if fits else per_device(*args)


def solution(mesh):
    return jax.shard_map(
        chosen,
        mesh=mesh,
        in_specs=(
            P(None, "gy", "gz"),
            P("sec", None, "gy", "gz"),
            P("sec", "gy", "gz"),
            P(),
            P(),
            P(),
            P(),
        ),
        out_specs=P("sec", None, "gy", "gz"),
        check_vma=False,
    )
```

```python
import functools

import jax
import jax.numpy as jnp
from jax import lax
from jax.experimental import pallas as pl
from jax.experimental.pallas import tpu as pltpu
from jax.sharding import PartitionSpec as P

NVAR = 5
ITERS = 4
CORRECTORS = 3
NEWTON = 2

STEP_RATIO = 0.25
WENO_EPS = 1e-06


def passed_along(value, axis, steps):
    count = lax.axis_size(axis)
    initial, last = (max(0, -steps), min(count, count - steps))
    return lax.ppermute(value, axis, [(source, source + steps) for source in range(initial, last)])


def extended(block, sides, width):
    for axis, dim in sides:
        count = lax.axis_size(axis)
        forward = [(i, i + 1) for i in range(count - 1)]
        backward = [(target, source) for source, target in forward]
        low = lax.ppermute(
            lax.slice_in_dim(block, block.shape[dim] - width, None, axis=dim), axis, forward
        )
        high = lax.ppermute(lax.slice_in_dim(block, 0, width, axis=dim), axis, backward)
        block = jnp.concatenate([low, block, high], axis=dim)
    return block


def weno_face(left_far, left_near, center, right_near, right_far):
    smooth_left = (
        13.0 / 12.0 * (left_far - 2.0 * left_near + center) ** 2
        + 0.25 * (left_far - 4.0 * left_near + 3.0 * center) ** 2
    )
    smooth_middle = (
        13.0 / 12.0 * (left_near - 2.0 * center + right_near) ** 2
        + 0.25 * (left_near - right_near) ** 2
    )
    smooth_right = (
        13.0 / 12.0 * (center - 2.0 * right_near + right_far) ** 2
        + 0.25 * (3.0 * center - 4.0 * right_near + right_far) ** 2
    )
    weight_left = 0.1 / (WENO_EPS + smooth_left) ** 2
    weight_middle = 0.6 / (WENO_EPS + smooth_middle) ** 2
    weight_right = 0.3 / (WENO_EPS + smooth_right) ** 2
    guess_left = (2.0 * left_far - 7.0 * left_near + 11.0 * center) / 6.0
    guess_middle = (-left_near + 5.0 * center + 2.0 * right_near) / 6.0
    guess_right = (2.0 * center + 5.0 * right_near - right_far) / 6.0
    total = weight_left * guess_left + weight_middle * guess_middle + weight_right * guess_right
    return total / (weight_left + weight_middle + weight_right)


def sweep(padded, speeds, axis):
    count = padded.shape[axis] - 6
    plus_flux = jnp.maximum(speeds, 0.0)[:, None, None] * padded
    minus_flux = jnp.minimum(speeds, 0.0)[:, None, None] * padded

    def window(source, offset):
        return lax.slice_in_dim(source, offset, offset + count + 1, axis=axis)

    faces = weno_face(*(window(plus_flux, i) for i in (0, 1, 2, 3, 4)))
    faces = faces + weno_face(*(window(minus_flux, i) for i in (5, 4, 3, 2, 1)))
    return lax.slice_in_dim(faces, 1, count + 1, axis=axis) - lax.slice_in_dim(
        faces, 0, count, axis=axis
    )


def crossflow(padded, speed_y, speed_z):
    rows_part = sweep(padded[:, :, 3:-3], speed_y, 1)
    cols_part = sweep(padded[:, 3:-3, :], speed_z, 2)
    return rows_part + cols_part


def streamwise(field, factor):
    return field + factor * field**3 / (1.0 + field**2)


def slope(field, factor):
    return 1.0 + factor * field**2 * (3.0 + field**2) / (1.0 + field**2) ** 2


def correct(padded, current, upstream, diff, blocked, params):
    speed_y, speed_z, vigneron, coupling = params
    factor = vigneron[:, None, None]
    mixed = jnp.einsum("vw,wyz->vyz", coupling, current, precision=lax.Precision.HIGHEST)
    target = (
        streamwise(upstream, factor)
        - STEP_RATIO * crossflow(padded, speed_y, speed_z)
        + STEP_RATIO * mixed
        - (1.0 - factor) * diff
    )
    guess = current
    for newton_index in range(NEWTON):
        guess = guess - (streamwise(guess, factor) - target) / slope(guess, factor)
    return jnp.where(blocked[None], 0.0, guess)


def per_device(inflow, initial, solid, speed_y, speed_z, vigneron, coupling):
    params = (speed_y, speed_z, vigneron, coupling)
    sections = lax.axis_size("sec")
    position = lax.axis_index("sec")
    is_first = position == 0
    start_plane = initial[0]
    guess_above = passed_along(start_plane, "sec", 1)
    guess_above = jnp.where(is_first, inflow, guess_above)
    solid_tile = solid[0] != 0

    def station(upstream, diff):
        current = upstream
        for corrector_index in range(CORRECTORS):
            padded = extended(current, (("gy", 1), ("gz", 2)), 3)
            current = correct(padded, current, upstream, diff, solid_tile, params)
        return current

    def advance(step_index, carry):
        sent, own_prior, upstream_prior = carry
        received = passed_along(sent, "sec", 1)
        received = jnp.where(is_first, inflow, received)
        iterate = step_index - position + 1
        active = (iterate >= 1) & (iterate <= ITERS)
        updated = station(received, own_prior - upstream_prior)
        own_next = jnp.where(active, updated, own_prior)
        upstream_next = jnp.where(active, received, upstream_prior)
        return (own_next, own_next, upstream_next)

    result = lax.fori_loop(
        0, ITERS + sections - 1, advance, (start_plane, start_plane, guess_above)
    )
    return result[1][None]


LANES = 128
SLAB = 32
TILE = 256
MEMBERS = 8
PIECE = 32
GUARD = 16
LEFT = 40
ROWS = GUARD + LEFT + SLAB + LEFT + GUARD
CHUNK_IN = 72
CHUNK_OUT = 40
NEAR = 24
EDGE_ONE = 11 * SLAB + 6 * NEAR
EDGE_TWO = 11 * 8
CHANNELS = 17


def lane_iota():
    return lax.broadcasted_iota(jnp.int32, (8, LANES), 1)


def turned(value, shift):
    shift = shift % LANES
    return value if shift == 0 else pltpu.roll(value, shift, 1)


def slab_of(member, odd):
    sec, gy = member // 4, member % 4
    j = 2 * gy + (sec ^ (gy & 1))
    return jnp.where(odd, MEMBERS - 1 - j, j)


def own_place():
    return lax.axis_index("sec"), lax.axis_index("gy"), lax.axis_index("gz") % 2 == 1


def own_slab():
    sec, gy, odd = own_place()
    return lax.axis_index("gz") * MEMBERS + slab_of(sec * 4 + gy, odd)


def slot(i, gy):
    return (i + gy) % 4


def pack_kernel(inflow, initial, solid, out, stacked, turned_ref, solids):
    sec, gy, odd = own_place()
    for group in range(2):
        for p in range(4):
            rows = pl.ds(pl.multiple_of(slot(p, gy) * PIECE, PIECE), PIECE)
            if group == 0:
                stacked[group, rows, :] = initial[0, p]
            elif p == 0:
                stacked[group, rows, :] = initial[0, 4]
            else:
                stacked[group, rows, :] = inflow[jnp.minimum(3 * sec + p - 1, NVAR - 1)]
    for half in range(2):
        solids[pl.ds(half * PIECE, PIECE), :] = solid[
            0, :, half * LANES:(half + 1) * LANES
        ].astype(jnp.float32)
    solids[pl.ds(2 * PIECE, 2 * PIECE), :] = jnp.zeros((2 * PIECE, LANES), jnp.float32)
    for group in range(2):
        for half in range(2):
            turned_ref[group, pl.ds(half * LANES, LANES), :] = stacked[
                group, :, half * LANES:(half + 1) * LANES
            ].T
    turned_ref[2, pl.ds(0, LANES), :] = solids[...].T
    quarter = lane_iota() // PIECE
    for member in range(MEMBERS):
        j = slab_of(member, odd)
        rows = pl.ds(pl.multiple_of(j * SLAB, SLAB), SLAB)
        for group in range(2):
            out[member, pl.ds(group * SLAB, SLAB), :] = turned_ref[group, rows, :]
        half, within = j // 4, j % 4
        packed = jnp.zeros((8, LANES), jnp.float32)
        for octet in range(4):
            piece = turned_ref[2, pl.ds(pl.multiple_of(within * SLAB + octet * 8, 8), 8), :]
            to = slot(octet, gy)
            piece = pltpu.roll(piece, (PIECE * (to - half)) & (LANES - 1), 1)
            packed = jnp.where(quarter == to, piece, packed)
        out[member, pl.ds(2 * SLAB, 8), :] = packed


def assemble_kernel(got, own, right_one, left_one, right_two, left_two):
    quarter = lane_iota() // PIECE

    def gathered(sec, row, i):
        value = got[sec * 4, pl.ds(row, 8), :]
        for gy in range(1, 4):
            value = jnp.where(quarter == slot(i, gy), got[sec * 4 + gy, pl.ds(row, 8), :], value)
        return turned(value, -PIECE * i)

    def source(channel, octet):
        if channel < 3:
            return gathered(0, SLAB + 8 * octet, channel + 1)
        if channel < 5:
            return gathered(1, SLAB + 8 * octet, channel - 2)
        sec, v = (channel - 5) // 6, (channel - 5) % 6
        if v < 4:
            return gathered(sec, 8 * octet, v)
        if v == 4:
            return gathered(sec, SLAB + 8 * octet, 0)
        return gathered(sec, 2 * SLAB, octet)

    for channel in range(CHANNELS):
        for octet in range(4):
            value = source(channel, octet)
            own[channel, pl.ds(8 * octet, 8), :] = value
            if channel < 11:
                rows = pl.ds(channel * SLAB + 8 * octet, 8)
                right_one[rows, :] = value
                left_one[rows, :] = value
                if octet == 3:
                    right_two[pl.ds(8 * channel, 8), :] = value
                if octet == 0:
                    left_two[pl.ds(8 * channel, 8), :] = value
            else:
                at = 11 * SLAB + (channel - 11) * NEAR
                if octet > 0:
                    right_one[pl.ds(at + 8 * (octet - 1), 8), :] = value
                if octet < 3:
                    left_one[pl.ds(at + 8 * octet, 8), :] = value


def unpack_kernel(got, out, stacked, packed, turned_ref):
    _, gy, odd = own_place()
    quarter = lane_iota() // PIECE

    def member_of(j):
        j = jnp.where(odd, MEMBERS - 1 - j, j)
        row_block = j // 2
        return (j + row_block) % 2 * 4 + row_block

    for half in range(2):
        for within in range(4):
            member = member_of(4 * half + within)
            stacked[half, pl.ds(within * SLAB, SLAB), :] = got[member, pl.ds(0, SLAB), :]
    for within in range(4):
        low = got[member_of(within), pl.ds(SLAB, 8), :]
        high = got[member_of(4 + within), pl.ds(SLAB, 8), :]
        for octet in range(4):
            back = -PIECE * slot(octet, gy)
            packed[pl.ds(within * SLAB + 8 * octet, 8), :] = jnp.where(
                quarter == 0,
                pltpu.roll(low, back & (LANES - 1), 1),
                pltpu.roll(high, (back + PIECE) & (LANES - 1), 1),
            )
    for half in range(2):
        turned_ref[half] = stacked[half].T
    block = packed[...].T
    for half in range(2):
        columns = slice(half * LANES, (half + 1) * LANES)
        for v in range(4):
            rows = pl.ds(pl.multiple_of(slot(v, gy) * PIECE, PIECE), PIECE)
            out[0, v, :, columns] = turned_ref[half, rows, :]
        out[0, 4, :, columns] = block[half * PIECE:(half + 1) * PIECE]


def weighted(d1, d2, d3, d4, t1, t2, t3):
    a = 3.0 * d2 - d1
    b = d2 + d3
    c = 3.0 * d3 - d4
    y1 = pltpu.reciprocal(t1 + a * a, approx=True)
    y2 = pltpu.reciprocal(t2 + b * b, approx=True)
    y3 = pltpu.reciprocal(t3 + c * c, approx=True)
    g1, g2, g3 = (1.0 / 6.0) * (y1 * y1), y2 * y2, 0.5 * (y3 * y3)
    over = g1 * (a + a - d2) + g2 * (b + d3) + g3 * (c + d3)
    under = g1 + g2 + g3
    return over * pltpu.reciprocal(under, approx=True)


def main_kernel(
    last, speed_y, speed_z, vigneron, coupling,
    own, from_left, from_right, from_left_two, from_right_two,
    out,
    inf, still, base, cur, s0, s1, work_inf, delta, curve, face, rows_part, blocked, half_block, *per_block,
):
    across, delta_y, curve_y, face_y = (per_block[NVAR * i:NVAR * (i + 1)] for i in range(4))
    lane = lane_iota()
    center = GUARD + LEFT

    def fill(ref, channel, wide):
        ref[pl.ds(0, GUARD), :] = jnp.zeros((GUARD, LANES), jnp.float32)
        ref[pl.ds(ROWS - GUARD, GUARD), :] = jnp.zeros((GUARD, LANES), jnp.float32)
        ref[pl.ds(center, SLAB), :] = own[channel]
        if wide:
            ref[pl.ds(GUARD, 8), :] = from_left_two[pl.ds(8 * channel, 8), :]
            ref[pl.ds(GUARD + 8, SLAB), :] = from_left[pl.ds(SLAB * channel, SLAB), :]
            ref[pl.ds(center + SLAB, SLAB), :] = from_right[pl.ds(SLAB * channel, SLAB), :]
            ref[pl.ds(center + 2 * SLAB, 8), :] = from_right_two[pl.ds(8 * channel, 8), :]
        else:
            at = 11 * SLAB + (channel - 11) * NEAR
            zeros = jnp.zeros((16, LANES), jnp.float32)
            ref[pl.ds(GUARD, 16), :] = zeros
            ref[pl.ds(center - NEAR, NEAR), :] = from_left[pl.ds(at, NEAR), :]
            ref[pl.ds(center + SLAB, NEAR), :] = from_right[pl.ds(at, NEAR), :]
            ref[pl.ds(center + SLAB + NEAR, 16), :] = zeros

    for v in range(NVAR):
        fill(inf.at[v], v, True)
        fill(s0.at[v], 5 + v, True)
        fill(cur.at[v], 11 + v, False)
    fill(blocked.at[0], 10, True)
    fill(blocked.at[1], 16, False)
    slab = own_slab()
    for octet in range(ROWS // 8):
        rows = pl.ds(8 * octet, 8)
        column = slab * SLAB + 8 * octet - center + lax.broadcasted_iota(jnp.int32, (8, LANES), 0)
        outside = (column < 0) | (column >= last)
        for station in range(2):
            blocked[station, rows, :] = jnp.where(
                outside | (blocked[station, rows, :] != 0.0), 0.0, 1.0
            )
    for v in range(NVAR):
        across[v][pl.ds(0, GUARD), :] = jnp.zeros((GUARD, LANES), jnp.float32)
        across[v][pl.ds(GUARD + LANES, GUARD), :] = jnp.zeros((GUARD, LANES), jnp.float32)

    sy = [speed_y[v] for v in range(NVAR)]
    sz = [speed_z[v] for v in range(NVAR)]
    half_y = [0.5 * jnp.maximum(s, -s) for s in sy]
    half_z = [0.5 * jnp.maximum(s, -s) for s in sz]
    step_y = [jnp.where(s >= 0.0, 1, -1) for s in sy]
    step_z = [jnp.where(s >= 0.0, 1, -1) for s in sz]
    vig = [vigneron[v] for v in range(NVAR)]
    forward = [(s >= 0.0).astype(jnp.int32) for s in sy]
    ahead = sum(forward)
    rank, seen = [], 0
    for v in range(NVAR):
        rank.append(jnp.where(forward[v] == 1, seen, ahead + v - seen))
        seen = seen + forward[v]

    def nth(r):
        return sum(jnp.where(rank[v] == r, v, 0) for v in range(NVAR))

    lone = jnp.where(ahead % 2 == 0, NVAR - 1, 0)
    begin = 1 - jnp.minimum(lone, 1)
    couples = [(nth(begin), nth(begin + 1)), (nth(begin + 2), nth(begin + 3)), (nth(lone), nth(lone))]
    for b, (va, vb) in enumerate(couples):
        both = [speed_y[va], speed_y[vb]]
        both = [0.5 * jnp.maximum(s, -s) for s in both]
        half_block[b] = jnp.where(lane < LANES // 2, both[0], both[1])
    per = [0.5 / vig[v] for v in range(NVAR)]
    stiff = [(1.0 + vig[v]) * per[v] for v in range(NVAR)]
    held = [(1.0 - vig[v]) * per[v] for v in range(NVAR)]
    spread = [(STEP_RATIO / 3.0) * per[v] for v in range(NVAR)]
    mix = [[STEP_RATIO * coupling[v, w] * per[v] for w in range(NVAR)] for v in range(NVAR)]

    def newton(v, guess, target):
        for _ in range(NEWTON):
            r = pltpu.reciprocal(1.0 + guess * guess, approx=True)
            square = r * r
            over = (r - square) * guess + target
            under = (0.5 * r - square) + stiff[v]
            guess = over * pltpu.reciprocal(under, approx=True)
        return guess

    def energy(v, field):
        r = pltpu.reciprocal(1.0 + field * field, approx=True)
        return field * (stiff[v] - 0.5 * r)

    def octet_rows(g):
        return pl.multiple_of(GUARD + 8 * g, 8)

    def pairs(low, high, body):
        def two(i, c):
            for k in range(2):
                body(octet_rows(low + 2 * i + k))
            return c
        lax.fori_loop(0, (high - low) // 2, two, 0)

    def differences(src, half, step, d_ref, t_ref, at):
        here = src[pl.ds(at, 8), :]
        down = src[pl.ds(at + step, 8), :]
        up = src[pl.ds(at - step, 8), :]
        d = down - here
        t = d - (here - up)
        d_ref[pl.ds(at, 8), :] = d * half
        t_ref[pl.ds(at, 8), :] = ((13.0 / 3.0) * (half * half)) * (t * t) + WENO_EPS

    def faces(src, half, step, d_ref, t_ref, f_ref, at):
        d3 = d_ref[pl.ds(at, 8), :]
        d2 = d_ref[pl.ds(at - step, 8), :]
        d1 = d_ref[pl.ds(at - 2 * step, 8), :]
        d4 = d_ref[pl.ds(at + step, 8), :]
        t1 = t_ref[pl.ds(at - step, 8), :]
        t2 = t_ref[pl.ds(at, 8), :]
        t3 = t_ref[pl.ds(at + step, 8), :]
        f_ref[pl.ds(at, 8), :] = (6.0 * half) * src[pl.ds(at, 8), :] + weighted(
            d1, d2, d3, d4, t1, t2, t3
        )

    def fluxes(src, n):
        g0 = 7 - n // 2
        octets = [GUARD + 8 * g for g in range(g0, g0 + n)]
        if n <= 8:
            middle = LANES // 2
            blocks = []
            for b, (va, vb) in enumerate(couples):
                two = [src[v, pl.ds(octets[0] - 8 * (4 - n // 2), middle), :] for v in (va, vb)]
                across[b][pl.ds(GUARD, LANES), :] = jnp.concatenate(two, axis=0).T
                blocks.append((half_block[b], jnp.where(speed_y[va] >= 0.0, 1, -1)))
        else:
            for v in range(NVAR):
                across[v][pl.ds(GUARD, LANES), :] = src[v, pl.ds(GUARD - 8, LANES), :].T
            blocks = list(zip(half_y, step_y))
        for at in [octets[0] - 8] + octets + [octets[-1] + 8]:
            for v in range(NVAR):
                differences(src.at[v], half_z[v], step_z[v], delta.at[v], curve.at[v], at)
        for b, (half, step) in enumerate(blocks):
            row = (across[b], half, step, delta_y[b], curve_y[b])
            for i in range(-1, 17):
                differences(*row, GUARD + 8 * i)
            for i in range(16):
                faces(*row, face_y[b], GUARD + 8 * i)
            faces(*row, face_y[b], GUARD + jnp.where(step > 0, -8, LANES))
            change = (
                face_y[b][pl.ds(GUARD, LANES), :] - face_y[b][pl.ds(GUARD - step, LANES), :]
            ).T
            if n <= 8:
                rows = pl.ds(octets[0] - 8 * (4 - n // 2) - (GUARD - 8), middle)
                rows_part[couples[b][0], rows, :] = change[:middle]
                rows_part[couples[b][1], rows, :] = change[middle:]
            else:
                rows_part[b] = change
        for at in octets:
            for v in range(NVAR):
                faces(src.at[v], half_z[v], step_z[v], delta.at[v], curve.at[v], face.at[v], at)
        return octets

    def sources(src, at):
        field = [src[v, pl.ds(at, 8), :] for v in range(NVAR)]
        result = []
        for v in range(NVAR):
            columns = face[v, pl.ds(at, 8), :] - face[v, pl.ds(at - step_z[v], 8), :]
            rows = rows_part[v, pl.ds(at - (GUARD - 8), 8), :]
            mixed = mix[v][0] * field[0]
            for w in range(1, NVAR):
                mixed = mixed + mix[v][w] * field[w]
            result.append(mixed - spread[v] * (rows + columns))
        return field, result

    def corrector(station, n):
        for at in fluxes(cur, n):
            field, terms = sources(cur, at)
            fluid = blocked[station, pl.ds(at, 8), :] != 0.0
            for v in range(NVAR):
                value = newton(v, field[v], still[v, pl.ds(at, 8), :] + terms[v])
                cur[v, pl.ds(at, 8), :] = jnp.where(fluid, value, 0.0)

    for at in fluxes(inf, 14):
        field, terms = sources(inf, at)
        for v in range(NVAR):
            base[v, pl.ds(at, 8), :] = energy(v, field[v])
            work_inf[v, pl.ds(at, 8), :] = terms[v]

    def first_of_0(at):
        fluid = blocked[0, pl.ds(at, 8), :] != 0.0
        for v in range(NVAR):
            s1[v, pl.ds(at, 8), :] = cur[v, pl.ds(at, 8), :]
            here = inf[v, pl.ds(at, 8), :]
            prior = s0[v, pl.ds(at, 8), :]
            fixed = base[v, pl.ds(at, 8), :] - held[v] * (prior - here)
            still[v, pl.ds(at, 8), :] = fixed
            value = newton(v, here, fixed + work_inf[v, pl.ds(at, 8), :])
            cur[v, pl.ds(at, 8), :] = jnp.where(fluid, value, 0.0)

    def start_of_1(at):
        for v in range(NVAR):
            above = cur[v, pl.ds(at, 8), :]
            prior = s1[v, pl.ds(at, 8), :] - s0[v, pl.ds(at, 8), :]
            still[v, pl.ds(at, 8), :] = energy(v, above) - held[v] * prior
            s0[v, pl.ds(at, 8), :] = above

    def pass_of(t, carry):
        k, c = t // 5, t % 5

        @pl.when(c == 0)
        def _():
            g0 = (6 + 6 * k) // 8
            pairs(g0, 14 - g0, first_of_0)

        @pl.when(c == 2)
        def _():
            g0 = (12 + 6 * k) // 8
            pairs(g0, 14 - g0, start_of_1)

        station = (c >= 2).astype(jnp.int32)
        g0 = (9 + 6 * k + 3 * c) // 8
        for n in (12, 10, 8, 6):
            @pl.when(g0 == 7 - n // 2)
            def _(n=n):
                corrector(station, n)
        return carry

    lax.fori_loop(0, 5 * ITERS, pass_of, 0)

    quarter = lane // PIECE
    for station, result in enumerate((s0, cur)):
        at_last = []
        for octet in range(4):
            rows = pl.ds(center + 8 * octet, 8)
            field = [turned(result[v, rows, :], PIECE * v) for v in range(4)]
            at_last.append(turned(result[4, rows, :], PIECE * octet))
            for gy in range(4):
                value = field[0]
                for v in range(1, 4):
                    value = jnp.where(quarter == slot(v, gy), field[v], value)
                out[station * 4 + gy, pl.ds(8 * octet, 8), :] = value
        for gy in range(4):
            value = at_last[0]
            for octet in range(1, 4):
                value = jnp.where(quarter == slot(octet, gy), at_last[octet], value)
            out[station * 4 + gy, pl.ds(SLAB, 8), :] = value


def slabs_per_device(inflow, initial, solid, speed_y, speed_z, vigneron, coupling):
    mesh_axes = ("sec", "gy", "gz")
    nz_parts = lax.axis_size("gz")
    path = []
    for z in range(nz_parts):
        members = [(s, y) for y in range(4) for s in ((0, 1) if y % 2 == 0 else (1, 0))]
        path += [(s * 4 + y) * nz_parts + z for s, y in (members if z % 2 == 0 else members[::-1])]

    def along(value, steps):
        count = len(path)
        low, high = max(0, -steps), min(count, count - steps)
        return lax.ppermute(value, mesh_axes, [(path[i], path[i + steps]) for i in range(low, high)])

    smem = pl.BlockSpec(memory_space=pltpu.SMEM)
    vmem = pl.BlockSpec(memory_space=pltpu.VMEM)
    f32 = functools.partial(jax.ShapeDtypeStruct, dtype=jnp.float32)

    packed = pl.pallas_call(
        pack_kernel,
        out_shape=pltpu.VMEM((MEMBERS, CHUNK_IN, LANES), jnp.float32),
        in_specs=[vmem, vmem, vmem],
        out_specs=vmem,
        scratch_shapes=[
            pltpu.VMEM((2, LANES, TILE), jnp.float32),
            pltpu.VMEM((3, TILE, LANES), jnp.float32),
            pltpu.VMEM((LANES, LANES), jnp.float32),
        ],
        name="pack",
    )(inflow, initial, solid)
    got = lax.all_to_all(packed, ("sec", "gy"), 0, 0)
    got = pltpu.with_memory_space_constraint(got, pltpu.VMEM)
    own, right_one, left_one, right_two, left_two = pl.pallas_call(
        assemble_kernel,
        out_shape=[
            pltpu.VMEM((CHANNELS, SLAB, LANES), jnp.float32),
            pltpu.VMEM((EDGE_ONE, LANES), jnp.float32),
            pltpu.VMEM((EDGE_ONE, LANES), jnp.float32),
            pltpu.VMEM((EDGE_TWO, LANES), jnp.float32),
            pltpu.VMEM((EDGE_TWO, LANES), jnp.float32),
        ],
        in_specs=[vmem],
        out_specs=[vmem] * 5,
        name="assemble",
    )(got)
    window = pltpu.VMEM((NVAR, ROWS, LANES), jnp.float32)
    sent = pl.pallas_call(
        functools.partial(main_kernel, len(path) * SLAB),
        out_shape=f32((MEMBERS, CHUNK_OUT, LANES)),
        in_specs=[smem] * 4 + [vmem] * 5,
        out_specs=vmem,
        scratch_shapes=[
            window, window, window, window, window, window, window, window, window, window,
            pltpu.VMEM((NVAR, LANES, LANES), jnp.float32),
            pltpu.VMEM((2, ROWS, LANES), jnp.float32),
            pltpu.VMEM((3, 8, LANES), jnp.float32),
        ] + [pltpu.VMEM((LANES + 2 * GUARD, LANES), jnp.float32)] * (4 * NVAR),
        compiler_params=pltpu.CompilerParams(vmem_limit_bytes=32 * 1024 * 1024),
        name="march",
    )(
        speed_y, speed_z, vigneron, coupling,
        own, along(right_one, 1), along(left_one, -1), along(right_two, 2), along(left_two, -2),
    )
    returned = lax.all_to_all(sent, ("sec", "gy"), 0, 0)
    returned = pltpu.with_memory_space_constraint(returned, pltpu.VMEM)
    return pl.pallas_call(
        unpack_kernel,
        out_shape=f32((1, NVAR, PIECE, TILE)),
        in_specs=[vmem],
        out_specs=vmem,
        scratch_shapes=[
            pltpu.VMEM((2, LANES, LANES), jnp.float32),
            pltpu.VMEM((LANES, LANES), jnp.float32),
            pltpu.VMEM((2, LANES, LANES), jnp.float32),
        ],
        name="unpack",
    )(returned)


def chosen(*args):
    inflow, initial = args[0], args[1]
    fits = (
        lax.axis_size("sec") == 2
        and lax.axis_size("gy") == 4
        and inflow.shape == (NVAR, PIECE, TILE)
        and initial.shape == (1, NVAR, PIECE, TILE)
    )
    return slabs_per_device(*args) if fits else per_device(*args)


def solution(mesh):
    return jax.shard_map(
        chosen,
        mesh=mesh,
        in_specs=(
            P(None, "gy", "gz"),
            P("sec", None, "gy", "gz"),
            P("sec", "gy", "gz"),
            P(),
            P(),
            P(),
            P(),
        ),
        out_specs=P("sec", None, "gy", "gz"),
        check_vma=False,
    )
```

```python
import functools

import jax
import jax.numpy as jnp
from jax import lax
from jax.experimental import pallas as pl
from jax.experimental.pallas import tpu as pltpu
from jax.sharding import PartitionSpec as P

NVAR = 5
ITERS = 4
CORRECTORS = 3
NEWTON = 2

STEP_RATIO = 0.25
WENO_EPS = 1e-06


def passed_along(value, axis, steps):
    count = lax.axis_size(axis)
    initial, last = (max(0, -steps), min(count, count - steps))
    return lax.ppermute(value, axis, [(source, source + steps) for source in range(initial, last)])


def extended(block, sides, width):
    for axis, dim in sides:
        count = lax.axis_size(axis)
        forward = [(i, i + 1) for i in range(count - 1)]
        backward = [(target, source) for source, target in forward]
        low = lax.ppermute(
            lax.slice_in_dim(block, block.shape[dim] - width, None, axis=dim), axis, forward
        )
        high = lax.ppermute(lax.slice_in_dim(block, 0, width, axis=dim), axis, backward)
        block = jnp.concatenate([low, block, high], axis=dim)
    return block


def weno_face(left_far, left_near, center, right_near, right_far):
    smooth_left = (
        13.0 / 12.0 * (left_far - 2.0 * left_near + center) ** 2
        + 0.25 * (left_far - 4.0 * left_near + 3.0 * center) ** 2
    )
    smooth_middle = (
        13.0 / 12.0 * (left_near - 2.0 * center + right_near) ** 2
        + 0.25 * (left_near - right_near) ** 2
    )
    smooth_right = (
        13.0 / 12.0 * (center - 2.0 * right_near + right_far) ** 2
        + 0.25 * (3.0 * center - 4.0 * right_near + right_far) ** 2
    )
    weight_left = 0.1 / (WENO_EPS + smooth_left) ** 2
    weight_middle = 0.6 / (WENO_EPS + smooth_middle) ** 2
    weight_right = 0.3 / (WENO_EPS + smooth_right) ** 2
    guess_left = (2.0 * left_far - 7.0 * left_near + 11.0 * center) / 6.0
    guess_middle = (-left_near + 5.0 * center + 2.0 * right_near) / 6.0
    guess_right = (2.0 * center + 5.0 * right_near - right_far) / 6.0
    total = weight_left * guess_left + weight_middle * guess_middle + weight_right * guess_right
    return total / (weight_left + weight_middle + weight_right)


def sweep(padded, speeds, axis):
    count = padded.shape[axis] - 6
    plus_flux = jnp.maximum(speeds, 0.0)[:, None, None] * padded
    minus_flux = jnp.minimum(speeds, 0.0)[:, None, None] * padded

    def window(source, offset):
        return lax.slice_in_dim(source, offset, offset + count + 1, axis=axis)

    faces = weno_face(*(window(plus_flux, i) for i in (0, 1, 2, 3, 4)))
    faces = faces + weno_face(*(window(minus_flux, i) for i in (5, 4, 3, 2, 1)))
    return lax.slice_in_dim(faces, 1, count + 1, axis=axis) - lax.slice_in_dim(
        faces, 0, count, axis=axis
    )


def crossflow(padded, speed_y, speed_z):
    rows_part = sweep(padded[:, :, 3:-3], speed_y, 1)
    cols_part = sweep(padded[:, 3:-3, :], speed_z, 2)
    return rows_part + cols_part


def streamwise(field, factor):
    return field + factor * field**3 / (1.0 + field**2)


def slope(field, factor):
    return 1.0 + factor * field**2 * (3.0 + field**2) / (1.0 + field**2) ** 2


def correct(padded, current, upstream, diff, blocked, params):
    speed_y, speed_z, vigneron, coupling = params
    factor = vigneron[:, None, None]
    mixed = jnp.einsum("vw,wyz->vyz", coupling, current, precision=lax.Precision.HIGHEST)
    target = (
        streamwise(upstream, factor)
        - STEP_RATIO * crossflow(padded, speed_y, speed_z)
        + STEP_RATIO * mixed
        - (1.0 - factor) * diff
    )
    guess = current
    for newton_index in range(NEWTON):
        guess = guess - (streamwise(guess, factor) - target) / slope(guess, factor)
    return jnp.where(blocked[None], 0.0, guess)


def per_device(inflow, initial, solid, speed_y, speed_z, vigneron, coupling):
    params = (speed_y, speed_z, vigneron, coupling)
    sections = lax.axis_size("sec")
    position = lax.axis_index("sec")
    is_first = position == 0
    start_plane = initial[0]
    guess_above = passed_along(start_plane, "sec", 1)
    guess_above = jnp.where(is_first, inflow, guess_above)
    solid_tile = solid[0] != 0

    def station(upstream, diff):
        current = upstream
        for corrector_index in range(CORRECTORS):
            padded = extended(current, (("gy", 1), ("gz", 2)), 3)
            current = correct(padded, current, upstream, diff, solid_tile, params)
        return current

    def advance(step_index, carry):
        sent, own_prior, upstream_prior = carry
        received = passed_along(sent, "sec", 1)
        received = jnp.where(is_first, inflow, received)
        iterate = step_index - position + 1
        active = (iterate >= 1) & (iterate <= ITERS)
        updated = station(received, own_prior - upstream_prior)
        own_next = jnp.where(active, updated, own_prior)
        upstream_next = jnp.where(active, received, upstream_prior)
        return (own_next, own_next, upstream_next)

    result = lax.fori_loop(
        0, ITERS + sections - 1, advance, (start_plane, start_plane, guess_above)
    )
    return result[1][None]


LANES = 128
SLAB = 32
TILE = 256
MEMBERS = 8
PIECE = 32
GUARD = 16
LEFT = 40
ROWS = GUARD + LEFT + SLAB + LEFT + GUARD
CHUNK_IN = 72
CHUNK_OUT = 40
NEAR = 24
EDGE_ONE = 11 * SLAB + 6 * NEAR
FAR = 4
EDGE_TWO = 32
CHANNELS = 17


def lane_iota():
    return lax.broadcasted_iota(jnp.int32, (8, LANES), 1)


def turned(value, shift):
    shift = shift % LANES
    return value if shift == 0 else pltpu.roll(value, shift, 1)


def slab_of(member, odd):
    sec, gy = member // 4, member % 4
    j = 2 * gy + (sec ^ (gy & 1))
    return jnp.where(odd, MEMBERS - 1 - j, j)


def own_place():
    return lax.axis_index("sec"), lax.axis_index("gy"), lax.axis_index("gz") % 2 == 1


def own_slab():
    sec, gy, odd = own_place()
    return lax.axis_index("gz") * MEMBERS + slab_of(sec * 4 + gy, odd)


def slot(i, gy):
    return (i + gy) % 4


def pack_kernel(inflow, initial, solid, out, stacked, turned_ref, solids):
    sec, gy, odd = own_place()
    for group in range(2):
        for p in range(4):
            rows = pl.ds(pl.multiple_of(slot(p, gy) * PIECE, PIECE), PIECE)
            if group == 0:
                stacked[group, rows, :] = initial[0, p]
            elif p == 0:
                stacked[group, rows, :] = initial[0, 4]
            else:
                stacked[group, rows, :] = inflow[jnp.minimum(3 * sec + p - 1, NVAR - 1)]
    for half in range(2):
        solids[pl.ds(half * PIECE, PIECE), :] = solid[
            0, :, half * LANES:(half + 1) * LANES
        ].astype(jnp.float32)
    solids[pl.ds(2 * PIECE, 2 * PIECE), :] = jnp.zeros((2 * PIECE, LANES), jnp.float32)
    for group in range(2):
        for half in range(2):
            turned_ref[group, pl.ds(half * LANES, LANES), :] = stacked[
                group, :, half * LANES:(half + 1) * LANES
            ].T
    turned_ref[2, pl.ds(0, LANES), :] = solids[...].T
    quarter = lane_iota() // PIECE
    for member in range(MEMBERS):
        j = slab_of(member, odd)
        rows = pl.ds(pl.multiple_of(j * SLAB, SLAB), SLAB)
        for group in range(2):
            out[member, pl.ds(group * SLAB, SLAB), :] = turned_ref[group, rows, :]
        half, within = j // 4, j % 4
        packed = jnp.zeros((8, LANES), jnp.float32)
        for octet in range(4):
            piece = turned_ref[2, pl.ds(pl.multiple_of(within * SLAB + octet * 8, 8), 8), :]
            to = slot(octet, gy)
            piece = pltpu.roll(piece, (PIECE * (to - half)) & (LANES - 1), 1)
            packed = jnp.where(quarter == to, piece, packed)
        out[member, pl.ds(2 * SLAB, 8), :] = packed


def far_rows(channel):
    return (FAR * channel, FAR) if channel < NVAR else (FAR * NVAR + channel - NVAR, 1)


def assemble_kernel(got, own, right_one, left_one, right_two, left_two):
    quarter = lane_iota() // PIECE

    def gathered(sec, row, i):
        value = got[sec * 4, pl.ds(row, 8), :]
        for gy in range(1, 4):
            value = jnp.where(quarter == slot(i, gy), got[sec * 4 + gy, pl.ds(row, 8), :], value)
        return turned(value, -PIECE * i)

    def source(channel, octet):
        if channel < 3:
            return gathered(0, SLAB + 8 * octet, channel + 1)
        if channel < 5:
            return gathered(1, SLAB + 8 * octet, channel - 2)
        sec, v = (channel - 5) // 6, (channel - 5) % 6
        if v < 4:
            return gathered(sec, 8 * octet, v)
        if v == 4:
            return gathered(sec, SLAB + 8 * octet, 0)
        return gathered(sec, 2 * SLAB, octet)

    for ref in (right_two, left_two):
        ref[...] = jnp.zeros((EDGE_TWO, LANES), jnp.float32)
    for channel in range(CHANNELS):
        for octet in range(4):
            value = source(channel, octet)
            own[channel, pl.ds(8 * octet, 8), :] = value
            if channel < 11:
                rows = pl.ds(channel * SLAB + 8 * octet, 8)
                right_one[rows, :] = value
                left_one[rows, :] = value
                at, width = far_rows(channel)
                if octet == 3:
                    right_two[pl.ds(at, width), :] = value[8 - width:]
                if octet == 0:
                    left_two[pl.ds(at, width), :] = value[:width]
            else:
                at = 11 * SLAB + (channel - 11) * NEAR
                if octet > 0:
                    right_one[pl.ds(at + 8 * (octet - 1), 8), :] = value
                if octet < 3:
                    left_one[pl.ds(at + 8 * octet, 8), :] = value


def unpack_kernel(got, out, stacked, packed, turned_ref):
    _, gy, odd = own_place()
    quarter = lane_iota() // PIECE

    def member_of(j):
        j = jnp.where(odd, MEMBERS - 1 - j, j)
        row_block = j // 2
        return (j + row_block) % 2 * 4 + row_block

    for half in range(2):
        for within in range(4):
            member = member_of(4 * half + within)
            stacked[half, pl.ds(within * SLAB, SLAB), :] = got[member, pl.ds(0, SLAB), :]
    for within in range(4):
        low = got[member_of(within), pl.ds(SLAB, 8), :]
        high = got[member_of(4 + within), pl.ds(SLAB, 8), :]
        for octet in range(4):
            back = -PIECE * slot(octet, gy)
            packed[pl.ds(within * SLAB + 8 * octet, 8), :] = jnp.where(
                quarter == 0,
                pltpu.roll(low, back & (LANES - 1), 1),
                pltpu.roll(high, (back + PIECE) & (LANES - 1), 1),
            )
    for half in range(2):
        turned_ref[half] = stacked[half].T
    block = packed[...].T
    for half in range(2):
        columns = slice(half * LANES, (half + 1) * LANES)
        for v in range(4):
            rows = pl.ds(pl.multiple_of(slot(v, gy) * PIECE, PIECE), PIECE)
            out[0, v, :, columns] = turned_ref[half, rows, :]
        out[0, 4, :, columns] = block[half * PIECE:(half + 1) * PIECE]


def weighted(d1, d2, d3, d4, t1, t2, t3):
    a = 3.0 * d2 - d1
    b = d2 + d3
    c = 3.0 * d3 - d4
    y1 = pltpu.reciprocal(t1 + a * a, approx=True)
    y2 = pltpu.reciprocal(t2 + b * b, approx=True)
    y3 = pltpu.reciprocal(t3 + c * c, approx=True)
    g1, g2, g3 = (1.0 / 6.0) * (y1 * y1), y2 * y2, 0.5 * (y3 * y3)
    over = g1 * (a + a - d2) + g2 * (b + d3) + g3 * (c + d3)
    under = g1 + g2 + g3
    return over * pltpu.reciprocal(under, approx=True)


def main_kernel(
    last, speed_y, speed_z, vigneron, coupling,
    own, from_left, from_right, from_left_two, from_right_two,
    out,
    inf, still, base, cur, s0, s1, work_inf, delta, curve, face, rows_part, blocked, half_block, *per_block,
):
    across, delta_y, curve_y, face_y = (per_block[NVAR * i:NVAR * (i + 1)] for i in range(4))
    lane = lane_iota()
    center = GUARD + LEFT

    def fill(ref, channel, wide):
        ref[pl.ds(0, GUARD), :] = jnp.zeros((GUARD, LANES), jnp.float32)
        ref[pl.ds(ROWS - GUARD, GUARD), :] = jnp.zeros((GUARD, LANES), jnp.float32)
        ref[pl.ds(center, SLAB), :] = own[channel]
        if wide:
            zeros = jnp.zeros((8, LANES), jnp.float32)
            far, width = far_rows(channel)
            ref[pl.ds(GUARD, 8), :] = zeros
            ref[pl.ds(GUARD + 8 - width, width), :] = from_left_two[pl.ds(far, width), :]
            ref[pl.ds(GUARD + 8, SLAB), :] = from_left[pl.ds(SLAB * channel, SLAB), :]
            ref[pl.ds(center + SLAB, SLAB), :] = from_right[pl.ds(SLAB * channel, SLAB), :]
            ref[pl.ds(center + 2 * SLAB, 8), :] = zeros
            ref[pl.ds(center + 2 * SLAB, width), :] = from_right_two[pl.ds(far, width), :]
        else:
            at = 11 * SLAB + (channel - 11) * NEAR
            zeros = jnp.zeros((16, LANES), jnp.float32)
            ref[pl.ds(GUARD, 16), :] = zeros
            ref[pl.ds(center - NEAR, NEAR), :] = from_left[pl.ds(at, NEAR), :]
            ref[pl.ds(center + SLAB, NEAR), :] = from_right[pl.ds(at, NEAR), :]
            ref[pl.ds(center + SLAB + NEAR, 16), :] = zeros

    for v in range(NVAR):
        fill(inf.at[v], v, True)
        fill(s0.at[v], 5 + v, True)
        fill(cur.at[v], 11 + v, False)
    fill(blocked.at[0], 10, True)
    fill(blocked.at[1], 16, False)
    slab = own_slab()
    for octet in range(ROWS // 8):
        rows = pl.ds(8 * octet, 8)
        column = slab * SLAB + 8 * octet - center + lax.broadcasted_iota(jnp.int32, (8, LANES), 0)
        outside = (column < 0) | (column >= last)
        for station in range(2):
            blocked[station, rows, :] = jnp.where(
                outside | (blocked[station, rows, :] != 0.0), 0.0, 1.0
            )
    for v in range(NVAR):
        across[v][pl.ds(0, GUARD), :] = jnp.zeros((GUARD, LANES), jnp.float32)
        across[v][pl.ds(GUARD + LANES, GUARD), :] = jnp.zeros((GUARD, LANES), jnp.float32)

    sy = [speed_y[v] for v in range(NVAR)]
    sz = [speed_z[v] for v in range(NVAR)]
    half_y = [0.5 * jnp.maximum(s, -s) for s in sy]
    half_z = [0.5 * jnp.maximum(s, -s) for s in sz]
    step_y = [jnp.where(s >= 0.0, 1, -1) for s in sy]
    step_z = [jnp.where(s >= 0.0, 1, -1) for s in sz]
    vig = [vigneron[v] for v in range(NVAR)]
    forward = [(s >= 0.0).astype(jnp.int32) for s in sy]
    ahead = sum(forward)
    rank, seen = [], 0
    for v in range(NVAR):
        rank.append(jnp.where(forward[v] == 1, seen, ahead + v - seen))
        seen = seen + forward[v]

    def nth(r):
        return sum(jnp.where(rank[v] == r, v, 0) for v in range(NVAR))

    lone = jnp.where(ahead % 2 == 0, NVAR - 1, 0)
    begin = 1 - jnp.minimum(lone, 1)
    couples = [(nth(begin), nth(begin + 1)), (nth(begin + 2), nth(begin + 3)), (nth(lone), nth(lone))]
    for b, (va, vb) in enumerate(couples):
        both = [speed_y[va], speed_y[vb]]
        both = [0.5 * jnp.maximum(s, -s) for s in both]
        half_block[b] = jnp.where(lane < LANES // 2, both[0], both[1])
    per = [0.5 / vig[v] for v in range(NVAR)]
    stiff = [(1.0 + vig[v]) * per[v] for v in range(NVAR)]
    held = [(1.0 - vig[v]) * per[v] for v in range(NVAR)]
    spread = [(STEP_RATIO / 3.0) * per[v] for v in range(NVAR)]
    mix = [[STEP_RATIO * coupling[v, w] * per[v] for w in range(NVAR)] for v in range(NVAR)]

    def newton(v, guess, target):
        for _ in range(NEWTON):
            r = pltpu.reciprocal(1.0 + guess * guess, approx=True)
            square = r * r
            over = (r - square) * guess + target
            under = (0.5 * r - square) + stiff[v]
            guess = over * pltpu.reciprocal(under, approx=True)
        return guess

    def energy(v, field):
        r = pltpu.reciprocal(1.0 + field * field, approx=True)
        return field * (stiff[v] - 0.5 * r)

    def octet_rows(g):
        return pl.multiple_of(GUARD + 8 * g, 8)

    def pairs(low, high, body):
        def two(i, c):
            for k in range(2):
                body(octet_rows(low + 2 * i + k))
            return c
        lax.fori_loop(0, (high - low) // 2, two, 0)

    def differences(src, half, step, d_ref, t_ref, at):
        here = src[pl.ds(at, 8), :]
        down = src[pl.ds(at + step, 8), :]
        up = src[pl.ds(at - step, 8), :]
        d = down - here
        t = d - (here - up)
        d_ref[pl.ds(at, 8), :] = d * half
        t_ref[pl.ds(at, 8), :] = ((13.0 / 3.0) * (half * half)) * (t * t) + WENO_EPS

    def faces(src, half, step, d_ref, t_ref, f_ref, at):
        d3 = d_ref[pl.ds(at, 8), :]
        d2 = d_ref[pl.ds(at - step, 8), :]
        d1 = d_ref[pl.ds(at - 2 * step, 8), :]
        d4 = d_ref[pl.ds(at + step, 8), :]
        t1 = t_ref[pl.ds(at - step, 8), :]
        t2 = t_ref[pl.ds(at, 8), :]
        t3 = t_ref[pl.ds(at + step, 8), :]
        f_ref[pl.ds(at, 8), :] = (6.0 * half) * src[pl.ds(at, 8), :] + weighted(
            d1, d2, d3, d4, t1, t2, t3
        )

    def octets_of(n):
        g0 = 7 - n // 2
        return [GUARD + 8 * g for g in range(g0, g0 + n)]

    def blocks_of(n):
        if n > 8:
            return list(zip(half_y, step_y))
        return [
            (half_block[b], jnp.where(speed_y[va] >= 0.0, 1, -1))
            for b, (va, _) in enumerate(couples)
        ]

    middle = LANES // 2
    narrow = pl.ds(GUARD + 24, middle)

    def turn_in(src, n):
        if n > 8:
            for v in range(NVAR):
                across[v][pl.ds(GUARD, LANES), :] = src[v, pl.ds(GUARD - 8, LANES), :].T
        else:
            for b, couple in enumerate(couples):
                two = [src[v, narrow, :] for v in couple]
                across[b][pl.ds(GUARD, LANES), :] = jnp.concatenate(two, axis=0).T

    def column_differences(src, n):
        octets = octets_of(n)
        for at in [octets[0] - 8] + octets + [octets[-1] + 8]:
            for v in range(NVAR):
                differences(src.at[v], half_z[v], step_z[v], delta.at[v], curve.at[v], at)

    def column_faces(src, octets):
        for at in octets:
            for v in range(NVAR):
                faces(src.at[v], half_z[v], step_z[v], delta.at[v], curve.at[v], face.at[v], at)

    def row_faces(n):
        for b, (half, step) in enumerate(blocks_of(n)):
            row = (across[b], half, step, delta_y[b], curve_y[b])
            for i in range(-1, 17):
                differences(*row, GUARD + 8 * i)
            for i in range(16):
                faces(*row, face_y[b], GUARD + 8 * i)
            faces(*row, face_y[b], GUARD + jnp.where(step > 0, -8, LANES))

    def turn_out(n):
        for b, (_, step) in enumerate(blocks_of(n)):
            change = (
                face_y[b][pl.ds(GUARD, LANES), :] - face_y[b][pl.ds(GUARD - step, LANES), :]
            ).T
            if n > 8:
                rows_part[b] = change
            else:
                rows = pl.ds(8 + 24, middle)
                rows_part[couples[b][0], rows, :] = change[:middle]
                rows_part[couples[b][1], rows, :] = change[middle:]

    def sources(src, at):
        field = [src[v, pl.ds(at, 8), :] for v in range(NVAR)]
        result = []
        for v in range(NVAR):
            columns = face[v, pl.ds(at, 8), :] - face[v, pl.ds(at - step_z[v], 8), :]
            rows = rows_part[v, pl.ds(at - (GUARD - 8), 8), :]
            mixed = mix[v][0] * field[0]
            for w in range(1, NVAR):
                mixed = mixed + mix[v][w] * field[w]
            result.append(mixed - spread[v] * (rows + columns))
        return field, result

    def steps(station, octets):
        for at in octets:
            field, terms = sources(cur, at)
            fluid = blocked[station, pl.ds(at, 8), :] != 0.0
            for v in range(NVAR):
                value = newton(v, field[v], still[v, pl.ds(at, 8), :] + terms[v])
                cur[v, pl.ds(at, 8), :] = jnp.where(fluid, value, 0.0)

    turn_in(inf, 14)
    column_differences(inf, 14)
    row_faces(14)
    turn_out(14)
    column_faces(inf, octets_of(14))
    for at in octets_of(14):
        field, terms = sources(inf, at)
        for v in range(NVAR):
            base[v, pl.ds(at, 8), :] = energy(v, field[v])
            work_inf[v, pl.ds(at, 8), :] = terms[v]

    def first_of_0(at):
        fluid = blocked[0, pl.ds(at, 8), :] != 0.0
        for v in range(NVAR):
            s1[v, pl.ds(at, 8), :] = cur[v, pl.ds(at, 8), :]
            here = inf[v, pl.ds(at, 8), :]
            prior = s0[v, pl.ds(at, 8), :]
            fixed = base[v, pl.ds(at, 8), :] - held[v] * (prior - here)
            still[v, pl.ds(at, 8), :] = fixed
            value = newton(v, here, fixed + work_inf[v, pl.ds(at, 8), :])
            cur[v, pl.ds(at, 8), :] = jnp.where(fluid, value, 0.0)

    def start_of_1(at):
        for v in range(NVAR):
            above = cur[v, pl.ds(at, 8), :]
            prior = s1[v, pl.ds(at, 8), :] - s0[v, pl.ds(at, 8), :]
            still[v, pl.ds(at, 8), :] = energy(v, above) - held[v] * prior
            s0[v, pl.ds(at, 8), :] = above

    def pass_of(t, carry):
        k, c = t // 5, t % 5

        @pl.when(c == 0)
        def _():
            g0 = (6 + 6 * k) // 8
            pairs(g0, 14 - g0, first_of_0)

        @pl.when(c == 2)
        def _():
            g0 = (12 + 6 * k) // 8
            pairs(g0, 14 - g0, start_of_1)

        station = (c >= 2).astype(jnp.int32)
        g0 = (9 + 6 * k + 3 * c) // 8
        for n in (12, 10, 8, 6):
            times = (g0 == 7 - n // 2).astype(jnp.int32)

            def part(i, c, n=n):
                turn_in(cur, n)
                column_differences(cur, n)
                column_faces(cur, octets_of(n)[:n // 2])
                return c
            lax.fori_loop(0, times, part, 0)

            def part(i, c, n=n):
                row_faces(n)
                return c
            lax.fori_loop(0, times, part, 0)

            def part(i, c, n=n):
                turn_out(n)
                column_faces(cur, octets_of(n)[n // 2:])
                steps(station, octets_of(n))
                return c
            lax.fori_loop(0, times, part, 0)
        return carry

    lax.fori_loop(0, 5 * ITERS, pass_of, 0)

    quarter = lane // PIECE
    for station, result in enumerate((s0, cur)):
        at_last = []
        for octet in range(4):
            rows = pl.ds(center + 8 * octet, 8)
            field = [turned(result[v, rows, :], PIECE * v) for v in range(4)]
            at_last.append(turned(result[4, rows, :], PIECE * octet))
            for gy in range(4):
                value = field[0]
                for v in range(1, 4):
                    value = jnp.where(quarter == slot(v, gy), field[v], value)
                out[station * 4 + gy, pl.ds(8 * octet, 8), :] = value
        for gy in range(4):
            value = at_last[0]
            for octet in range(1, 4):
                value = jnp.where(quarter == slot(octet, gy), at_last[octet], value)
            out[station * 4 + gy, pl.ds(SLAB, 8), :] = value


def slabs_per_device(inflow, initial, solid, speed_y, speed_z, vigneron, coupling):
    mesh_axes = ("sec", "gy", "gz")
    nz_parts = lax.axis_size("gz")
    path = []
    for z in range(nz_parts):
        members = [(s, y) for y in range(4) for s in ((0, 1) if y % 2 == 0 else (1, 0))]
        path += [(s * 4 + y) * nz_parts + z for s, y in (members if z % 2 == 0 else members[::-1])]

    def along(value, steps):
        count = len(path)
        low, high = max(0, -steps), min(count, count - steps)
        return lax.ppermute(value, mesh_axes, [(path[i], path[i + steps]) for i in range(low, high)])

    smem = pl.BlockSpec(memory_space=pltpu.SMEM)
    vmem = pl.BlockSpec(memory_space=pltpu.VMEM)
    f32 = functools.partial(jax.ShapeDtypeStruct, dtype=jnp.float32)

    packed = pl.pallas_call(
        pack_kernel,
        out_shape=pltpu.VMEM((MEMBERS, CHUNK_IN, LANES), jnp.float32),
        in_specs=[vmem, vmem, vmem],
        out_specs=vmem,
        scratch_shapes=[
            pltpu.VMEM((2, LANES, TILE), jnp.float32),
            pltpu.VMEM((3, TILE, LANES), jnp.float32),
            pltpu.VMEM((LANES, LANES), jnp.float32),
        ],
        name="pack",
    )(inflow, initial, solid)
    got = lax.all_to_all(packed, ("sec", "gy"), 0, 0)
    got = pltpu.with_memory_space_constraint(got, pltpu.VMEM)
    own, right_one, left_one, right_two, left_two = pl.pallas_call(
        assemble_kernel,
        out_shape=[
            pltpu.VMEM((CHANNELS, SLAB, LANES), jnp.float32),
            pltpu.VMEM((EDGE_ONE, LANES), jnp.float32),
            pltpu.VMEM((EDGE_ONE, LANES), jnp.float32),
            pltpu.VMEM((EDGE_TWO, LANES), jnp.float32),
            pltpu.VMEM((EDGE_TWO, LANES), jnp.float32),
        ],
        in_specs=[vmem],
        out_specs=[vmem] * 5,
        name="assemble",
    )(got)
    window = pltpu.VMEM((NVAR, ROWS, LANES), jnp.float32)
    sent = pl.pallas_call(
        functools.partial(main_kernel, len(path) * SLAB),
        out_shape=f32((MEMBERS, CHUNK_OUT, LANES)),
        in_specs=[smem] * 4 + [vmem] * 5,
        out_specs=vmem,
        scratch_shapes=[
            window, window, window, window, window, window, window, window, window, window,
            pltpu.VMEM((NVAR, LANES, LANES), jnp.float32),
            pltpu.VMEM((2, ROWS, LANES), jnp.float32),
            pltpu.VMEM((3, 8, LANES), jnp.float32),
        ] + [pltpu.VMEM((LANES + 2 * GUARD, LANES), jnp.float32)] * (4 * NVAR),
        compiler_params=pltpu.CompilerParams(vmem_limit_bytes=32 * 1024 * 1024),
        name="march",
    )(
        speed_y, speed_z, vigneron, coupling,
        own, along(right_one, 1), along(left_one, -1), along(right_two, 2), along(left_two, -2),
    )
    returned = lax.all_to_all(sent, ("sec", "gy"), 0, 0)
    returned = pltpu.with_memory_space_constraint(returned, pltpu.VMEM)
    return pl.pallas_call(
        unpack_kernel,
        out_shape=f32((1, NVAR, PIECE, TILE)),
        in_specs=[vmem],
        out_specs=vmem,
        scratch_shapes=[
            pltpu.VMEM((2, LANES, LANES), jnp.float32),
            pltpu.VMEM((LANES, LANES), jnp.float32),
            pltpu.VMEM((2, LANES, LANES), jnp.float32),
        ],
        name="unpack",
    )(returned)


def chosen(*args):
    inflow, initial = args[0], args[1]
    fits = (
        lax.axis_size("sec") == 2
        and lax.axis_size("gy") == 4
        and inflow.shape == (NVAR, PIECE, TILE)
        and initial.shape == (1, NVAR, PIECE, TILE)
    )
    return slabs_per_device(*args) if fits else per_device(*args)


def solution(mesh):
    return jax.shard_map(
        chosen,
        mesh=mesh,
        in_specs=(
            P(None, "gy", "gz"),
            P("sec", None, "gy", "gz"),
            P("sec", "gy", "gz"),
            P(),
            P(),
            P(),
            P(),
        ),
        out_specs=P("sec", None, "gy", "gz"),
        check_vma=False,
    )
```

```python
import functools

import jax
import jax.numpy as jnp
from jax import lax
from jax.experimental import pallas as pl
from jax.experimental.pallas import tpu as pltpu
from jax.sharding import PartitionSpec as P

NVAR = 5
ITERS = 4
CORRECTORS = 3
NEWTON = 2

STEP_RATIO = 0.25
WENO_EPS = 1e-06


def passed_along(value, axis, steps):
    count = lax.axis_size(axis)
    initial, last = (max(0, -steps), min(count, count - steps))
    return lax.ppermute(value, axis, [(source, source + steps) for source in range(initial, last)])


def extended(block, sides, width):
    for axis, dim in sides:
        count = lax.axis_size(axis)
        forward = [(i, i + 1) for i in range(count - 1)]
        backward = [(target, source) for source, target in forward]
        low = lax.ppermute(
            lax.slice_in_dim(block, block.shape[dim] - width, None, axis=dim), axis, forward
        )
        high = lax.ppermute(lax.slice_in_dim(block, 0, width, axis=dim), axis, backward)
        block = jnp.concatenate([low, block, high], axis=dim)
    return block


def weno_face(left_far, left_near, center, right_near, right_far):
    smooth_left = (
        13.0 / 12.0 * (left_far - 2.0 * left_near + center) ** 2
        + 0.25 * (left_far - 4.0 * left_near + 3.0 * center) ** 2
    )
    smooth_middle = (
        13.0 / 12.0 * (left_near - 2.0 * center + right_near) ** 2
        + 0.25 * (left_near - right_near) ** 2
    )
    smooth_right = (
        13.0 / 12.0 * (center - 2.0 * right_near + right_far) ** 2
        + 0.25 * (3.0 * center - 4.0 * right_near + right_far) ** 2
    )
    weight_left = 0.1 / (WENO_EPS + smooth_left) ** 2
    weight_middle = 0.6 / (WENO_EPS + smooth_middle) ** 2
    weight_right = 0.3 / (WENO_EPS + smooth_right) ** 2
    guess_left = (2.0 * left_far - 7.0 * left_near + 11.0 * center) / 6.0
    guess_middle = (-left_near + 5.0 * center + 2.0 * right_near) / 6.0
    guess_right = (2.0 * center + 5.0 * right_near - right_far) / 6.0
    total = weight_left * guess_left + weight_middle * guess_middle + weight_right * guess_right
    return total / (weight_left + weight_middle + weight_right)


def sweep(padded, speeds, axis):
    count = padded.shape[axis] - 6
    plus_flux = jnp.maximum(speeds, 0.0)[:, None, None] * padded
    minus_flux = jnp.minimum(speeds, 0.0)[:, None, None] * padded

    def window(source, offset):
        return lax.slice_in_dim(source, offset, offset + count + 1, axis=axis)

    faces = weno_face(*(window(plus_flux, i) for i in (0, 1, 2, 3, 4)))
    faces = faces + weno_face(*(window(minus_flux, i) for i in (5, 4, 3, 2, 1)))
    return lax.slice_in_dim(faces, 1, count + 1, axis=axis) - lax.slice_in_dim(
        faces, 0, count, axis=axis
    )


def crossflow(padded, speed_y, speed_z):
    rows_part = sweep(padded[:, :, 3:-3], speed_y, 1)
    cols_part = sweep(padded[:, 3:-3, :], speed_z, 2)
    return rows_part + cols_part


def streamwise(field, factor):
    return field + factor * field**3 / (1.0 + field**2)


def slope(field, factor):
    return 1.0 + factor * field**2 * (3.0 + field**2) / (1.0 + field**2) ** 2


def correct(padded, current, upstream, diff, blocked, params):
    speed_y, speed_z, vigneron, coupling = params
    factor = vigneron[:, None, None]
    mixed = jnp.einsum("vw,wyz->vyz", coupling, current, precision=lax.Precision.HIGHEST)
    target = (
        streamwise(upstream, factor)
        - STEP_RATIO * crossflow(padded, speed_y, speed_z)
        + STEP_RATIO * mixed
        - (1.0 - factor) * diff
    )
    guess = current
    for newton_index in range(NEWTON):
        guess = guess - (streamwise(guess, factor) - target) / slope(guess, factor)
    return jnp.where(blocked[None], 0.0, guess)


def per_device(inflow, initial, solid, speed_y, speed_z, vigneron, coupling):
    params = (speed_y, speed_z, vigneron, coupling)
    sections = lax.axis_size("sec")
    position = lax.axis_index("sec")
    is_first = position == 0
    start_plane = initial[0]
    guess_above = passed_along(start_plane, "sec", 1)
    guess_above = jnp.where(is_first, inflow, guess_above)
    solid_tile = solid[0] != 0

    def station(upstream, diff):
        current = upstream
        for corrector_index in range(CORRECTORS):
            padded = extended(current, (("gy", 1), ("gz", 2)), 3)
            current = correct(padded, current, upstream, diff, solid_tile, params)
        return current

    def advance(step_index, carry):
        sent, own_prior, upstream_prior = carry
        received = passed_along(sent, "sec", 1)
        received = jnp.where(is_first, inflow, received)
        iterate = step_index - position + 1
        active = (iterate >= 1) & (iterate <= ITERS)
        updated = station(received, own_prior - upstream_prior)
        own_next = jnp.where(active, updated, own_prior)
        upstream_next = jnp.where(active, received, upstream_prior)
        return (own_next, own_next, upstream_next)

    result = lax.fori_loop(
        0, ITERS + sections - 1, advance, (start_plane, start_plane, guess_above)
    )
    return result[1][None]


LANES = 128
SLAB = 32
TILE = 256
MEMBERS = 8
PIECE = 32
GUARD = 16
STRIP = 80
LEFT = 40
ROWS = GUARD + LEFT + SLAB + LEFT + GUARD
CHUNK_IN = 72
CHUNK_OUT = 40
NEAR = 24
EDGE_ONE = 11 * SLAB + 6 * NEAR
FAR = 4
EDGE_TWO = 32
CHANNELS = 17


def lane_iota():
    return lax.broadcasted_iota(jnp.int32, (8, LANES), 1)


def turned(value, shift):
    shift = shift % LANES
    return value if shift == 0 else pltpu.roll(value, shift, 1)


def slab_of(member, odd):
    sec, gy = member // 4, member % 4
    j = 2 * gy + (sec ^ (gy & 1))
    return jnp.where(odd, MEMBERS - 1 - j, j)


def own_place():
    return lax.axis_index("sec"), lax.axis_index("gy"), lax.axis_index("gz") % 2 == 1


def own_slab():
    sec, gy, odd = own_place()
    return lax.axis_index("gz") * MEMBERS + slab_of(sec * 4 + gy, odd)


def slot(i, gy):
    return (i + gy) % 4


def pack_kernel(inflow, initial, solid, out, stacked, turned_ref, solids):
    sec, gy, odd = own_place()
    for group in range(2):
        for p in range(4):
            rows = pl.ds(pl.multiple_of(slot(p, gy) * PIECE, PIECE), PIECE)
            if group == 0:
                stacked[group, rows, :] = initial[0, p]
            elif p == 0:
                stacked[group, rows, :] = initial[0, 4]
            else:
                stacked[group, rows, :] = inflow[jnp.minimum(3 * sec + p - 1, NVAR - 1)]
    for half in range(2):
        solids[pl.ds(half * PIECE, PIECE), :] = solid[
            0, :, half * LANES:(half + 1) * LANES
        ].astype(jnp.float32)
    solids[pl.ds(2 * PIECE, 2 * PIECE), :] = jnp.zeros((2 * PIECE, LANES), jnp.float32)
    for group in range(2):
        for half in range(2):
            turned_ref[group, pl.ds(half * LANES, LANES), :] = stacked[
                group, :, half * LANES:(half + 1) * LANES
            ].T
    turned_ref[2, pl.ds(0, LANES), :] = solids[...].T
    quarter = lane_iota() // PIECE
    for member in range(MEMBERS):
        j = slab_of(member, odd)
        rows = pl.ds(pl.multiple_of(j * SLAB, SLAB), SLAB)
        for group in range(2):
            out[member, pl.ds(group * SLAB, SLAB), :] = turned_ref[group, rows, :]
        half, within = j // 4, j % 4
        packed = jnp.zeros((8, LANES), jnp.float32)
        for octet in range(4):
            piece = turned_ref[2, pl.ds(pl.multiple_of(within * SLAB + octet * 8, 8), 8), :]
            to = slot(octet, gy)
            piece = pltpu.roll(piece, (PIECE * (to - half)) & (LANES - 1), 1)
            packed = jnp.where(quarter == to, piece, packed)
        out[member, pl.ds(2 * SLAB, 8), :] = packed


def far_rows(channel):
    return (FAR * channel, FAR) if channel < NVAR else (FAR * NVAR + channel - NVAR, 1)


def assemble_kernel(got, own, right_one, left_one, right_two, left_two):
    quarter = lane_iota() // PIECE

    def gathered(sec, row, i):
        value = got[sec * 4, pl.ds(row, 8), :]
        for gy in range(1, 4):
            value = jnp.where(quarter == slot(i, gy), got[sec * 4 + gy, pl.ds(row, 8), :], value)
        return turned(value, -PIECE * i)

    def source(channel, octet):
        if channel < 3:
            return gathered(0, SLAB + 8 * octet, channel + 1)
        if channel < 5:
            return gathered(1, SLAB + 8 * octet, channel - 2)
        sec, v = (channel - 5) // 6, (channel - 5) % 6
        if v < 4:
            return gathered(sec, 8 * octet, v)
        if v == 4:
            return gathered(sec, SLAB + 8 * octet, 0)
        return gathered(sec, 2 * SLAB, octet)

    for ref in (right_two, left_two):
        ref[...] = jnp.zeros((EDGE_TWO, LANES), jnp.float32)
    for channel in range(CHANNELS):
        for octet in range(4):
            value = source(channel, octet)
            own[channel, pl.ds(8 * octet, 8), :] = value
            if channel < 11:
                rows = pl.ds(channel * SLAB + 8 * octet, 8)
                right_one[rows, :] = value
                left_one[rows, :] = value
                at, width = far_rows(channel)
                if octet == 3:
                    right_two[pl.ds(at, width), :] = value[8 - width:]
                if octet == 0:
                    left_two[pl.ds(at, width), :] = value[:width]
            else:
                at = 11 * SLAB + (channel - 11) * NEAR
                if octet > 0:
                    right_one[pl.ds(at + 8 * (octet - 1), 8), :] = value
                if octet < 3:
                    left_one[pl.ds(at + 8 * octet, 8), :] = value


def unpack_kernel(got, out, stacked, packed, turned_ref):
    _, gy, odd = own_place()
    quarter = lane_iota() // PIECE

    def member_of(j):
        j = jnp.where(odd, MEMBERS - 1 - j, j)
        row_block = j // 2
        return (j + row_block) % 2 * 4 + row_block

    for half in range(2):
        for within in range(4):
            member = member_of(4 * half + within)
            stacked[half, pl.ds(within * SLAB, SLAB), :] = got[member, pl.ds(0, SLAB), :]
    for within in range(4):
        low = got[member_of(within), pl.ds(SLAB, 8), :]
        high = got[member_of(4 + within), pl.ds(SLAB, 8), :]
        for octet in range(4):
            back = -PIECE * slot(octet, gy)
            packed[pl.ds(within * SLAB + 8 * octet, 8), :] = jnp.where(
                quarter == 0,
                pltpu.roll(low, back & (LANES - 1), 1),
                pltpu.roll(high, (back + PIECE) & (LANES - 1), 1),
            )
    for half in range(2):
        turned_ref[half] = stacked[half].T
    block = packed[...].T
    for half in range(2):
        columns = slice(half * LANES, (half + 1) * LANES)
        for v in range(4):
            rows = pl.ds(pl.multiple_of(slot(v, gy) * PIECE, PIECE), PIECE)
            out[0, v, :, columns] = turned_ref[half, rows, :]
        out[0, 4, :, columns] = block[half * PIECE:(half + 1) * PIECE]


def weighted(d1, d2, d3, d4, t1, t2, t3):
    a = 3.0 * d2 - d1
    b = d2 + d3
    c = 3.0 * d3 - d4
    y1 = pltpu.reciprocal(t1 + a * a, approx=True)
    y2 = pltpu.reciprocal(t2 + b * b, approx=True)
    y3 = pltpu.reciprocal(t3 + c * c, approx=True)
    g1, g2, g3 = (1.0 / 6.0) * (y1 * y1), y2 * y2, 0.5 * (y3 * y3)
    over = g1 * (a + a - d2) + g2 * (b + d3) + g3 * (c + d3)
    under = g1 + g2 + g3
    return over * pltpu.reciprocal(under, approx=True)


def main_kernel(
    last, speed_y, speed_z, vigneron, coupling,
    own, from_left, from_right, from_left_two, from_right_two,
    out,
    inf, still, base, cur, s0, s1, work_inf, delta, curve, face, rows_part, blocked, half_block, half_strip, strips, *per_block,
):
    across, delta_y, curve_y, face_y = (per_block[NVAR * i:NVAR * (i + 1)] for i in range(4))
    lane = lane_iota()
    center = GUARD + LEFT

    def fill(ref, channel, wide):
        ref[pl.ds(0, GUARD), :] = jnp.zeros((GUARD, LANES), jnp.float32)
        ref[pl.ds(ROWS - GUARD, GUARD), :] = jnp.zeros((GUARD, LANES), jnp.float32)
        ref[pl.ds(center, SLAB), :] = own[channel]
        if wide:
            zeros = jnp.zeros((8, LANES), jnp.float32)
            far, width = far_rows(channel)
            ref[pl.ds(GUARD, 8), :] = zeros
            ref[pl.ds(GUARD + 8 - width, width), :] = from_left_two[pl.ds(far, width), :]
            ref[pl.ds(GUARD + 8, SLAB), :] = from_left[pl.ds(SLAB * channel, SLAB), :]
            ref[pl.ds(center + SLAB, SLAB), :] = from_right[pl.ds(SLAB * channel, SLAB), :]
            ref[pl.ds(center + 2 * SLAB, 8), :] = zeros
            ref[pl.ds(center + 2 * SLAB, width), :] = from_right_two[pl.ds(far, width), :]
        else:
            at = 11 * SLAB + (channel - 11) * NEAR
            zeros = jnp.zeros((16, LANES), jnp.float32)
            ref[pl.ds(GUARD, 16), :] = zeros
            ref[pl.ds(center - NEAR, NEAR), :] = from_left[pl.ds(at, NEAR), :]
            ref[pl.ds(center + SLAB, NEAR), :] = from_right[pl.ds(at, NEAR), :]
            ref[pl.ds(center + SLAB + NEAR, 16), :] = zeros

    for v in range(NVAR):
        fill(inf.at[v], v, True)
        fill(s0.at[v], 5 + v, True)
        fill(cur.at[v], 11 + v, False)
    fill(blocked.at[0], 10, True)
    fill(blocked.at[1], 16, False)
    slab = own_slab()
    for octet in range(ROWS // 8):
        rows = pl.ds(8 * octet, 8)
        column = slab * SLAB + 8 * octet - center + lax.broadcasted_iota(jnp.int32, (8, LANES), 0)
        outside = (column < 0) | (column >= last)
        for station in range(2):
            blocked[station, rows, :] = jnp.where(
                outside | (blocked[station, rows, :] != 0.0), 0.0, 1.0
            )
    for v in range(NVAR):
        across[v][pl.ds(0, GUARD), :] = jnp.zeros((GUARD, LANES), jnp.float32)
        across[v][pl.ds(GUARD + LANES, GUARD), :] = jnp.zeros((GUARD, LANES), jnp.float32)

    sy = [speed_y[v] for v in range(NVAR)]
    sz = [speed_z[v] for v in range(NVAR)]
    half_y = [0.5 * jnp.maximum(s, -s) for s in sy]
    half_z = [0.5 * jnp.maximum(s, -s) for s in sz]
    step_y = [jnp.where(s >= 0.0, 1, -1) for s in sy]
    step_z = [jnp.where(s >= 0.0, 1, -1) for s in sz]
    vig = [vigneron[v] for v in range(NVAR)]
    forward = [(s >= 0.0).astype(jnp.int32) for s in sy]
    ahead = sum(forward)
    rank, seen = [], 0
    for v in range(NVAR):
        rank.append(jnp.where(forward[v] == 1, seen, ahead + v - seen))
        seen = seen + forward[v]

    def nth(r):
        return sum(jnp.where(rank[v] == r, v, 0) for v in range(NVAR))

    turning = (STRIP * ahead + LANES - 1) // LANES * LANES
    place_of = [
        pl.multiple_of(
            jnp.where(forward[v] == 1, STRIP * rank[v], turning + STRIP * (rank[v] - ahead)), 16
        )
        for v in range(NVAR)
    ]
    for b in range(4):
        value = jnp.zeros((8, LANES), jnp.float32)
        for v in range(NVAR):
            at = lane + LANES * b - place_of[v]
            value = jnp.where((at >= 0) & (at < STRIP), half_y[v], value)
        half_strip[b] = value
    strips[...] = jnp.zeros((4 * LANES, LANES), jnp.float32)
    lone = jnp.where(ahead % 2 == 0, NVAR - 1, 0)
    begin = 1 - jnp.minimum(lone, 1)
    couples = [(nth(begin), nth(begin + 1)), (nth(begin + 2), nth(begin + 3)), (nth(lone), nth(lone))]
    for b, (va, vb) in enumerate(couples):
        both = [speed_y[va], speed_y[vb]]
        both = [0.5 * jnp.maximum(s, -s) for s in both]
        half_block[b] = jnp.where(lane < LANES // 2, both[0], both[1])
    per = [0.5 / vig[v] for v in range(NVAR)]
    stiff = [(1.0 + vig[v]) * per[v] for v in range(NVAR)]
    held = [(1.0 - vig[v]) * per[v] for v in range(NVAR)]
    spread = [(STEP_RATIO / 3.0) * per[v] for v in range(NVAR)]
    mix = [[STEP_RATIO * coupling[v, w] * per[v] for w in range(NVAR)] for v in range(NVAR)]

    def newton(v, guess, target):
        for _ in range(NEWTON):
            r = pltpu.reciprocal(1.0 + guess * guess, approx=True)
            square = r * r
            over = (r - square) * guess + target
            under = (0.5 * r - square) + stiff[v]
            guess = over * pltpu.reciprocal(under, approx=True)
        return guess

    def energy(v, field):
        r = pltpu.reciprocal(1.0 + field * field, approx=True)
        return field * (stiff[v] - 0.5 * r)

    def octet_rows(g):
        return pl.multiple_of(GUARD + 8 * g, 8)

    def pairs(low, high, body):
        def two(i, c):
            for k in range(2):
                body(octet_rows(low + 2 * i + k))
            return c
        lax.fori_loop(0, (high - low) // 2, two, 0)

    def differences(src, half, step, d_ref, t_ref, at):
        here = src[pl.ds(at, 8), :]
        down = src[pl.ds(at + step, 8), :]
        up = src[pl.ds(at - step, 8), :]
        d = down - here
        t = d - (here - up)
        d_ref[pl.ds(at, 8), :] = d * half
        t_ref[pl.ds(at, 8), :] = ((13.0 / 3.0) * (half * half)) * (t * t) + WENO_EPS

    def faces(src, half, step, d_ref, t_ref, f_ref, at):
        d3 = d_ref[pl.ds(at, 8), :]
        d2 = d_ref[pl.ds(at - step, 8), :]
        d1 = d_ref[pl.ds(at - 2 * step, 8), :]
        d4 = d_ref[pl.ds(at + step, 8), :]
        t1 = t_ref[pl.ds(at - step, 8), :]
        t2 = t_ref[pl.ds(at, 8), :]
        t3 = t_ref[pl.ds(at + step, 8), :]
        f_ref[pl.ds(at, 8), :] = (6.0 * half) * src[pl.ds(at, 8), :] + weighted(
            d1, d2, d3, d4, t1, t2, t3
        )

    def octets_of(n):
        g0 = 7 - n // 2
        return [GUARD + 8 * g for g in range(g0, g0 + n)]

    def blocks_of(n):
        if n > 8:
            if n == STRIP // 8:
                return [
                    (half_strip[b], jnp.where(LANES * b < turning, 1, -1)) for b in range(4)
                ]
            return list(zip(half_y, step_y))
        return [
            (half_block[b], jnp.where(speed_y[va] >= 0.0, 1, -1))
            for b, (va, _) in enumerate(couples)
        ]

    middle = LANES // 2
    narrow = pl.ds(GUARD + 24, middle)

    strip = pl.ds(GUARD + LEFT + SLAB // 2 - STRIP // 2, STRIP)

    def turn_in(src, n):
        if n == STRIP // 8:
            for v in range(NVAR):
                strips[pl.ds(place_of[v], STRIP), :] = src[v, strip, :]
            for b in range(4):
                across[b][pl.ds(GUARD, LANES), :] = strips[pl.ds(LANES * b, LANES), :].T
        elif n > 8:
            for v in range(NVAR):
                across[v][pl.ds(GUARD, LANES), :] = src[v, pl.ds(GUARD - 8, LANES), :].T
        else:
            for b, couple in enumerate(couples):
                two = [src[v, narrow, :] for v in couple]
                across[b][pl.ds(GUARD, LANES), :] = jnp.concatenate(two, axis=0).T

    def column_differences(src, n):
        octets = octets_of(n)
        for at in [octets[0] - 8] + octets + [octets[-1] + 8]:
            for v in range(NVAR):
                differences(src.at[v], half_z[v], step_z[v], delta.at[v], curve.at[v], at)

    def column_faces(src, octets):
        for at in octets:
            for v in range(NVAR):
                faces(src.at[v], half_z[v], step_z[v], delta.at[v], curve.at[v], face.at[v], at)

    def row_faces(n):
        for b, (half, step) in enumerate(blocks_of(n)):
            row = (across[b], half, step, delta_y[b], curve_y[b])
            for i in range(-1, 17):
                differences(*row, GUARD + 8 * i)
            for i in range(16):
                faces(*row, face_y[b], GUARD + 8 * i)
            faces(*row, face_y[b], GUARD + jnp.where(step > 0, -8, LANES))

    def turn_out(n):
        for b, (_, step) in enumerate(blocks_of(n)):
            change = (
                face_y[b][pl.ds(GUARD, LANES), :] - face_y[b][pl.ds(GUARD - step, LANES), :]
            ).T
            if n == STRIP // 8:
                strips[pl.ds(LANES * b, LANES), :] = change
            elif n > 8:
                rows_part[b] = change
            else:
                rows = pl.ds(8 + 24, middle)
                rows_part[couples[b][0], rows, :] = change[:middle]
                rows_part[couples[b][1], rows, :] = change[middle:]
        if n == STRIP // 8:
            rows = pl.ds(8 + LEFT + SLAB // 2 - STRIP // 2, STRIP)
            for v in range(NVAR):
                rows_part[v, rows, :] = strips[pl.ds(place_of[v], STRIP), :]

    def sources(src, at):
        field = [src[v, pl.ds(at, 8), :] for v in range(NVAR)]
        result = []
        for v in range(NVAR):
            columns = face[v, pl.ds(at, 8), :] - face[v, pl.ds(at - step_z[v], 8), :]
            rows = rows_part[v, pl.ds(at - (GUARD - 8), 8), :]
            mixed = mix[v][0] * field[0]
            for w in range(1, NVAR):
                mixed = mixed + mix[v][w] * field[w]
            result.append(mixed - spread[v] * (rows + columns))
        return field, result

    def steps(station, octets):
        for at in octets:
            field, terms = sources(cur, at)
            fluid = blocked[station, pl.ds(at, 8), :] != 0.0
            for v in range(NVAR):
                value = newton(v, field[v], still[v, pl.ds(at, 8), :] + terms[v])
                cur[v, pl.ds(at, 8), :] = jnp.where(fluid, value, 0.0)

    turn_in(inf, 14)
    column_differences(inf, 14)
    row_faces(14)
    turn_out(14)
    column_faces(inf, octets_of(14))
    for at in octets_of(14):
        field, terms = sources(inf, at)
        for v in range(NVAR):
            base[v, pl.ds(at, 8), :] = energy(v, field[v])
            work_inf[v, pl.ds(at, 8), :] = terms[v]

    def first_of_0(at):
        fluid = blocked[0, pl.ds(at, 8), :] != 0.0
        for v in range(NVAR):
            s1[v, pl.ds(at, 8), :] = cur[v, pl.ds(at, 8), :]
            here = inf[v, pl.ds(at, 8), :]
            prior = s0[v, pl.ds(at, 8), :]
            fixed = base[v, pl.ds(at, 8), :] - held[v] * (prior - here)
            still[v, pl.ds(at, 8), :] = fixed
            value = newton(v, here, fixed + work_inf[v, pl.ds(at, 8), :])
            cur[v, pl.ds(at, 8), :] = jnp.where(fluid, value, 0.0)

    def start_of_1(at):
        for v in range(NVAR):
            above = cur[v, pl.ds(at, 8), :]
            prior = s1[v, pl.ds(at, 8), :] - s0[v, pl.ds(at, 8), :]
            still[v, pl.ds(at, 8), :] = energy(v, above) - held[v] * prior
            s0[v, pl.ds(at, 8), :] = above

    def pass_of(t, carry):
        k, c = t // 5, t % 5

        @pl.when(c == 0)
        def _():
            g0 = (6 + 6 * k) // 8
            pairs(g0, 14 - g0, first_of_0)

        @pl.when(c == 2)
        def _():
            g0 = (12 + 6 * k) // 8
            pairs(g0, 14 - g0, start_of_1)

        station = (c >= 2).astype(jnp.int32)
        g0 = (9 + 6 * k + 3 * c) // 8
        for n in (12, 10, 8, 6):
            times = (g0 == 7 - n // 2).astype(jnp.int32)

            def part(i, c, n=n):
                turn_in(cur, n)
                column_differences(cur, n)
                column_faces(cur, octets_of(n)[:n // 3])
                return c
            lax.fori_loop(0, times, part, 0)

            def part(i, c, n=n):
                row_faces(n)
                return c
            lax.fori_loop(0, times, part, 0)

            def part(i, c, n=n):
                turn_out(n)
                column_faces(cur, octets_of(n)[n // 3:])
                steps(station, octets_of(n))
                return c
            lax.fori_loop(0, times, part, 0)
        return carry

    lax.fori_loop(0, 5 * ITERS, pass_of, 0)

    quarter = lane // PIECE
    for station, result in enumerate((s0, cur)):
        at_last = []
        for octet in range(4):
            rows = pl.ds(center + 8 * octet, 8)
            field = [turned(result[v, rows, :], PIECE * v) for v in range(4)]
            at_last.append(turned(result[4, rows, :], PIECE * octet))
            for gy in range(4):
                value = field[0]
                for v in range(1, 4):
                    value = jnp.where(quarter == slot(v, gy), field[v], value)
                out[station * 4 + gy, pl.ds(8 * octet, 8), :] = value
        for gy in range(4):
            value = at_last[0]
            for octet in range(1, 4):
                value = jnp.where(quarter == slot(octet, gy), at_last[octet], value)
            out[station * 4 + gy, pl.ds(SLAB, 8), :] = value


def slabs_per_device(inflow, initial, solid, speed_y, speed_z, vigneron, coupling):
    mesh_axes = ("sec", "gy", "gz")
    nz_parts = lax.axis_size("gz")
    path = []
    for z in range(nz_parts):
        members = [(s, y) for y in range(4) for s in ((0, 1) if y % 2 == 0 else (1, 0))]
        path += [(s * 4 + y) * nz_parts + z for s, y in (members if z % 2 == 0 else members[::-1])]

    def along(value, steps):
        count = len(path)
        low, high = max(0, -steps), min(count, count - steps)
        return lax.ppermute(value, mesh_axes, [(path[i], path[i + steps]) for i in range(low, high)])

    smem = pl.BlockSpec(memory_space=pltpu.SMEM)
    vmem = pl.BlockSpec(memory_space=pltpu.VMEM)
    f32 = functools.partial(jax.ShapeDtypeStruct, dtype=jnp.float32)

    packed = pl.pallas_call(
        pack_kernel,
        out_shape=pltpu.VMEM((MEMBERS, CHUNK_IN, LANES), jnp.float32),
        in_specs=[vmem, vmem, vmem],
        out_specs=vmem,
        scratch_shapes=[
            pltpu.VMEM((2, LANES, TILE), jnp.float32),
            pltpu.VMEM((3, TILE, LANES), jnp.float32),
            pltpu.VMEM((LANES, LANES), jnp.float32),
        ],
        name="pack",
    )(inflow, initial, solid)
    got = lax.all_to_all(packed, ("sec", "gy"), 0, 0)
    got = pltpu.with_memory_space_constraint(got, pltpu.VMEM)
    own, right_one, left_one, right_two, left_two = pl.pallas_call(
        assemble_kernel,
        out_shape=[
            pltpu.VMEM((CHANNELS, SLAB, LANES), jnp.float32),
            pltpu.VMEM((EDGE_ONE, LANES), jnp.float32),
            pltpu.VMEM((EDGE_ONE, LANES), jnp.float32),
            pltpu.VMEM((EDGE_TWO, LANES), jnp.float32),
            pltpu.VMEM((EDGE_TWO, LANES), jnp.float32),
        ],
        in_specs=[vmem],
        out_specs=[vmem] * 5,
        name="assemble",
    )(got)
    window = pltpu.VMEM((NVAR, ROWS, LANES), jnp.float32)
    sent = pl.pallas_call(
        functools.partial(main_kernel, len(path) * SLAB),
        out_shape=f32((MEMBERS, CHUNK_OUT, LANES)),
        in_specs=[smem] * 4 + [vmem] * 5,
        out_specs=vmem,
        scratch_shapes=[
            window, window, window, window, window, window, window, window, window, window,
            pltpu.VMEM((NVAR, LANES, LANES), jnp.float32),
            pltpu.VMEM((2, ROWS, LANES), jnp.float32),
            pltpu.VMEM((3, 8, LANES), jnp.float32),
            pltpu.VMEM((4, 8, LANES), jnp.float32),
            pltpu.VMEM((4 * LANES, LANES), jnp.float32),
        ] + [pltpu.VMEM((LANES + 2 * GUARD, LANES), jnp.float32)] * (4 * NVAR),
        compiler_params=pltpu.CompilerParams(vmem_limit_bytes=32 * 1024 * 1024),
        name="march",
    )(
        speed_y, speed_z, vigneron, coupling,
        own, along(right_one, 1), along(left_one, -1), along(right_two, 2), along(left_two, -2),
    )
    returned = lax.all_to_all(sent, ("sec", "gy"), 0, 0)
    returned = pltpu.with_memory_space_constraint(returned, pltpu.VMEM)
    return pl.pallas_call(
        unpack_kernel,
        out_shape=f32((1, NVAR, PIECE, TILE)),
        in_specs=[vmem],
        out_specs=vmem,
        scratch_shapes=[
            pltpu.VMEM((2, LANES, LANES), jnp.float32),
            pltpu.VMEM((LANES, LANES), jnp.float32),
            pltpu.VMEM((2, LANES, LANES), jnp.float32),
        ],
        name="unpack",
    )(returned)


def chosen(*args):
    inflow, initial = args[0], args[1]
    fits = (
        lax.axis_size("sec") == 2
        and lax.axis_size("gy") == 4
        and inflow.shape == (NVAR, PIECE, TILE)
        and initial.shape == (1, NVAR, PIECE, TILE)
    )
    return slabs_per_device(*args) if fits else per_device(*args)


def solution(mesh):
    return jax.shard_map(
        chosen,
        mesh=mesh,
        in_specs=(
            P(None, "gy", "gz"),
            P("sec", None, "gy", "gz"),
            P("sec", "gy", "gz"),
            P(),
            P(),
            P(),
            P(),
        ),
        out_specs=P("sec", None, "gy", "gz"),
        check_vma=False,
    )
```

```python
import functools

import jax
import jax.numpy as jnp
from jax import lax
from jax.experimental import pallas as pl
from jax.experimental.pallas import tpu as pltpu
from jax.sharding import PartitionSpec as P

NVAR = 5
ITERS = 4
CORRECTORS = 3
NEWTON = 2

STEP_RATIO = 0.25
WENO_EPS = 1e-06


def passed_along(value, axis, steps):
    count = lax.axis_size(axis)
    initial, last = (max(0, -steps), min(count, count - steps))
    return lax.ppermute(value, axis, [(source, source + steps) for source in range(initial, last)])


def extended(block, sides, width):
    for axis, dim in sides:
        count = lax.axis_size(axis)
        forward = [(i, i + 1) for i in range(count - 1)]
        backward = [(target, source) for source, target in forward]
        low = lax.ppermute(
            lax.slice_in_dim(block, block.shape[dim] - width, None, axis=dim), axis, forward
        )
        high = lax.ppermute(lax.slice_in_dim(block, 0, width, axis=dim), axis, backward)
        block = jnp.concatenate([low, block, high], axis=dim)
    return block


def weno_face(left_far, left_near, center, right_near, right_far):
    smooth_left = (
        13.0 / 12.0 * (left_far - 2.0 * left_near + center) ** 2
        + 0.25 * (left_far - 4.0 * left_near + 3.0 * center) ** 2
    )
    smooth_middle = (
        13.0 / 12.0 * (left_near - 2.0 * center + right_near) ** 2
        + 0.25 * (left_near - right_near) ** 2
    )
    smooth_right = (
        13.0 / 12.0 * (center - 2.0 * right_near + right_far) ** 2
        + 0.25 * (3.0 * center - 4.0 * right_near + right_far) ** 2
    )
    weight_left = 0.1 / (WENO_EPS + smooth_left) ** 2
    weight_middle = 0.6 / (WENO_EPS + smooth_middle) ** 2
    weight_right = 0.3 / (WENO_EPS + smooth_right) ** 2
    guess_left = (2.0 * left_far - 7.0 * left_near + 11.0 * center) / 6.0
    guess_middle = (-left_near + 5.0 * center + 2.0 * right_near) / 6.0
    guess_right = (2.0 * center + 5.0 * right_near - right_far) / 6.0
    total = weight_left * guess_left + weight_middle * guess_middle + weight_right * guess_right
    return total / (weight_left + weight_middle + weight_right)


def sweep(padded, speeds, axis):
    count = padded.shape[axis] - 6
    plus_flux = jnp.maximum(speeds, 0.0)[:, None, None] * padded
    minus_flux = jnp.minimum(speeds, 0.0)[:, None, None] * padded

    def window(source, offset):
        return lax.slice_in_dim(source, offset, offset + count + 1, axis=axis)

    faces = weno_face(*(window(plus_flux, i) for i in (0, 1, 2, 3, 4)))
    faces = faces + weno_face(*(window(minus_flux, i) for i in (5, 4, 3, 2, 1)))
    return lax.slice_in_dim(faces, 1, count + 1, axis=axis) - lax.slice_in_dim(
        faces, 0, count, axis=axis
    )


def crossflow(padded, speed_y, speed_z):
    rows_part = sweep(padded[:, :, 3:-3], speed_y, 1)
    cols_part = sweep(padded[:, 3:-3, :], speed_z, 2)
    return rows_part + cols_part


def streamwise(field, factor):
    return field + factor * field**3 / (1.0 + field**2)


def slope(field, factor):
    return 1.0 + factor * field**2 * (3.0 + field**2) / (1.0 + field**2) ** 2


def correct(padded, current, upstream, diff, blocked, params):
    speed_y, speed_z, vigneron, coupling = params
    factor = vigneron[:, None, None]
    mixed = jnp.einsum("vw,wyz->vyz", coupling, current, precision=lax.Precision.HIGHEST)
    target = (
        streamwise(upstream, factor)
        - STEP_RATIO * crossflow(padded, speed_y, speed_z)
        + STEP_RATIO * mixed
        - (1.0 - factor) * diff
    )
    guess = current
    for newton_index in range(NEWTON):
        guess = guess - (streamwise(guess, factor) - target) / slope(guess, factor)
    return jnp.where(blocked[None], 0.0, guess)


def per_device(inflow, initial, solid, speed_y, speed_z, vigneron, coupling):
    params = (speed_y, speed_z, vigneron, coupling)
    sections = lax.axis_size("sec")
    position = lax.axis_index("sec")
    is_first = position == 0
    start_plane = initial[0]
    guess_above = passed_along(start_plane, "sec", 1)
    guess_above = jnp.where(is_first, inflow, guess_above)
    solid_tile = solid[0] != 0

    def station(upstream, diff):
        current = upstream
        for corrector_index in range(CORRECTORS):
            padded = extended(current, (("gy", 1), ("gz", 2)), 3)
            current = correct(padded, current, upstream, diff, solid_tile, params)
        return current

    def advance(step_index, carry):
        sent, own_prior, upstream_prior = carry
        received = passed_along(sent, "sec", 1)
        received = jnp.where(is_first, inflow, received)
        iterate = step_index - position + 1
        active = (iterate >= 1) & (iterate <= ITERS)
        updated = station(received, own_prior - upstream_prior)
        own_next = jnp.where(active, updated, own_prior)
        upstream_next = jnp.where(active, received, upstream_prior)
        return (own_next, own_next, upstream_next)

    result = lax.fori_loop(
        0, ITERS + sections - 1, advance, (start_plane, start_plane, guess_above)
    )
    return result[1][None]


LANES = 128
SLAB = 32
TILE = 256
MEMBERS = 8
PIECE = 32
GUARD = 16
STRIP = 80
LEFT = 40
ROWS = GUARD + LEFT + SLAB + LEFT + GUARD
CHUNK_IN = 72
CHUNK_OUT = 40
NEAR = 24
EDGE_ONE = 11 * SLAB + 6 * NEAR
FAR = 4
EDGE_TWO = 32
CHANNELS = 17


def lane_iota():
    return lax.broadcasted_iota(jnp.int32, (8, LANES), 1)


def turned(value, shift):
    shift = shift % LANES
    return value if shift == 0 else pltpu.roll(value, shift, 1)


def slab_of(member, odd):
    sec, gy = member // 4, member % 4
    j = 2 * gy + (sec ^ (gy & 1))
    return jnp.where(odd, MEMBERS - 1 - j, j)


def own_place():
    return lax.axis_index("sec"), lax.axis_index("gy"), lax.axis_index("gz") % 2 == 1


def own_slab():
    sec, gy, odd = own_place()
    return lax.axis_index("gz") * MEMBERS + slab_of(sec * 4 + gy, odd)


def slot(i, gy):
    return (i + gy) % 4


def pack_kernel(inflow, initial, solid, out, stacked, turned_ref, solids):
    sec, gy, odd = own_place()
    for group in range(2):
        for p in range(4):
            rows = pl.ds(pl.multiple_of(slot(p, gy) * PIECE, PIECE), PIECE)
            if group == 0:
                stacked[group, rows, :] = initial[0, p]
            elif p == 0:
                stacked[group, rows, :] = initial[0, 4]
            else:
                stacked[group, rows, :] = inflow[jnp.minimum(3 * sec + p - 1, NVAR - 1)]
    for half in range(2):
        solids[pl.ds(half * PIECE, PIECE), :] = solid[
            0, :, half * LANES:(half + 1) * LANES
        ].astype(jnp.float32)
    solids[pl.ds(2 * PIECE, 2 * PIECE), :] = jnp.zeros((2 * PIECE, LANES), jnp.float32)
    for group in range(2):
        for half in range(2):
            turned_ref[group, pl.ds(half * LANES, LANES), :] = stacked[
                group, :, half * LANES:(half + 1) * LANES
            ].T
    turned_ref[2, pl.ds(0, LANES), :] = solids[...].T
    quarter = lane_iota() // PIECE
    for member in range(MEMBERS):
        j = slab_of(member, odd)
        rows = pl.ds(pl.multiple_of(j * SLAB, SLAB), SLAB)
        for group in range(2):
            out[member, pl.ds(group * SLAB, SLAB), :] = turned_ref[group, rows, :]
        half, within = j // 4, j % 4
        packed = jnp.zeros((8, LANES), jnp.float32)
        for octet in range(4):
            piece = turned_ref[2, pl.ds(pl.multiple_of(within * SLAB + octet * 8, 8), 8), :]
            to = slot(octet, gy)
            piece = pltpu.roll(piece, (PIECE * (to - half)) & (LANES - 1), 1)
            packed = jnp.where(quarter == to, piece, packed)
        out[member, pl.ds(2 * SLAB, 8), :] = packed


def far_rows(channel):
    return (FAR * channel, FAR) if channel < NVAR else (FAR * NVAR + channel - NVAR, 1)


def assemble_kernel(got, own, right_one, left_one, right_two, left_two):
    quarter = lane_iota() // PIECE

    def gathered(sec, row, i):
        value = got[sec * 4, pl.ds(row, 8), :]
        for gy in range(1, 4):
            value = jnp.where(quarter == slot(i, gy), got[sec * 4 + gy, pl.ds(row, 8), :], value)
        return turned(value, -PIECE * i)

    def source(channel, octet):
        if channel < 3:
            return gathered(0, SLAB + 8 * octet, channel + 1)
        if channel < 5:
            return gathered(1, SLAB + 8 * octet, channel - 2)
        sec, v = (channel - 5) // 6, (channel - 5) % 6
        if v < 4:
            return gathered(sec, 8 * octet, v)
        if v == 4:
            return gathered(sec, SLAB + 8 * octet, 0)
        return gathered(sec, 2 * SLAB, octet)

    for ref in (right_two, left_two):
        ref[...] = jnp.zeros((EDGE_TWO, LANES), jnp.float32)
    for channel in range(CHANNELS):
        for octet in range(4):
            value = source(channel, octet)
            own[channel, pl.ds(8 * octet, 8), :] = value
            if channel < 11:
                rows = pl.ds(channel * SLAB + 8 * octet, 8)
                right_one[rows, :] = value
                left_one[rows, :] = value
                at, width = far_rows(channel)
                if octet == 3:
                    right_two[pl.ds(at, width), :] = value[8 - width:]
                if octet == 0:
                    left_two[pl.ds(at, width), :] = value[:width]
            else:
                at = 11 * SLAB + (channel - 11) * NEAR
                if octet > 0:
                    right_one[pl.ds(at + 8 * (octet - 1), 8), :] = value
                if octet < 3:
                    left_one[pl.ds(at + 8 * octet, 8), :] = value


def unpack_kernel(got, out, stacked, packed, turned_ref):
    _, gy, odd = own_place()
    quarter = lane_iota() // PIECE

    def member_of(j):
        j = jnp.where(odd, MEMBERS - 1 - j, j)
        row_block = j // 2
        return (j + row_block) % 2 * 4 + row_block

    for half in range(2):
        for within in range(4):
            member = member_of(4 * half + within)
            stacked[half, pl.ds(within * SLAB, SLAB), :] = got[member, pl.ds(0, SLAB), :]
    for within in range(4):
        low = got[member_of(within), pl.ds(SLAB, 8), :]
        high = got[member_of(4 + within), pl.ds(SLAB, 8), :]
        for octet in range(4):
            back = -PIECE * slot(octet, gy)
            packed[pl.ds(within * SLAB + 8 * octet, 8), :] = jnp.where(
                quarter == 0,
                pltpu.roll(low, back & (LANES - 1), 1),
                pltpu.roll(high, (back + PIECE) & (LANES - 1), 1),
            )
    for half in range(2):
        turned_ref[half] = stacked[half].T
    block = packed[...].T
    for half in range(2):
        columns = slice(half * LANES, (half + 1) * LANES)
        for v in range(4):
            rows = pl.ds(pl.multiple_of(slot(v, gy) * PIECE, PIECE), PIECE)
            out[0, v, :, columns] = turned_ref[half, rows, :]
        out[0, 4, :, columns] = block[half * PIECE:(half + 1) * PIECE]


def weighted(d1, d2, d3, d4, t1, t2, t3):
    a = 3.0 * d2 - d1
    b = d2 + d3
    c = 3.0 * d3 - d4
    y1 = pltpu.reciprocal(t1 + a * a, approx=True)
    y2 = pltpu.reciprocal(t2 + b * b, approx=True)
    y3 = pltpu.reciprocal(t3 + c * c, approx=True)
    g1, g2, g3 = (1.0 / 6.0) * (y1 * y1), y2 * y2, 0.5 * (y3 * y3)
    over = g1 * (a + a - d2) + g2 * (b + d3) + g3 * (c + d3)
    under = g1 + g2 + g3
    return over * pltpu.reciprocal(under, approx=True)


def main_kernel(
    last, speed_y, speed_z, vigneron, coupling,
    own, from_left, from_right, from_left_two, from_right_two,
    out,
    inf, still, base, cur, s0, s1, work_inf, delta, curve, face, rows_part, blocked, half_block, half_strip, strips, *per_block,
):
    across, delta_y, curve_y, face_y = (per_block[NVAR * i:NVAR * (i + 1)] for i in range(4))
    lane = lane_iota()
    center = GUARD + LEFT

    def fill(ref, channel, wide):
        ref[pl.ds(0, GUARD), :] = jnp.zeros((GUARD, LANES), jnp.float32)
        ref[pl.ds(ROWS - GUARD, GUARD), :] = jnp.zeros((GUARD, LANES), jnp.float32)
        ref[pl.ds(center, SLAB), :] = own[channel]
        if wide:
            zeros = jnp.zeros((8, LANES), jnp.float32)
            far, width = far_rows(channel)
            ref[pl.ds(GUARD, 8), :] = zeros
            ref[pl.ds(GUARD + 8 - width, width), :] = from_left_two[pl.ds(far, width), :]
            ref[pl.ds(GUARD + 8, SLAB), :] = from_left[pl.ds(SLAB * channel, SLAB), :]
            ref[pl.ds(center + SLAB, SLAB), :] = from_right[pl.ds(SLAB * channel, SLAB), :]
            ref[pl.ds(center + 2 * SLAB, 8), :] = zeros
            ref[pl.ds(center + 2 * SLAB, width), :] = from_right_two[pl.ds(far, width), :]
        else:
            at = 11 * SLAB + (channel - 11) * NEAR
            zeros = jnp.zeros((16, LANES), jnp.float32)
            ref[pl.ds(GUARD, 16), :] = zeros
            ref[pl.ds(center - NEAR, NEAR), :] = from_left[pl.ds(at, NEAR), :]
            ref[pl.ds(center + SLAB, NEAR), :] = from_right[pl.ds(at, NEAR), :]
            ref[pl.ds(center + SLAB + NEAR, 16), :] = zeros

    for v in range(NVAR):
        fill(inf.at[v], v, True)
        fill(s0.at[v], 5 + v, True)
        fill(cur.at[v], 11 + v, False)
    fill(blocked.at[0], 10, True)
    fill(blocked.at[1], 16, False)
    slab = own_slab()
    for octet in range(ROWS // 8):
        rows = pl.ds(8 * octet, 8)
        column = slab * SLAB + 8 * octet - center + lax.broadcasted_iota(jnp.int32, (8, LANES), 0)
        outside = (column < 0) | (column >= last)
        for station in range(2):
            blocked[station, rows, :] = jnp.where(
                outside | (blocked[station, rows, :] != 0.0), 0.0, 1.0
            )
    for v in range(NVAR):
        across[v][pl.ds(0, GUARD), :] = jnp.zeros((GUARD, LANES), jnp.float32)
        across[v][pl.ds(GUARD + LANES, GUARD), :] = jnp.zeros((GUARD, LANES), jnp.float32)

    sy = [speed_y[v] for v in range(NVAR)]
    sz = [speed_z[v] for v in range(NVAR)]
    half_y = [0.5 * jnp.maximum(s, -s) for s in sy]
    half_z = [0.5 * jnp.maximum(s, -s) for s in sz]
    step_y = [jnp.where(s >= 0.0, 1, -1) for s in sy]
    step_z = [jnp.where(s >= 0.0, 1, -1) for s in sz]
    vig = [vigneron[v] for v in range(NVAR)]
    forward = [(s >= 0.0).astype(jnp.int32) for s in sy]
    ahead = sum(forward)
    rank, seen = [], 0
    for v in range(NVAR):
        rank.append(jnp.where(forward[v] == 1, seen, ahead + v - seen))
        seen = seen + forward[v]

    def nth(r):
        return sum(jnp.where(rank[v] == r, v, 0) for v in range(NVAR))

    turning = (STRIP * ahead + LANES - 1) // LANES * LANES
    place_of = [
        pl.multiple_of(
            jnp.where(forward[v] == 1, STRIP * rank[v], turning + STRIP * (rank[v] - ahead)), 16
        )
        for v in range(NVAR)
    ]
    for b in range(4):
        value = jnp.zeros((8, LANES), jnp.float32)
        for v in range(NVAR):
            at = lane + LANES * b - place_of[v]
            value = jnp.where((at >= 0) & (at < STRIP), half_y[v], value)
        half_strip[b] = value
    strips[...] = jnp.zeros((4 * LANES, LANES), jnp.float32)
    lone = jnp.where(ahead % 2 == 0, NVAR - 1, 0)
    begin = 1 - jnp.minimum(lone, 1)
    couples = [(nth(begin), nth(begin + 1)), (nth(begin + 2), nth(begin + 3)), (nth(lone), nth(lone))]
    for b, (va, vb) in enumerate(couples):
        both = [speed_y[va], speed_y[vb]]
        both = [0.5 * jnp.maximum(s, -s) for s in both]
        half_block[b] = jnp.where(lane < LANES // 2, both[0], both[1])
    per = [0.5 / vig[v] for v in range(NVAR)]
    stiff = [(1.0 + vig[v]) * per[v] for v in range(NVAR)]
    held = [(1.0 - vig[v]) * per[v] for v in range(NVAR)]
    spread = [(STEP_RATIO / 3.0) * per[v] for v in range(NVAR)]
    mix = [[STEP_RATIO * coupling[v, w] * per[v] for w in range(NVAR)] for v in range(NVAR)]

    def newton(v, guess, target):
        for _ in range(NEWTON):
            r = pltpu.reciprocal(1.0 + guess * guess, approx=True)
            square = r * r
            over = (r - square) * guess + target
            under = (0.5 * r - square) + stiff[v]
            guess = over * pltpu.reciprocal(under, approx=True)
        return guess

    def energy(v, field):
        r = pltpu.reciprocal(1.0 + field * field, approx=True)
        return field * (stiff[v] - 0.5 * r)

    def octet_rows(g):
        return pl.multiple_of(GUARD + 8 * g, 8)

    def pairs(low, high, body):
        def two(i, c):
            for k in range(2):
                body(octet_rows(low + 2 * i + k))
            return c
        lax.fori_loop(0, (high - low) // 2, two, 0)

    def differences(src, half, step, d_ref, t_ref, at):
        here = src[pl.ds(at, 8), :]
        down = src[pl.ds(at + step, 8), :]
        up = src[pl.ds(at - step, 8), :]
        d = down - here
        t = d - (here - up)
        d_ref[pl.ds(at, 8), :] = d * half
        t_ref[pl.ds(at, 8), :] = ((13.0 / 3.0) * (half * half)) * (t * t) + WENO_EPS

    def faces(src, half, step, d_ref, t_ref, f_ref, at):
        d3 = d_ref[pl.ds(at, 8), :]
        d2 = d_ref[pl.ds(at - step, 8), :]
        d1 = d_ref[pl.ds(at - 2 * step, 8), :]
        d4 = d_ref[pl.ds(at + step, 8), :]
        t1 = t_ref[pl.ds(at - step, 8), :]
        t2 = t_ref[pl.ds(at, 8), :]
        t3 = t_ref[pl.ds(at + step, 8), :]
        f_ref[pl.ds(at, 8), :] = (6.0 * half) * src[pl.ds(at, 8), :] + weighted(
            d1, d2, d3, d4, t1, t2, t3
        )

    def octets_of(n):
        g0 = 7 - n // 2
        return [GUARD + 8 * g for g in range(g0, g0 + n)]

    def blocks_of(n):
        if n > 8:
            if n == STRIP // 8:
                return [
                    (half_strip[b], jnp.where(LANES * b < turning, 1, -1)) for b in range(4)
                ]
            return list(zip(half_y, step_y))
        return [
            (half_block[b], jnp.where(speed_y[va] >= 0.0, 1, -1))
            for b, (va, _) in enumerate(couples)
        ]

    middle = LANES // 2
    narrow = pl.ds(GUARD + 24, middle)

    strip = pl.ds(GUARD + LEFT + SLAB // 2 - STRIP // 2, STRIP)

    def turn_in(src, n):
        if n == STRIP // 8:
            for v in range(NVAR):
                strips[pl.ds(place_of[v], STRIP), :] = src[v, strip, :]
            for b in range(4):
                across[b][pl.ds(GUARD, LANES), :] = strips[pl.ds(LANES * b, LANES), :].T
        elif n > 8:
            for v in range(NVAR):
                across[v][pl.ds(GUARD, LANES), :] = src[v, pl.ds(GUARD - 8, LANES), :].T
        else:
            for b, couple in enumerate(couples):
                two = [src[v, narrow, :] for v in couple]
                across[b][pl.ds(GUARD, LANES), :] = jnp.concatenate(two, axis=0).T

    def column_differences(src, n):
        octets = octets_of(n)
        for at in [octets[0] - 8] + octets + [octets[-1] + 8]:
            for v in range(NVAR):
                differences(src.at[v], half_z[v], step_z[v], delta.at[v], curve.at[v], at)

    def column_faces(src, octets):
        for at in octets:
            for v in range(NVAR):
                faces(src.at[v], half_z[v], step_z[v], delta.at[v], curve.at[v], face.at[v], at)

    def entry_faces(src, n):
        octets = octets_of(n)
        for v in range(NVAR):
            at = jnp.where(step_z[v] > 0, octets[0] - 8, octets[-1] + 8)
            faces(src.at[v], half_z[v], step_z[v], delta.at[v], curve.at[v], face.at[v], at)

    def row_faces(n):
        for b, (half, step) in enumerate(blocks_of(n)):
            row = (across[b], half, step, delta_y[b], curve_y[b])
            for i in range(-1, 17):
                differences(*row, GUARD + 8 * i)
            for i in range(16):
                faces(*row, face_y[b], GUARD + 8 * i)
            faces(*row, face_y[b], GUARD + jnp.where(step > 0, -8, LANES))

    def turn_out(n):
        for b, (_, step) in enumerate(blocks_of(n)):
            change = (
                face_y[b][pl.ds(GUARD, LANES), :] - face_y[b][pl.ds(GUARD - step, LANES), :]
            ).T
            if n == STRIP // 8:
                strips[pl.ds(LANES * b, LANES), :] = change
            elif n > 8:
                rows_part[b] = change
            else:
                rows = pl.ds(8 + 24, middle)
                rows_part[couples[b][0], rows, :] = change[:middle]
                rows_part[couples[b][1], rows, :] = change[middle:]
        if n == STRIP // 8:
            rows = pl.ds(8 + LEFT + SLAB // 2 - STRIP // 2, STRIP)
            for v in range(NVAR):
                rows_part[v, rows, :] = strips[pl.ds(place_of[v], STRIP), :]

    def sources(src, at):
        field = [src[v, pl.ds(at, 8), :] for v in range(NVAR)]
        result = []
        for v in range(NVAR):
            columns = face[v, pl.ds(at, 8), :] - face[v, pl.ds(at - step_z[v], 8), :]
            rows = rows_part[v, pl.ds(at - (GUARD - 8), 8), :]
            mixed = mix[v][0] * field[0]
            for w in range(1, NVAR):
                mixed = mixed + mix[v][w] * field[w]
            result.append(mixed - spread[v] * (rows + columns))
        return field, result

    def steps(station, octets):
        for at in octets:
            field, terms = sources(cur, at)
            fluid = blocked[station, pl.ds(at, 8), :] != 0.0
            for v in range(NVAR):
                value = newton(v, field[v], still[v, pl.ds(at, 8), :] + terms[v])
                cur[v, pl.ds(at, 8), :] = jnp.where(fluid, value, 0.0)

    turn_in(inf, 14)
    column_differences(inf, 14)
    row_faces(14)
    turn_out(14)
    column_faces(inf, octets_of(14))
    for at in octets_of(14):
        field, terms = sources(inf, at)
        for v in range(NVAR):
            base[v, pl.ds(at, 8), :] = energy(v, field[v])
            work_inf[v, pl.ds(at, 8), :] = terms[v]

    def first_of_0(at):
        fluid = blocked[0, pl.ds(at, 8), :] != 0.0
        for v in range(NVAR):
            s1[v, pl.ds(at, 8), :] = cur[v, pl.ds(at, 8), :]
            here = inf[v, pl.ds(at, 8), :]
            prior = s0[v, pl.ds(at, 8), :]
            fixed = base[v, pl.ds(at, 8), :] - held[v] * (prior - here)
            still[v, pl.ds(at, 8), :] = fixed
            value = newton(v, here, fixed + work_inf[v, pl.ds(at, 8), :])
            cur[v, pl.ds(at, 8), :] = jnp.where(fluid, value, 0.0)

    def start_of_1(at):
        for v in range(NVAR):
            above = cur[v, pl.ds(at, 8), :]
            prior = s1[v, pl.ds(at, 8), :] - s0[v, pl.ds(at, 8), :]
            still[v, pl.ds(at, 8), :] = energy(v, above) - held[v] * prior
            s0[v, pl.ds(at, 8), :] = above

    def pass_of(t, carry):
        k, c = t // 5, t % 5

        @pl.when(c == 0)
        def _():
            g0 = (6 + 6 * k) // 8
            pairs(g0, 14 - g0, first_of_0)

        @pl.when(c == 2)
        def _():
            g0 = (12 + 6 * k) // 8
            pairs(g0, 14 - g0, start_of_1)

        station = (c >= 2).astype(jnp.int32)
        g0 = jnp.minimum((10 + 6 * k + 3 * c) // 8, 4)
        for n in (12, 10, 8, 6):
            times = (g0 == 7 - n // 2).astype(jnp.int32)

            def part(i, c, n=n):
                turn_in(cur, n)
                column_differences(cur, n)
                column_faces(cur, octets_of(n)[:n // 3])
                return c
            lax.fori_loop(0, times, part, 0)

            def part(i, c, n=n):
                row_faces(n)
                return c
            lax.fori_loop(0, times, part, 0)

            def part(i, c, n=n):
                turn_out(n)
                column_faces(cur, octets_of(n)[n // 3:])
                if n == STRIP // 8:
                    entry_faces(cur, n)
                steps(station, octets_of(n))
                return c
            lax.fori_loop(0, times, part, 0)
        return carry

    lax.fori_loop(0, 5 * ITERS, pass_of, 0)

    quarter = lane // PIECE
    for station, result in enumerate((s0, cur)):
        at_last = []
        for octet in range(4):
            rows = pl.ds(center + 8 * octet, 8)
            field = [turned(result[v, rows, :], PIECE * v) for v in range(4)]
            at_last.append(turned(result[4, rows, :], PIECE * octet))
            for gy in range(4):
                value = field[0]
                for v in range(1, 4):
                    value = jnp.where(quarter == slot(v, gy), field[v], value)
                out[station * 4 + gy, pl.ds(8 * octet, 8), :] = value
        for gy in range(4):
            value = at_last[0]
            for octet in range(1, 4):
                value = jnp.where(quarter == slot(octet, gy), at_last[octet], value)
            out[station * 4 + gy, pl.ds(SLAB, 8), :] = value


def slabs_per_device(inflow, initial, solid, speed_y, speed_z, vigneron, coupling):
    mesh_axes = ("sec", "gy", "gz")
    nz_parts = lax.axis_size("gz")
    path = []
    for z in range(nz_parts):
        members = [(s, y) for y in range(4) for s in ((0, 1) if y % 2 == 0 else (1, 0))]
        path += [(s * 4 + y) * nz_parts + z for s, y in (members if z % 2 == 0 else members[::-1])]

    def along(value, steps):
        count = len(path)
        low, high = max(0, -steps), min(count, count - steps)
        return lax.ppermute(value, mesh_axes, [(path[i], path[i + steps]) for i in range(low, high)])

    smem = pl.BlockSpec(memory_space=pltpu.SMEM)
    vmem = pl.BlockSpec(memory_space=pltpu.VMEM)
    f32 = functools.partial(jax.ShapeDtypeStruct, dtype=jnp.float32)

    packed = pl.pallas_call(
        pack_kernel,
        out_shape=pltpu.VMEM((MEMBERS, CHUNK_IN, LANES), jnp.float32),
        in_specs=[vmem, vmem, vmem],
        out_specs=vmem,
        scratch_shapes=[
            pltpu.VMEM((2, LANES, TILE), jnp.float32),
            pltpu.VMEM((3, TILE, LANES), jnp.float32),
            pltpu.VMEM((LANES, LANES), jnp.float32),
        ],
        name="pack",
    )(inflow, initial, solid)
    got = lax.all_to_all(packed, ("sec", "gy"), 0, 0)
    got = pltpu.with_memory_space_constraint(got, pltpu.VMEM)
    own, right_one, left_one, right_two, left_two = pl.pallas_call(
        assemble_kernel,
        out_shape=[
            pltpu.VMEM((CHANNELS, SLAB, LANES), jnp.float32),
            pltpu.VMEM((EDGE_ONE, LANES), jnp.float32),
            pltpu.VMEM((EDGE_ONE, LANES), jnp.float32),
            pltpu.VMEM((EDGE_TWO, LANES), jnp.float32),
            pltpu.VMEM((EDGE_TWO, LANES), jnp.float32),
        ],
        in_specs=[vmem],
        out_specs=[vmem] * 5,
        name="assemble",
    )(got)
    window = pltpu.VMEM((NVAR, ROWS, LANES), jnp.float32)
    sent = pl.pallas_call(
        functools.partial(main_kernel, len(path) * SLAB),
        out_shape=f32((MEMBERS, CHUNK_OUT, LANES)),
        in_specs=[smem] * 4 + [vmem] * 5,
        out_specs=vmem,
        scratch_shapes=[
            window, window, window, window, window, window, window, window, window, window,
            pltpu.VMEM((NVAR, LANES, LANES), jnp.float32),
            pltpu.VMEM((2, ROWS, LANES), jnp.float32),
            pltpu.VMEM((3, 8, LANES), jnp.float32),
            pltpu.VMEM((4, 8, LANES), jnp.float32),
            pltpu.VMEM((4 * LANES, LANES), jnp.float32),
        ] + [pltpu.VMEM((LANES + 2 * GUARD, LANES), jnp.float32)] * (4 * NVAR),
        compiler_params=pltpu.CompilerParams(vmem_limit_bytes=32 * 1024 * 1024),
        name="march",
    )(
        speed_y, speed_z, vigneron, coupling,
        own, along(right_one, 1), along(left_one, -1), along(right_two, 2), along(left_two, -2),
    )
    returned = lax.all_to_all(sent, ("sec", "gy"), 0, 0)
    returned = pltpu.with_memory_space_constraint(returned, pltpu.VMEM)
    return pl.pallas_call(
        unpack_kernel,
        out_shape=f32((1, NVAR, PIECE, TILE)),
        in_specs=[vmem],
        out_specs=vmem,
        scratch_shapes=[
            pltpu.VMEM((2, LANES, LANES), jnp.float32),
            pltpu.VMEM((LANES, LANES), jnp.float32),
            pltpu.VMEM((2, LANES, LANES), jnp.float32),
        ],
        name="unpack",
    )(returned)


def chosen(*args):
    inflow, initial = args[0], args[1]
    fits = (
        lax.axis_size("sec") == 2
        and lax.axis_size("gy") == 4
        and inflow.shape == (NVAR, PIECE, TILE)
        and initial.shape == (1, NVAR, PIECE, TILE)
    )
    return slabs_per_device(*args) if fits else per_device(*args)


def solution(mesh):
    return jax.shard_map(
        chosen,
        mesh=mesh,
        in_specs=(
            P(None, "gy", "gz"),
            P("sec", None, "gy", "gz"),
            P("sec", "gy", "gz"),
            P(),
            P(),
            P(),
            P(),
        ),
        out_specs=P("sec", None, "gy", "gz"),
        check_vma=False,
    )
```

```python
import functools

import jax
import jax.numpy as jnp
from jax import lax
from jax.experimental import pallas as pl
from jax.experimental.pallas import tpu as pltpu
from jax.sharding import PartitionSpec as P

NVAR = 5
ITERS = 4
CORRECTORS = 3
NEWTON = 2

STEP_RATIO = 0.25
WENO_EPS = 1e-06


def passed_along(value, axis, steps):
    count = lax.axis_size(axis)
    initial, last = (max(0, -steps), min(count, count - steps))
    return lax.ppermute(value, axis, [(source, source + steps) for source in range(initial, last)])


def extended(block, sides, width):
    for axis, dim in sides:
        count = lax.axis_size(axis)
        forward = [(i, i + 1) for i in range(count - 1)]
        backward = [(target, source) for source, target in forward]
        low = lax.ppermute(
            lax.slice_in_dim(block, block.shape[dim] - width, None, axis=dim), axis, forward
        )
        high = lax.ppermute(lax.slice_in_dim(block, 0, width, axis=dim), axis, backward)
        block = jnp.concatenate([low, block, high], axis=dim)
    return block


def weno_face(left_far, left_near, center, right_near, right_far):
    smooth_left = (
        13.0 / 12.0 * (left_far - 2.0 * left_near + center) ** 2
        + 0.25 * (left_far - 4.0 * left_near + 3.0 * center) ** 2
    )
    smooth_middle = (
        13.0 / 12.0 * (left_near - 2.0 * center + right_near) ** 2
        + 0.25 * (left_near - right_near) ** 2
    )
    smooth_right = (
        13.0 / 12.0 * (center - 2.0 * right_near + right_far) ** 2
        + 0.25 * (3.0 * center - 4.0 * right_near + right_far) ** 2
    )
    weight_left = 0.1 / (WENO_EPS + smooth_left) ** 2
    weight_middle = 0.6 / (WENO_EPS + smooth_middle) ** 2
    weight_right = 0.3 / (WENO_EPS + smooth_right) ** 2
    guess_left = (2.0 * left_far - 7.0 * left_near + 11.0 * center) / 6.0
    guess_middle = (-left_near + 5.0 * center + 2.0 * right_near) / 6.0
    guess_right = (2.0 * center + 5.0 * right_near - right_far) / 6.0
    total = weight_left * guess_left + weight_middle * guess_middle + weight_right * guess_right
    return total / (weight_left + weight_middle + weight_right)


def sweep(padded, speeds, axis):
    count = padded.shape[axis] - 6
    plus_flux = jnp.maximum(speeds, 0.0)[:, None, None] * padded
    minus_flux = jnp.minimum(speeds, 0.0)[:, None, None] * padded

    def window(source, offset):
        return lax.slice_in_dim(source, offset, offset + count + 1, axis=axis)

    faces = weno_face(*(window(plus_flux, i) for i in (0, 1, 2, 3, 4)))
    faces = faces + weno_face(*(window(minus_flux, i) for i in (5, 4, 3, 2, 1)))
    return lax.slice_in_dim(faces, 1, count + 1, axis=axis) - lax.slice_in_dim(
        faces, 0, count, axis=axis
    )


def crossflow(padded, speed_y, speed_z):
    rows_part = sweep(padded[:, :, 3:-3], speed_y, 1)
    cols_part = sweep(padded[:, 3:-3, :], speed_z, 2)
    return rows_part + cols_part


def streamwise(field, factor):
    return field + factor * field**3 / (1.0 + field**2)


def slope(field, factor):
    return 1.0 + factor * field**2 * (3.0 + field**2) / (1.0 + field**2) ** 2


def correct(padded, current, upstream, diff, blocked, params):
    speed_y, speed_z, vigneron, coupling = params
    factor = vigneron[:, None, None]
    mixed = jnp.einsum("vw,wyz->vyz", coupling, current, precision=lax.Precision.HIGHEST)
    target = (
        streamwise(upstream, factor)
        - STEP_RATIO * crossflow(padded, speed_y, speed_z)
        + STEP_RATIO * mixed
        - (1.0 - factor) * diff
    )
    guess = current
    for newton_index in range(NEWTON):
        guess = guess - (streamwise(guess, factor) - target) / slope(guess, factor)
    return jnp.where(blocked[None], 0.0, guess)


def per_device(inflow, initial, solid, speed_y, speed_z, vigneron, coupling):
    params = (speed_y, speed_z, vigneron, coupling)
    sections = lax.axis_size("sec")
    position = lax.axis_index("sec")
    is_first = position == 0
    start_plane = initial[0]
    guess_above = passed_along(start_plane, "sec", 1)
    guess_above = jnp.where(is_first, inflow, guess_above)
    solid_tile = solid[0] != 0

    def station(upstream, diff):
        current = upstream
        for corrector_index in range(CORRECTORS):
            padded = extended(current, (("gy", 1), ("gz", 2)), 3)
            current = correct(padded, current, upstream, diff, solid_tile, params)
        return current

    def advance(step_index, carry):
        sent, own_prior, upstream_prior = carry
        received = passed_along(sent, "sec", 1)
        received = jnp.where(is_first, inflow, received)
        iterate = step_index - position + 1
        active = (iterate >= 1) & (iterate <= ITERS)
        updated = station(received, own_prior - upstream_prior)
        own_next = jnp.where(active, updated, own_prior)
        upstream_next = jnp.where(active, received, upstream_prior)
        return (own_next, own_next, upstream_next)

    result = lax.fori_loop(
        0, ITERS + sections - 1, advance, (start_plane, start_plane, guess_above)
    )
    return result[1][None]


LANES = 128
SLAB = 32
TILE = 256
MEMBERS = 8
PIECE = 32
GUARD = 16
STRIP = 80
LEFT = 40
ROWS = GUARD + LEFT + SLAB + LEFT + GUARD
CHUNK_IN = 72
CHUNK_OUT = 40
NEAR = 24
EDGE_ONE = 11 * SLAB + 6 * NEAR
FAR = 4
EDGE_TWO = 32
CHANNELS = 17


def lane_iota():
    return lax.broadcasted_iota(jnp.int32, (8, LANES), 1)


def turned(value, shift):
    shift = shift % LANES
    return value if shift == 0 else pltpu.roll(value, shift, 1)


def slab_of(member, odd):
    sec, gy = member // 4, member % 4
    j = 2 * gy + (sec ^ (gy & 1))
    return jnp.where(odd, MEMBERS - 1 - j, j)


def own_place():
    return lax.axis_index("sec"), lax.axis_index("gy"), lax.axis_index("gz") % 2 == 1


def own_slab():
    sec, gy, odd = own_place()
    return lax.axis_index("gz") * MEMBERS + slab_of(sec * 4 + gy, odd)


def slot(i, gy):
    return (i + gy) % 4


def pack_kernel(inflow, initial, solid, out, stacked, turned_ref, solids):
    sec, gy, odd = own_place()
    for group in range(2):
        for p in range(4):
            rows = pl.ds(pl.multiple_of(slot(p, gy) * PIECE, PIECE), PIECE)
            if group == 0:
                stacked[group, rows, :] = initial[0, p]
            elif p == 0:
                stacked[group, rows, :] = initial[0, 4]
            else:
                stacked[group, rows, :] = inflow[jnp.minimum(3 * sec + p - 1, NVAR - 1)]
    for half in range(2):
        solids[pl.ds(half * PIECE, PIECE), :] = solid[
            0, :, half * LANES:(half + 1) * LANES
        ].astype(jnp.float32)
    solids[pl.ds(2 * PIECE, 2 * PIECE), :] = jnp.zeros((2 * PIECE, LANES), jnp.float32)
    for group in range(2):
        for half in range(2):
            turned_ref[group, pl.ds(half * LANES, LANES), :] = stacked[
                group, :, half * LANES:(half + 1) * LANES
            ].T
    turned_ref[2, pl.ds(0, LANES), :] = solids[...].T
    quarter = lane_iota() // PIECE
    for member in range(MEMBERS):
        j = slab_of(member, odd)
        rows = pl.ds(pl.multiple_of(j * SLAB, SLAB), SLAB)
        for group in range(2):
            out[member, pl.ds(group * SLAB, SLAB), :] = turned_ref[group, rows, :]
        half, within = j // 4, j % 4
        packed = jnp.zeros((8, LANES), jnp.float32)
        for octet in range(4):
            piece = turned_ref[2, pl.ds(pl.multiple_of(within * SLAB + octet * 8, 8), 8), :]
            to = slot(octet, gy)
            piece = pltpu.roll(piece, (PIECE * (to - half)) & (LANES - 1), 1)
            packed = jnp.where(quarter == to, piece, packed)
        out[member, pl.ds(2 * SLAB, 8), :] = packed


def far_rows(channel):
    return (FAR * channel, FAR) if channel < NVAR else (FAR * NVAR + channel - NVAR, 1)


def assemble_kernel(got, own, right_one, left_one, right_two, left_two):
    quarter = lane_iota() // PIECE

    def gathered(sec, row, i):
        value = got[sec * 4, pl.ds(row, 8), :]
        for gy in range(1, 4):
            value = jnp.where(quarter == slot(i, gy), got[sec * 4 + gy, pl.ds(row, 8), :], value)
        return turned(value, -PIECE * i)

    def source(channel, octet):
        if channel < 3:
            return gathered(0, SLAB + 8 * octet, channel + 1)
        if channel < 5:
            return gathered(1, SLAB + 8 * octet, channel - 2)
        sec, v = (channel - 5) // 6, (channel - 5) % 6
        if v < 4:
            return gathered(sec, 8 * octet, v)
        if v == 4:
            return gathered(sec, SLAB + 8 * octet, 0)
        return gathered(sec, 2 * SLAB, octet)

    for ref in (right_two, left_two):
        ref[...] = jnp.zeros((EDGE_TWO, LANES), jnp.float32)
    for channel in range(CHANNELS):
        for octet in range(4):
            value = source(channel, octet)
            own[channel, pl.ds(8 * octet, 8), :] = value
            if channel < 11:
                rows = pl.ds(channel * SLAB + 8 * octet, 8)
                right_one[rows, :] = value
                left_one[rows, :] = value
                at, width = far_rows(channel)
                if octet == 3:
                    right_two[pl.ds(at, width), :] = value[8 - width:]
                if octet == 0:
                    left_two[pl.ds(at, width), :] = value[:width]
            else:
                at = 11 * SLAB + (channel - 11) * NEAR
                if octet > 0:
                    right_one[pl.ds(at + 8 * (octet - 1), 8), :] = value
                if octet < 3:
                    left_one[pl.ds(at + 8 * octet, 8), :] = value


def unpack_kernel(got, out, stacked, packed, turned_ref):
    _, gy, odd = own_place()
    quarter = lane_iota() // PIECE

    def member_of(j):
        j = jnp.where(odd, MEMBERS - 1 - j, j)
        row_block = j // 2
        return (j + row_block) % 2 * 4 + row_block

    for half in range(2):
        for within in range(4):
            member = member_of(4 * half + within)
            stacked[half, pl.ds(within * SLAB, SLAB), :] = got[member, pl.ds(0, SLAB), :]
    for within in range(4):
        low = got[member_of(within), pl.ds(SLAB, 8), :]
        high = got[member_of(4 + within), pl.ds(SLAB, 8), :]
        for octet in range(4):
            back = -PIECE * slot(octet, gy)
            packed[pl.ds(within * SLAB + 8 * octet, 8), :] = jnp.where(
                quarter == 0,
                pltpu.roll(low, back & (LANES - 1), 1),
                pltpu.roll(high, (back + PIECE) & (LANES - 1), 1),
            )
    for half in range(2):
        turned_ref[half] = stacked[half].T
    block = packed[...].T
    for half in range(2):
        columns = slice(half * LANES, (half + 1) * LANES)
        for v in range(4):
            rows = pl.ds(pl.multiple_of(slot(v, gy) * PIECE, PIECE), PIECE)
            out[0, v, :, columns] = turned_ref[half, rows, :]
        out[0, 4, :, columns] = block[half * PIECE:(half + 1) * PIECE]


def weighted(d1, d2, d3, d4, t1, t2, t3):
    a = 3.0 * d2 - d1
    b = d2 + d3
    c = 3.0 * d3 - d4
    y1 = pltpu.reciprocal(t1 + a * a, approx=True)
    y2 = pltpu.reciprocal(t2 + b * b, approx=True)
    y3 = pltpu.reciprocal(t3 + c * c, approx=True)
    g1, g2, g3 = (1.0 / 6.0) * (y1 * y1), y2 * y2, 0.5 * (y3 * y3)
    over = g1 * (a + a - d2) + g2 * (b + d3) + g3 * (c + d3)
    under = g1 + g2 + g3
    return over * pltpu.reciprocal(under, approx=True)


def main_kernel(
    last, speed_y, speed_z, vigneron, coupling,
    own, from_left, from_right, from_left_two, from_right_two,
    out,
    inf, still, base, cur, s0, s1, work_inf, delta, curve, face, rows_part, blocked, half_block, half_strip, strips, *per_block,
):
    across, delta_y, curve_y, face_y = (per_block[NVAR * i:NVAR * (i + 1)] for i in range(4))
    lane = lane_iota()
    center = GUARD + LEFT

    def fill(ref, channel, wide):
        ref[pl.ds(0, GUARD), :] = jnp.zeros((GUARD, LANES), jnp.float32)
        ref[pl.ds(ROWS - GUARD, GUARD), :] = jnp.zeros((GUARD, LANES), jnp.float32)
        ref[pl.ds(center, SLAB), :] = own[channel]
        if wide:
            zeros = jnp.zeros((8, LANES), jnp.float32)
            far, width = far_rows(channel)
            ref[pl.ds(GUARD, 8), :] = zeros
            ref[pl.ds(GUARD + 8 - width, width), :] = from_left_two[pl.ds(far, width), :]
            ref[pl.ds(GUARD + 8, SLAB), :] = from_left[pl.ds(SLAB * channel, SLAB), :]
            ref[pl.ds(center + SLAB, SLAB), :] = from_right[pl.ds(SLAB * channel, SLAB), :]
            ref[pl.ds(center + 2 * SLAB, 8), :] = zeros
            ref[pl.ds(center + 2 * SLAB, width), :] = from_right_two[pl.ds(far, width), :]
        else:
            at = 11 * SLAB + (channel - 11) * NEAR
            zeros = jnp.zeros((16, LANES), jnp.float32)
            ref[pl.ds(GUARD, 16), :] = zeros
            ref[pl.ds(center - NEAR, NEAR), :] = from_left[pl.ds(at, NEAR), :]
            ref[pl.ds(center + SLAB, NEAR), :] = from_right[pl.ds(at, NEAR), :]
            ref[pl.ds(center + SLAB + NEAR, 16), :] = zeros

    for v in range(NVAR):
        fill(inf.at[v], v, True)
        fill(s0.at[v], 5 + v, True)
        fill(cur.at[v], 11 + v, False)
    fill(blocked.at[0], 10, True)
    fill(blocked.at[1], 16, False)
    slab = own_slab()
    for octet in range(ROWS // 8):
        rows = pl.ds(8 * octet, 8)
        column = slab * SLAB + 8 * octet - center + lax.broadcasted_iota(jnp.int32, (8, LANES), 0)
        outside = (column < 0) | (column >= last)
        for station in range(2):
            blocked[station, rows, :] = jnp.where(
                outside | (blocked[station, rows, :] != 0.0), 0.0, 1.0
            )
    for v in range(NVAR):
        across[v][pl.ds(0, GUARD), :] = jnp.zeros((GUARD, LANES), jnp.float32)
        across[v][pl.ds(GUARD + LANES, GUARD), :] = jnp.zeros((GUARD, LANES), jnp.float32)

    sy = [speed_y[v] for v in range(NVAR)]
    sz = [speed_z[v] for v in range(NVAR)]
    half_y = [0.5 * jnp.maximum(s, -s) for s in sy]
    half_z = [0.5 * jnp.maximum(s, -s) for s in sz]
    step_y = [jnp.where(s >= 0.0, 1, -1) for s in sy]
    step_z = [jnp.where(s >= 0.0, 1, -1) for s in sz]
    vig = [vigneron[v] for v in range(NVAR)]
    forward = [(s >= 0.0).astype(jnp.int32) for s in sy]
    ahead = sum(forward)
    rank, seen = [], 0
    for v in range(NVAR):
        rank.append(jnp.where(forward[v] == 1, seen, ahead + v - seen))
        seen = seen + forward[v]

    def nth(r):
        return sum(jnp.where(rank[v] == r, v, 0) for v in range(NVAR))

    turning = (STRIP * ahead + LANES - 1) // LANES * LANES
    place_of = [
        pl.multiple_of(
            jnp.where(forward[v] == 1, STRIP * rank[v], turning + STRIP * (rank[v] - ahead)), 16
        )
        for v in range(NVAR)
    ]
    for b in range(4):
        value = jnp.zeros((8, LANES), jnp.float32)
        for v in range(NVAR):
            at = lane + LANES * b - place_of[v]
            value = jnp.where((at >= 0) & (at < STRIP), half_y[v], value)
        half_strip[b] = value
    strips[...] = jnp.zeros((4 * LANES, LANES), jnp.float32)
    lone = jnp.where(ahead % 2 == 0, NVAR - 1, 0)
    begin = 1 - jnp.minimum(lone, 1)
    couples = [(nth(begin), nth(begin + 1)), (nth(begin + 2), nth(begin + 3)), (nth(lone), nth(lone))]
    for b, (va, vb) in enumerate(couples):
        both = [speed_y[va], speed_y[vb]]
        both = [0.5 * jnp.maximum(s, -s) for s in both]
        half_block[b] = jnp.where(lane < LANES // 2, both[0], both[1])
    per = [0.5 / vig[v] for v in range(NVAR)]
    stiff = [(1.0 + vig[v]) * per[v] for v in range(NVAR)]
    held = [(1.0 - vig[v]) * per[v] for v in range(NVAR)]
    spread = [(STEP_RATIO / 3.0) * per[v] for v in range(NVAR)]
    mix = [[STEP_RATIO * coupling[v, w] * per[v] for w in range(NVAR)] for v in range(NVAR)]

    def newton(v, guess, target):
        for _ in range(NEWTON):
            r = pltpu.reciprocal(1.0 + guess * guess, approx=True)
            square = r * r
            over = (r - square) * guess + target
            under = (0.5 * r - square) + stiff[v]
            guess = over * pltpu.reciprocal(under, approx=True)
        return guess

    def energy(v, field):
        r = pltpu.reciprocal(1.0 + field * field, approx=True)
        return field * (stiff[v] - 0.5 * r)

    def octet_rows(g):
        return pl.multiple_of(GUARD + 8 * g, 8)

    def pairs(low, high, body):
        def two(i, c):
            for k in range(2):
                body(octet_rows(low + 2 * i + k))
            return c
        lax.fori_loop(0, (high - low) // 2, two, 0)

    def differences(src, half, step, d_ref, t_ref, at):
        here = src[pl.ds(at, 8), :]
        down = src[pl.ds(at + step, 8), :]
        up = src[pl.ds(at - step, 8), :]
        d = down - here
        t = d - (here - up)
        d_ref[pl.ds(at, 8), :] = d * half
        t_ref[pl.ds(at, 8), :] = ((13.0 / 3.0) * (half * half)) * (t * t) + WENO_EPS

    def faces(src, half, step, d_ref, t_ref, f_ref, at):
        d3 = d_ref[pl.ds(at, 8), :]
        d2 = d_ref[pl.ds(at - step, 8), :]
        d1 = d_ref[pl.ds(at - 2 * step, 8), :]
        d4 = d_ref[pl.ds(at + step, 8), :]
        t1 = t_ref[pl.ds(at - step, 8), :]
        t2 = t_ref[pl.ds(at, 8), :]
        t3 = t_ref[pl.ds(at + step, 8), :]
        f_ref[pl.ds(at, 8), :] = (6.0 * half) * src[pl.ds(at, 8), :] + weighted(
            d1, d2, d3, d4, t1, t2, t3
        )

    def octets_of(n):
        g0 = 7 - n // 2
        return [GUARD + 8 * g for g in range(g0, g0 + n)]

    def blocks_of(n):
        if n > 8:
            if n == STRIP // 8:
                return [
                    (half_strip[b], jnp.where(LANES * b < turning, 1, -1)) for b in range(4)
                ]
            return list(zip(half_y, step_y))
        return [
            (half_block[b], jnp.where(speed_y[va] >= 0.0, 1, -1))
            for b, (va, _) in enumerate(couples)
        ]

    middle = LANES // 2
    narrow = pl.ds(GUARD + 24, middle)

    strip = pl.ds(GUARD + LEFT + SLAB // 2 - STRIP // 2, STRIP)

    def turn_in(src, n):
        if n == STRIP // 8:
            for v in range(NVAR):
                strips[pl.ds(place_of[v], STRIP), :] = src[v, strip, :]
            for b in range(4):
                across[b][pl.ds(GUARD, LANES), :] = strips[pl.ds(LANES * b, LANES), :].T
        elif n > 8:
            for v in range(NVAR):
                across[v][pl.ds(GUARD, LANES), :] = src[v, pl.ds(GUARD - 8, LANES), :].T
        else:
            for b, couple in enumerate(couples):
                two = [src[v, narrow, :] for v in couple]
                across[b][pl.ds(GUARD, LANES), :] = jnp.concatenate(two, axis=0).T

    def column_differences(src, n):
        octets = octets_of(n)
        for at in [octets[0] - 8] + octets + [octets[-1] + 8]:
            for v in range(NVAR):
                differences(src.at[v], half_z[v], step_z[v], delta.at[v], curve.at[v], at)

    def column_faces(src, octets):
        for at in octets:
            for v in range(NVAR):
                faces(src.at[v], half_z[v], step_z[v], delta.at[v], curve.at[v], face.at[v], at)

    def entry_faces(src, n):
        octets = octets_of(n)
        for v in range(NVAR):
            at = jnp.where(step_z[v] > 0, octets[0] - 8, octets[-1] + 8)
            faces(src.at[v], half_z[v], step_z[v], delta.at[v], curve.at[v], face.at[v], at)

    def row_faces(n):
        for b, (half, step) in enumerate(blocks_of(n)):
            row = (across[b], half, step, delta_y[b], curve_y[b])
            for i in range(-1, 17):
                differences(*row, GUARD + 8 * i)
            for i in range(16):
                faces(*row, face_y[b], GUARD + 8 * i)
            faces(*row, face_y[b], GUARD + jnp.where(step > 0, -8, LANES))

    def turn_out(n):
        for b, (_, step) in enumerate(blocks_of(n)):
            change = (
                face_y[b][pl.ds(GUARD, LANES), :] - face_y[b][pl.ds(GUARD - step, LANES), :]
            ).T
            if n == STRIP // 8:
                strips[pl.ds(LANES * b, LANES), :] = change
            elif n > 8:
                rows_part[b] = change
            else:
                rows = pl.ds(8 + 24, middle)
                rows_part[couples[b][0], rows, :] = change[:middle]
                rows_part[couples[b][1], rows, :] = change[middle:]
        if n == STRIP // 8:
            rows = pl.ds(8 + LEFT + SLAB // 2 - STRIP // 2, STRIP)
            for v in range(NVAR):
                rows_part[v, rows, :] = strips[pl.ds(place_of[v], STRIP), :]

    def sources(src, at):
        field = [src[v, pl.ds(at, 8), :] for v in range(NVAR)]
        result = []
        for v in range(NVAR):
            columns = face[v, pl.ds(at, 8), :] - face[v, pl.ds(at - step_z[v], 8), :]
            rows = rows_part[v, pl.ds(at - (GUARD - 8), 8), :]
            mixed = mix[v][0] * field[0]
            for w in range(1, NVAR):
                mixed = mixed + mix[v][w] * field[w]
            result.append(mixed - spread[v] * (rows + columns))
        return field, result

    def steps(station, octets):
        for at in octets:
            field, terms = sources(cur, at)
            fluid = blocked[station, pl.ds(at, 8), :] != 0.0
            for v in range(NVAR):
                value = newton(v, field[v], still[v, pl.ds(at, 8), :] + terms[v])
                cur[v, pl.ds(at, 8), :] = jnp.where(fluid, value, 0.0)

    turn_in(inf, 14)
    column_differences(inf, 14)
    row_faces(14)
    turn_out(14)
    column_faces(inf, octets_of(14))
    for at in octets_of(14):
        field, terms = sources(inf, at)
        for v in range(NVAR):
            base[v, pl.ds(at, 8), :] = energy(v, field[v])
            work_inf[v, pl.ds(at, 8), :] = terms[v]

    def first_of_0(at):
        fluid = blocked[0, pl.ds(at, 8), :] != 0.0
        for v in range(NVAR):
            s1[v, pl.ds(at, 8), :] = cur[v, pl.ds(at, 8), :]
            here = inf[v, pl.ds(at, 8), :]
            prior = s0[v, pl.ds(at, 8), :]
            fixed = base[v, pl.ds(at, 8), :] - held[v] * (prior - here)
            still[v, pl.ds(at, 8), :] = fixed
            value = newton(v, here, fixed + work_inf[v, pl.ds(at, 8), :])
            cur[v, pl.ds(at, 8), :] = jnp.where(fluid, value, 0.0)

    def start_of_1(at):
        for v in range(NVAR):
            above = cur[v, pl.ds(at, 8), :]
            prior = s1[v, pl.ds(at, 8), :] - s0[v, pl.ds(at, 8), :]
            still[v, pl.ds(at, 8), :] = energy(v, above) - held[v] * prior
            s0[v, pl.ds(at, 8), :] = above

    def pass_of(t, carry):
        k, c = t // 5, t % 5

        @pl.when(c == 0)
        def _():
            g0 = (6 + 6 * k) // 8
            pairs(g0, 14 - g0, first_of_0)

        @pl.when(c == 2)
        def _():
            g0 = (12 + 6 * k) // 8
            pairs(g0, 14 - g0, start_of_1)

        station = (c >= 2).astype(jnp.int32)
        g0 = (10 + 6 * k + 3 * c) // 8
        for n in (12, 10, 8, 6, 4):
            times = (g0 == 7 - n // 2).astype(jnp.int32)

            def part(i, c, n=n):
                turn_in(cur, n)
                column_differences(cur, n)
                column_faces(cur, octets_of(n)[:n // 3])
                return c
            lax.fori_loop(0, times, part, 0)

            def part(i, c, n=n):
                row_faces(n)
                return c
            lax.fori_loop(0, times, part, 0)

            def part(i, c, n=n):
                turn_out(n)
                column_faces(cur, octets_of(n)[n // 3:])
                if n in (STRIP // 8, SLAB // 8):
                    entry_faces(cur, n)
                steps(station, octets_of(n))
                return c
            lax.fori_loop(0, times, part, 0)
        return carry

    lax.fori_loop(0, 5 * ITERS, pass_of, 0)

    quarter = lane // PIECE
    for station, result in enumerate((s0, cur)):
        at_last = []
        for octet in range(4):
            rows = pl.ds(center + 8 * octet, 8)
            field = [turned(result[v, rows, :], PIECE * v) for v in range(4)]
            at_last.append(turned(result[4, rows, :], PIECE * octet))
            for gy in range(4):
                value = field[0]
                for v in range(1, 4):
                    value = jnp.where(quarter == slot(v, gy), field[v], value)
                out[station * 4 + gy, pl.ds(8 * octet, 8), :] = value
        for gy in range(4):
            value = at_last[0]
            for octet in range(1, 4):
                value = jnp.where(quarter == slot(octet, gy), at_last[octet], value)
            out[station * 4 + gy, pl.ds(SLAB, 8), :] = value


def slabs_per_device(inflow, initial, solid, speed_y, speed_z, vigneron, coupling):
    mesh_axes = ("sec", "gy", "gz")
    nz_parts = lax.axis_size("gz")
    path = []
    for z in range(nz_parts):
        members = [(s, y) for y in range(4) for s in ((0, 1) if y % 2 == 0 else (1, 0))]
        path += [(s * 4 + y) * nz_parts + z for s, y in (members if z % 2 == 0 else members[::-1])]

    def along(value, steps):
        count = len(path)
        low, high = max(0, -steps), min(count, count - steps)
        return lax.ppermute(value, mesh_axes, [(path[i], path[i + steps]) for i in range(low, high)])

    smem = pl.BlockSpec(memory_space=pltpu.SMEM)
    vmem = pl.BlockSpec(memory_space=pltpu.VMEM)
    f32 = functools.partial(jax.ShapeDtypeStruct, dtype=jnp.float32)

    packed = pl.pallas_call(
        pack_kernel,
        out_shape=pltpu.VMEM((MEMBERS, CHUNK_IN, LANES), jnp.float32),
        in_specs=[vmem, vmem, vmem],
        out_specs=vmem,
        scratch_shapes=[
            pltpu.VMEM((2, LANES, TILE), jnp.float32),
            pltpu.VMEM((3, TILE, LANES), jnp.float32),
            pltpu.VMEM((LANES, LANES), jnp.float32),
        ],
        name="pack",
    )(inflow, initial, solid)
    got = lax.all_to_all(packed, ("sec", "gy"), 0, 0)
    got = pltpu.with_memory_space_constraint(got, pltpu.VMEM)
    own, right_one, left_one, right_two, left_two = pl.pallas_call(
        assemble_kernel,
        out_shape=[
            pltpu.VMEM((CHANNELS, SLAB, LANES), jnp.float32),
            pltpu.VMEM((EDGE_ONE, LANES), jnp.float32),
            pltpu.VMEM((EDGE_ONE, LANES), jnp.float32),
            pltpu.VMEM((EDGE_TWO, LANES), jnp.float32),
            pltpu.VMEM((EDGE_TWO, LANES), jnp.float32),
        ],
        in_specs=[vmem],
        out_specs=[vmem] * 5,
        name="assemble",
    )(got)
    window = pltpu.VMEM((NVAR, ROWS, LANES), jnp.float32)
    sent = pl.pallas_call(
        functools.partial(main_kernel, len(path) * SLAB),
        out_shape=f32((MEMBERS, CHUNK_OUT, LANES)),
        in_specs=[smem] * 4 + [vmem] * 5,
        out_specs=vmem,
        scratch_shapes=[
            window, window, window, window, window, window, window, window, window, window,
            pltpu.VMEM((NVAR, LANES, LANES), jnp.float32),
            pltpu.VMEM((2, ROWS, LANES), jnp.float32),
            pltpu.VMEM((3, 8, LANES), jnp.float32),
            pltpu.VMEM((4, 8, LANES), jnp.float32),
            pltpu.VMEM((4 * LANES, LANES), jnp.float32),
        ] + [pltpu.VMEM((LANES + 2 * GUARD, LANES), jnp.float32)] * (4 * NVAR),
        compiler_params=pltpu.CompilerParams(vmem_limit_bytes=32 * 1024 * 1024),
        name="march",
    )(
        speed_y, speed_z, vigneron, coupling,
        own, along(right_one, 1), along(left_one, -1), along(right_two, 2), along(left_two, -2),
    )
    returned = lax.all_to_all(sent, ("sec", "gy"), 0, 0)
    returned = pltpu.with_memory_space_constraint(returned, pltpu.VMEM)
    return pl.pallas_call(
        unpack_kernel,
        out_shape=f32((1, NVAR, PIECE, TILE)),
        in_specs=[vmem],
        out_specs=vmem,
        scratch_shapes=[
            pltpu.VMEM((2, LANES, LANES), jnp.float32),
            pltpu.VMEM((LANES, LANES), jnp.float32),
            pltpu.VMEM((2, LANES, LANES), jnp.float32),
        ],
        name="unpack",
    )(returned)


def chosen(*args):
    inflow, initial = args[0], args[1]
    fits = (
        lax.axis_size("sec") == 2
        and lax.axis_size("gy") == 4
        and inflow.shape == (NVAR, PIECE, TILE)
        and initial.shape == (1, NVAR, PIECE, TILE)
    )
    return slabs_per_device(*args) if fits else per_device(*args)


def solution(mesh):
    return jax.shard_map(
        chosen,
        mesh=mesh,
        in_specs=(
            P(None, "gy", "gz"),
            P("sec", None, "gy", "gz"),
            P("sec", "gy", "gz"),
            P(),
            P(),
            P(),
            P(),
        ),
        out_specs=P("sec", None, "gy", "gz"),
        check_vma=False,
    )
```
